32 devices in a mesh: group: 2 (over y), batch: 4 (over x, core), tensor: 4 (over z).
Axes of the slice: x: 2, y: 2, z: 4, core: 2. Of those that a mesh axis runs over, the one named last changes fastest.
Arguments:
- query: bfloat16 [256, 4096], P(('group', 'batch', 'tensor')), parts along dimension 0, may hold values from -200 to 200
- fresh_key: bfloat16 [256, 512], P(('group', 'batch', 'tensor')), parts along dimension 0, may hold values from -6 to 6
- fresh_value: bfloat16 [256, 512], P(('group', 'batch', 'tensor')), parts along dimension 0, may hold values from -12 to 12
- stored_keys: bfloat16 [256, 4, 128, 128], P(('group', 'batch', 'tensor')), parts along dimension 0, may hold values from -6 to 6
- stored_values: bfloat16 [256, 4, 128, 128], P(('group', 'batch', 'tensor')), parts along dimension 0, may hold values from -12 to 12
- cached_length: int32 [256], P(('group', 'batch', 'tensor')), parts along dimension 0, may hold values from 32 to 128
- request_adapter: int32 [256], P(('group', 'batch', 'tensor')), parts along dimension 0, may hold values from 0 to 15, as said below
- rank_per_adapter: int32 [16], replicated, may hold values from 8 to 128, as said below
- output_weight: bfloat16 [4096, 8192], P('tensor'), may hold values from -0.125 to 0.125
- adapter_down_weight: bfloat16 [16, 4096, 128], P('batch', 'tensor'), may hold values from -0.09375 to 0.09375
- adapter_up_weight: bfloat16 [16, 128, 8192], P('batch', None, 'tensor'), may hold values from -0.75 to 0.75
Outputs:
- mixed: bfloat16 [256, 8192], P(('group', 'batch'), 'tensor'), parts along dimension 0
The draws below stay inside these ranges and needn't reach their ends.
There are 2 independent parts, one for each index of `group`. The reference program is written for one: setup_inputs(seed, part) draws one part's arguments, and reference() takes and returns one part's arrays. A program takes and returns all parts, laid end to end along the dimension named above; an argument that names none is the same for every part. Nothing has to cross between parts.
Inputs may be any that keep to these rules, and one draw needn't show every extreme that they name: `rank_per_adapter`: each rank is 128 divided by a power of two. `request_adapter`: adapter a is held by owner a // 4. Among the 32 requests of one batch index (aligned blocks), at most 16 name adapters of one owner; some owner has exactly 16 in every block.
All inputs are finite; a program needn't handle non-finite values.
Results may differ from the reference program's by a relative error of at most 0.013.
Values may be sent and summed in bfloat16 or wider, within the bound.
No kernel may reach another device: no remote copies, remote signals or barrier semaphores. Data moves between devices by JAX's collectives and lax.ppermute only.
A program may use at most 128 MiB of HBM per device.

```python
import math
import jax
import jax.numpy as jnp
from jax import lax

MODEL_WIDTH = 8192
QUERY_HEADS = 32
KVH = 4
HEAD_WIDTH = 128
LARGEST_RANK = 128
A_DEV = 4
REQ_DEV = 8
LMAX = 128
REQS = 128
ADAPTER_TOTAL = 16
N_BATCH = 4
N_TENSOR = 4


def shared_first(key):
    return jax.random.normal(key, (REQS, KVH, HEAD_WIDTH), jnp.float32)


def draw_query(key, part):
    key = jax.random.fold_in(key, 11)
    queries = jax.random.normal(key, (REQS, QUERY_HEADS, HEAD_WIDTH), jnp.float32)
    return queries.reshape(REQS, QUERY_HEADS * HEAD_WIDTH).astype(jnp.bfloat16)


def draw_stored_keys(key, part):
    first_keys = shared_first(key)
    key = jax.random.fold_in(key, 12)
    keys_all = jax.random.normal(key, (REQS, KVH, LMAX, HEAD_WIDTH), jnp.float32)
    keys_all = jnp.clip(keys_all, -6.0, 6.0)
    first_keys = jnp.clip(first_keys, -6.0, 6.0)
    keys_all = keys_all.at[:, :, 0, :].set(first_keys)
    return keys_all.astype(jnp.bfloat16)


def draw_cached_length(key, part):
    key = jax.random.fold_in(key, 13)
    lengths = jax.random.randint(key, (REQS,), LMAX // 4, LMAX + 1)
    longest = jax.random.randint(jax.random.fold_in(key, 1), (), 0, REQS)
    lengths = lengths.at[longest].set(LMAX)
    lengths = lengths.at[(longest + 1) % REQS].set(LMAX // 4)
    return lengths.astype(jnp.int32)


def draw_rank_per_adapter(key, part):
    key = jax.random.fold_in(key, 14)
    shifts = jax.random.randint(key, (ADAPTER_TOTAL,), 0, 5)
    request_ranks = LARGEST_RANK // 2 ** shifts
    widest = jax.random.randint(jax.random.fold_in(key, 1), (), 0, ADAPTER_TOTAL)
    request_ranks = request_ranks.at[widest].set(LARGEST_RANK)
    request_ranks = request_ranks.at[(widest + 1) % ADAPTER_TOTAL].set(LARGEST_RANK // 16)
    return request_ranks.astype(jnp.int32)


def draw_request_adapter(key, part):
    key = jax.random.fold_in(key, 15)
    block_rows = REQ_DEV * N_TENSOR
    block_total = REQS // block_rows
    capacity = 2 * block_rows // N_BATCH
    busiest = jax.random.randint(jax.random.fold_in(key, 1), (), 0, N_BATCH)
    others = jnp.arange(N_BATCH - 1, dtype=jnp.int32)
    others = others + (others >= busiest).astype(jnp.int32)
    others_pool = jnp.repeat(others, capacity)

    def one_block(block_key):
        first_key, second_key, third_key = jax.random.split(block_key, 3)
        remaining = jax.random.permutation(first_key, others_pool)[:block_rows - capacity]
        owners = jnp.concatenate([jnp.full((capacity,), busiest, jnp.int32), remaining])
        owners = jax.random.permutation(second_key, owners)
        within = jax.random.randint(third_key, (block_rows,), 0, A_DEV)
        return owners * A_DEV + within
    block_keys = jax.random.split(jax.random.fold_in(key, 2), block_total)
    return jax.vmap(one_block)(block_keys).reshape(REQS).astype(jnp.int32)


def raised(drawn, rng, source, target, shards_of, factor):
    def block_of(position):
        return (jnp.arange(drawn.shape[position]) // (drawn.shape[position] // shards_of)).reshape((-1,) + (1,) * (drawn.ndim - 1 - position))

    near = jax.random.permutation(rng, shards_of)[block_of(target)]
    second = (block_of(target) + shards_of // 2) % shards_of
    return jnp.where((block_of(source) == near) | (block_of(source) == second), factor * drawn, drawn)


def shard_levels(rng, dims, pieces, smallest, largest):
    gain = 1.0
    for position, blocks in pieces:
        steps = jax.random.uniform(jax.random.fold_in(jax.random.fold_in(rng, 6), position), (blocks,), jnp.float32, smallest / len(pieces), largest / len(pieces))
        gain = gain * jnp.repeat(jnp.exp(steps), dims[position] // blocks).reshape((-1,) + (1,) * (len(dims) - 1 - position))
    return gain


def centred(key, extent, spread, limit, cuts=(), kind=jnp.bfloat16):
    values = spread * jax.random.normal(key, extent, jnp.float32)
    if cuts:
        values = values * shard_levels(key, extent, cuts, -0.22, 0.18)
    return jnp.clip(values, -limit, limit).astype(kind)


def heavy_noise(stream_key, shape, width, most, cuts, heavy, kind=jnp.bfloat16):
    drawn = width * jax.random.normal(stream_key, shape, jnp.float32)
    if cuts:
        drawn = drawn * shard_levels(stream_key, shape, cuts, -0.22, 0.18)
    return jnp.clip(raised(drawn, jax.random.fold_in(stream_key, 3), *heavy), -most, most).astype(kind)


def setup_inputs(seed: int = 0, part: int = 0) -> dict:
    key_of = jax.random.split(jax.random.key(seed), 12)
    part_keys = jax.random.split(jax.random.fold_in(key_of[11], part), 12)
    return {
        "query": draw_query(jax.random.fold_in(jax.random.fold_in(key_of[11], part), 71), part),
        "fresh_key": centred(part_keys[1], (REQS, KVH * HEAD_WIDTH), 1.0, 6.0, ((0, 16),)),
        "fresh_value": centred(part_keys[2], (REQS, KVH * HEAD_WIDTH), 2.0, 12.0, ((0, 16),)),
        "stored_keys": draw_stored_keys(jax.random.fold_in(jax.random.fold_in(key_of[11], part), 71), part),
        "stored_values": centred(part_keys[4], (REQS, KVH, LMAX, HEAD_WIDTH), 2.0, 12.0, ((0, 16),)),
        "cached_length": draw_cached_length(jax.random.fold_in(jax.random.fold_in(key_of[11], part), 71), part),
        "request_adapter": draw_request_adapter(jax.random.fold_in(jax.random.fold_in(key_of[11], part), 71), part),
        "rank_per_adapter": draw_rank_per_adapter(jax.random.fold_in(key_of[11], 71), part),
        "output_weight": heavy_noise(key_of[8], (QUERY_HEADS * HEAD_WIDTH, MODEL_WIDTH), (QUERY_HEADS * HEAD_WIDTH) ** -0.5, 0.125, ((0, 4),), (0, 1, 4, 2.0)),
        "adapter_down_weight": centred(key_of[9], (ADAPTER_TOTAL, QUERY_HEADS * HEAD_WIDTH, LARGEST_RANK), (QUERY_HEADS * HEAD_WIDTH) ** -0.5, 0.09375, ((0, 4), (1, 4))),
        "adapter_up_weight": centred(key_of[10], (ADAPTER_TOTAL, LARGEST_RANK, MODEL_WIDTH), 0.125, 0.75, ((0, 4), (2, 4))),
    }


ADAPTER_SCALE = 16.0

def attend_block(query, fresh_key, fresh_value, stored_keys, stored_values, cached_length):
    requests = query.shape[0]
    group_size = QUERY_HEADS // KVH
    queries = query.astype(jnp.float32).reshape(requests, KVH, group_size, HEAD_WIDTH)
    scaling = 1.0 / math.sqrt(HEAD_WIDTH)
    scores = jnp.einsum('rkgd,rkld->rkgl', queries, stored_keys.astype(jnp.float32)) * scaling
    own_score = jnp.einsum('rkgd,rkd->rkg', queries, fresh_key.astype(jnp.float32).reshape(requests, KVH, HEAD_WIDTH)) * scaling
    valid = (jnp.arange(LMAX, dtype=jnp.int32)[None, :] < cached_length[:, None])[:, None, None, :]
    scores = jnp.where(valid, scores, -1e+30)
    highest = jnp.maximum(lax.optimization_barrier(jnp.max(scores, axis=-1)), own_score)
    exponent = jnp.where(valid, jnp.exp(scores - highest[..., None]), 0.0)
    own_exp = jnp.exp(own_score - highest)
    sum_exp = lax.optimization_barrier(jnp.sum(exponent, axis=-1)) + own_exp
    weights = lax.optimization_barrier((exponent / sum_exp[..., None]).astype(jnp.bfloat16)).astype(jnp.float32)
    own_weight = lax.optimization_barrier((own_exp / sum_exp).astype(jnp.bfloat16)).astype(jnp.float32)
    result = jnp.einsum('rkgl,rkld->rkgd', weights, stored_values.astype(jnp.float32))
    result = result + own_weight[..., None] * fresh_value.astype(jnp.float32).reshape(requests, KVH, 1, HEAD_WIDTH)
    return result.reshape(requests, QUERY_HEADS * HEAD_WIDTH).astype(jnp.bfloat16)

def shrink(values, request_ranks):
    keep_mask = jnp.arange(values.shape[-1], dtype=jnp.int32) < request_ranks[..., None]
    rank_factor = ADAPTER_SCALE / request_ranks.astype(jnp.float32)
    return jnp.where(keep_mask, values * rank_factor[..., None], 0.0).astype(jnp.bfloat16)

def reference(query, fresh_key, fresh_value, stored_keys, stored_values, cached_length, request_adapter, rank_per_adapter, output_weight, adapter_down_weight, adapter_up_weight):
    row_block = math.gcd(REQS, 64)
    block_count = REQS // row_block

    def split_rows(array):
        return array.reshape((block_count, row_block) + array.shape[1:])

    def attend_one(blocks):
        return attend_block(*blocks)
    attention_result = lax.map(attend_one, (split_rows(query), split_rows(fresh_key), split_rows(fresh_value), split_rows(stored_keys), split_rows(stored_values), split_rows(cached_length)))
    attention_result = attention_result.reshape(REQS, QUERY_HEADS * HEAD_WIDTH)
    columns = QUERY_HEADS * HEAD_WIDTH // N_TENSOR

    def add_block(running, block_index):
        head_part = lax.dynamic_slice_in_dim(attention_result, block_index * columns, columns, 1)
        weight_rows = lax.dynamic_slice_in_dim(output_weight, block_index * columns, columns, 0)
        down_product = jnp.dot(head_part, weight_rows, preferred_element_type=jnp.float32)
        rounded = lax.optimization_barrier(down_product.astype(jnp.bfloat16)).astype(jnp.float32)
        return (running + rounded, None)
    base, _ = lax.scan(add_block, jnp.zeros((REQS, MODEL_WIDTH), jnp.float32), jnp.arange(N_TENSOR, dtype=jnp.int32))
    slots = request_adapter
    request_ranks = rank_per_adapter[request_adapter]

    def add_down(running, cache_slot_index):
        selected = (slots == cache_slot_index)[:, None]
        down_product = jnp.dot(attention_result, adapter_down_weight[cache_slot_index], preferred_element_type=jnp.float32)
        return (running + jnp.where(selected, down_product, 0.0), None)
    low_full, _ = lax.scan(add_down, jnp.zeros((REQS, LARGEST_RANK), jnp.float32), jnp.arange(ADAPTER_TOTAL, dtype=jnp.int32))
    adapter_delta = shrink(low_full, request_ranks)

    def add_up(running, cache_slot_index):
        selected = (slots == cache_slot_index)[:, None]
        down_product = jnp.dot(adapter_delta, adapter_up_weight[cache_slot_index], preferred_element_type=jnp.float32)
        return (running + jnp.where(selected, down_product, 0.0), None)
    adapted, _ = lax.scan(add_up, jnp.zeros((REQS, MODEL_WIDTH), jnp.float32), jnp.arange(ADAPTER_TOTAL, dtype=jnp.int32))
    adapted = lax.optimization_barrier(adapted.astype(jnp.bfloat16)).astype(jnp.float32)
    return (base + adapted).astype(jnp.bfloat16)
```

```python
import functools
import math

import jax
import jax.numpy as jnp
from jax import lax
from jax.experimental import pallas as pl
from jax.experimental.pallas import tpu as pltpu
from jax.sharding import PartitionSpec as P

ADAPTER_SCALE = 16.0
F32 = jnp.float32
BF16 = jnp.bfloat16
LANES = 128
MIB = 1024 * 1024


def params(grid_rank=0, vmem=24 * MIB):
    if grid_rank:
        return pltpu.CompilerParams(
            dimension_semantics=("arbitrary",) * grid_rank, vmem_limit_bytes=vmem
        )
    return pltpu.CompilerParams(vmem_limit_bytes=vmem)


def cost(flops, nbytes):
    return pl.CostEstimate(flops=flops, bytes_accessed=nbytes, transcendentals=0)


def sds(shape, dtype=BF16):
    return jax.ShapeDtypeStruct(shape, dtype)


def column_of(ref, count):
    rows = lax.broadcasted_iota(jnp.int32, (count, LANES), 0)
    out = jnp.full((count, LANES), ref[0], jnp.int32)
    for i in range(1, count):
        out = jnp.where(rows == i, ref[i], out)
    return out


def attend_kernel(place, length, adapter, q_ref, fk_ref, fv_ref, k_ref, v_ref, *outs):
    step = pl.program_id(0)
    requests, _, longest, dim = k_ref.shape
    group = q_ref.shape[1] // dim
    rows = group * requests
    scaling = 1.0 / math.sqrt(dim)
    q32 = q_ref[...].astype(F32)
    queries = jnp.concatenate([q32[:, h * dim : (h + 1) * dim] for h in range(group)], axis=0)
    keys = k_ref[...].reshape(requests * longest, dim)
    every = lax.dot_general(
        queries.astype(BF16), keys, (((1,), (1,)), ((), ())), preferred_element_type=F32
    )
    request = lax.rem(lax.broadcasted_iota(jnp.int32, (rows, longest), 0), requests)
    scores = every[:, :longest]
    for r in range(1, requests):
        scores = jnp.where(request == r, every[:, r * longest : (r + 1) * longest], scores)
    lengths = jnp.concatenate([column_of(length, requests)] * group, axis=0)
    valid = lax.broadcasted_iota(jnp.int32, (rows, longest), 1) < lengths
    scores = jnp.where(valid, scores * scaling, -1e30)
    fresh_key = jnp.concatenate([fk_ref[...].astype(F32)] * group, axis=0)
    fresh_value = jnp.concatenate([fv_ref[...].astype(F32)] * group, axis=0)
    own = jnp.sum(queries * fresh_key, axis=1, keepdims=True) * scaling
    highest = jnp.maximum(jnp.max(scores, axis=1, keepdims=True), own)
    exponent = jnp.where(valid, jnp.exp(scores - highest), 0.0)
    own_exp = jnp.exp(own - highest)
    total = jnp.sum(exponent, axis=1, keepdims=True) + own_exp
    weights = exponent / total
    own_weight = (own_exp / total).astype(BF16).astype(F32)
    spread = jnp.concatenate(
        [jnp.where(request == r, weights, 0.0) for r in range(requests)], axis=1
    ).astype(BF16)
    values = v_ref[...].reshape(requests * longest, dim)
    result = jnp.dot(spread, values, preferred_element_type=F32) + own_weight * fresh_value
    pieces = [result[h * requests : (h + 1) * requests] for h in range(group)]
    pieces.append(column_of(adapter, requests).astype(F32))
    block = jnp.concatenate(pieces, axis=1).astype(BF16)
    for i, out in enumerate(outs):

        @pl.when(step == i)
        def _(out=out):
            out[...] = block


def attend_blocks(place, length, adapter, query, fresh_key, fresh_value, keys, values):
    requests, kv, longest, dim = keys.shape
    width = query.shape[1] // kv

    def column(s, place, *_):
        return (0, jnp.bitwise_xor(place[0], s))

    def cache(s, place, *_):
        return (0, jnp.bitwise_xor(place[0], s), 0, 0)

    return pl.pallas_call(
        attend_kernel,
        grid_spec=pltpu.PrefetchScalarGridSpec(
            num_scalar_prefetch=3,
            grid=(kv,),
            in_specs=[
                pl.BlockSpec((requests, width), column),
                pl.BlockSpec((requests, dim), column),
                pl.BlockSpec((requests, dim), column),
                pl.BlockSpec((requests, 1, longest, dim), cache),
                pl.BlockSpec((requests, 1, longest, dim), cache),
            ],
            out_specs=[pl.BlockSpec((requests, width + LANES), lambda s, *_: (0, 0))] * kv,
        ),
        out_shape=[sds((requests, width + LANES))] * kv,
        compiler_params=params(1),
        cost_estimate=cost(2**28, 2 * keys.size * 2),
        name="attend",
    )(place, length, adapter, query, fresh_key, fresh_value, keys, values)


def route_kernel(place, x0, x1, x2, x3, rows_ref, pick_ref, c0, c1, c2, c3, held, *, local, cap):
    me, mine = place[0], place[1]
    count = x0.shape[0]
    for r, x in enumerate((x0, x1, x2, x3)):
        held[pl.ds(pl.multiple_of(jnp.bitwise_xor(me, r) * count, count), count), :] = x[
            ...
        ].astype(F32)
    every = held[...]
    packed = every.astype(BF16)
    rows, wide = every.shape
    width = wide - LANES
    rows_ref[...] = packed[:, :width]
    adapter = every[:, width:].astype(jnp.int32)
    lane = lax.broadcasted_iota(jnp.int32, (rows, LANES), 1)
    part, slot = lax.div(lane, cap), lax.rem(lane, cap)
    first = jnp.bitwise_xor(mine, part) * local
    held_there = (adapter >= first) & (adapter < first + local) & (part < 4)
    held_f = held_there.astype(F32)
    lower = lax.broadcasted_iota(jnp.int32, (rows, rows), 0) >= lax.broadcasted_iota(
        jnp.int32, (rows, rows), 1
    )
    place_in = jnp.dot(
        lower.astype(F32).astype(BF16), held_f.astype(BF16), preferred_element_type=F32
    )
    pick = jnp.where(held_there & (place_in == (slot + 1).astype(F32)), 1.0, 0.0).astype(BF16)
    pick_ref[...] = pick
    chosen = lax.dot_general(
        pick, packed, (((0,), (0,)), ((), ())), preferred_element_type=F32
    ).astype(BF16)
    for r, c in enumerate((c0, c1, c2, c3)):
        c[...] = chosen[r * cap : (r + 1) * cap]


def route(place, blocks, local, cap):
    count, wide = blocks[0].shape
    rows = count * len(blocks)
    smem = pl.BlockSpec(memory_space=pltpu.SMEM)
    vmem = pl.BlockSpec(memory_space=pltpu.VMEM)
    return pl.pallas_call(
        functools.partial(route_kernel, local=local, cap=cap),
        in_specs=[smem] + [vmem] * 4,
        out_specs=[vmem] * 6,
        out_shape=[sds((rows, wide - LANES)), sds((rows, LANES))] + [sds((cap, wide))] * 4,
        scratch_shapes=[pltpu.VMEM((rows, wide), F32)],
        compiler_params=params(),
        cost_estimate=cost(2**20, rows * wide * 8),
        name="route",
    )(place, *blocks)


def project_kernel(place, rows_ref, w_ref, *rest, add):
    step = pl.program_id(0)
    product = jnp.dot(rows_ref[...], w_ref[...], preferred_element_type=F32)
    if add:
        product = product + rest[0][...].astype(F32)
        rest = rest[1:]
    for i, out in enumerate(rest):

        @pl.when(step == i)
        def _(out=out):
            out[...] = product.astype(BF16)


def project(place, rows, weight, width, which, addend=None, tile=512):
    count, depth = rows.shape
    tiles = width // tile
    parts = len(which)

    def column(i, j, place):
        r = which[0] if parts == 1 else jnp.where(i == 0, which[0], which[1])
        return (0, jnp.bitwise_xor(place[0], r) * tiles + j)

    def target(k):
        return lambda i, j, place: (0, jnp.where(i < k, 0, jnp.where(i > k, tiles - 1, j)))

    in_specs = [
        pl.BlockSpec((count, depth), lambda i, j, place: (0, 0)),
        pl.BlockSpec((depth, tile), column),
    ]
    operands = [place, rows, weight]
    if addend is not None:
        in_specs.append(pl.BlockSpec((count, tile), lambda i, j, place: (0, j)))
        operands.append(addend)
    return pl.pallas_call(
        functools.partial(project_kernel, add=addend is not None),
        grid_spec=pltpu.PrefetchScalarGridSpec(
            num_scalar_prefetch=1,
            grid=(parts, tiles),
            in_specs=in_specs,
            out_specs=[pl.BlockSpec((count, tile), target(k)) for k in range(parts)],
        ),
        out_shape=[sds((count, width))] * parts,
        compiler_params=params(2),
        cost_estimate=cost(2 * count * depth * width * parts, depth * width * 2 * parts),
        name="project",
    )(*operands)


def down_kernel(place, c0, c1, c2, c3, down_ref, low_ref, slot_ref):
    local, width, rank = down_ref.shape
    chosen = jnp.concatenate([c[...] for c in (c0, c1, c2, c3)], axis=0)
    values = chosen[:, :width]
    slot = chosen[:, width:].astype(F32).astype(jnp.int32) - place[1] * local
    low = jnp.zeros((chosen.shape[0], rank), F32)
    for a in range(local):
        product = jnp.dot(values, down_ref[a], preferred_element_type=F32)
        low = jnp.where(slot == a, product, low)
    low_ref[...] = low.astype(BF16)
    slot_ref[...] = slot


def down(place, chosen, weight):
    local, width, rank = weight.shape
    rows = chosen[0].shape[0] * len(chosen)
    smem = pl.BlockSpec(memory_space=pltpu.SMEM)
    vmem = pl.BlockSpec(memory_space=pltpu.VMEM)
    return pl.pallas_call(
        down_kernel,
        in_specs=[smem] + [vmem] * 5,
        out_specs=[vmem] * 2,
        out_shape=[sds((rows, rank)), sds((rows, rank), jnp.int32)],
        compiler_params=params(),
        cost_estimate=cost(2 * rows * weight.size, weight.size * 2),
        name="down",
    )(place, *chosen, weight)


def up_kernel(place, ranks, l0, l1, l2, l3, slot_ref, up_ref, *outs):
    local = up_ref.shape[0]
    low = l0[...].astype(F32)
    for share in (l1, l2, l3):
        low = low + share[...].astype(F32)
    slot = slot_ref[...]
    lane = lax.broadcasted_iota(jnp.int32, low.shape, 1)
    total = None
    for a in range(local):
        rank = ranks[place[1] * local + a]
        factor = ADAPTER_SCALE / jnp.full(low.shape, rank, jnp.int32).astype(F32)
        kept = jnp.where((slot == a) & (lane < rank), low * factor, 0.0).astype(BF16)
        product = jnp.dot(kept, up_ref[a], preferred_element_type=F32)
        total = product if total is None else total + product
    adapted = total.astype(BF16)
    cap = outs[0].shape[0]
    for r, out in enumerate(outs):
        out[...] = adapted[r * cap : (r + 1) * cap]


def up(place, ranks, shares, slot, weight, parts, tile=512):
    local, rank, width = weight.shape
    rows = slot.shape[0]
    cap = rows // parts
    tiles = width // tile
    whole = pl.BlockSpec((rows, rank), lambda j, *_: (0, 0))
    return pl.pallas_call(
        up_kernel,
        grid_spec=pltpu.PrefetchScalarGridSpec(
            num_scalar_prefetch=2,
            grid=(tiles,),
            in_specs=[whole] * 5 + [pl.BlockSpec((local, rank, tile), lambda j, *_: (0, 0, j))],
            out_specs=[pl.BlockSpec((cap, tile), lambda j, *_: (0, j))] * parts,
        ),
        out_shape=[sds((cap, width))] * parts,
        compiler_params=params(1),
        cost_estimate=cost(2 * rows * weight.size, weight.size * 2),
        name="up",
    )(place, ranks, *shares, slot, weight)


def finish_kernel(pick_ref, y0, y1, y2, a0, a1, a2, a3, out):
    rows = jnp.concatenate([a[...] for a in (a0, a1, a2, a3)], axis=0)
    pick = pick_ref[...][:, : rows.shape[0]]
    adapted = jnp.dot(pick, rows, preferred_element_type=F32)
    base = y0[...].astype(F32) + y1[...].astype(F32) + y2[...].astype(F32)
    out[...] = (base + adapted).astype(BF16)


def finish(pick, shares, adapted):
    vmem = pl.BlockSpec(memory_space=pltpu.VMEM)
    return pl.pallas_call(
        finish_kernel,
        in_specs=[vmem] * 8,
        out_specs=vmem,
        out_shape=sds(shares[0].shape),
        compiler_params=params(),
        cost_estimate=cost(2**24, shares[0].size * 16),
        name="finish",
    )(pick, *shares, *adapted)


def across(value, axis, r):
    n = lax.axis_size(axis)
    return lax.ppermute(value, axis, [(i, i ^ r) for i in range(n)])


def per_device_four(
    query,
    fresh_key,
    fresh_value,
    stored_keys,
    stored_values,
    cached_length,
    request_adapter,
    rank_per_adapter,
    output_weight,
    adapter_down_weight,
    adapter_up_weight,
):
    tensor_count = lax.axis_size("tensor")
    batch_count = lax.axis_size("batch")
    local = adapter_down_weight.shape[0]
    width = adapter_up_weight.shape[2]
    requests = query.shape[0]
    cap = 2 * requests * tensor_count // batch_count
    place = jnp.stack([lax.axis_index("tensor"), lax.axis_index("batch")]).astype(jnp.int32)

    blocks = attend_blocks(
        place,
        cached_length,
        request_adapter,
        query,
        fresh_key,
        fresh_value,
        stored_keys,
        stored_values,
    )
    blocks = [blocks[0]] + [across(blocks[r], "tensor", r) for r in (1, 2, 3)]
    rows, pick, *chosen = route(place, blocks, local, cap)

    gathered = [chosen[0]] + [across(chosen[r], "batch", r) for r in (1, 2, 3)]
    far, near = project(place, rows, output_weight, width, (3, 1))
    far_in = across(far, "tensor", 1)
    near_in = across(near, "tensor", 1)

    low, slot = down(place, gathered, adapter_down_weight)
    shares = [low] + [across(low, "tensor", r) for r in (1, 2, 3)]
    (cross,) = project(place, rows, output_weight, width, (2,), addend=far_in)
    (mine,) = project(place, rows, output_weight, width, (0,))
    cross_in = across(cross, "tensor", 2)

    lifted = up(place, rank_per_adapter, shares, slot, adapter_up_weight, batch_count)
    lifted = [lifted[0]] + [across(lifted[r], "batch", r) for r in (1, 2, 3)]
    return finish(pick, (mine, near_in, cross_in), lifted)


def attend(query, fresh_key, fresh_value, stored_keys, stored_values, cached_length):
    requests = query.shape[0]
    kv_heads, longest, head_dim = stored_keys.shape[1:]
    group_size = query.shape[1] // (kv_heads * head_dim)
    queries = query.reshape(requests, kv_heads, group_size, head_dim)
    scaling = 1.0 / math.sqrt(head_dim)
    scores = (
        jnp.einsum("rkgd,rkld->rkgl", queries, stored_keys, preferred_element_type=F32) * scaling
    )
    own_score = (
        jnp.einsum(
            "rkgd,rkd->rkg",
            queries,
            fresh_key.reshape(requests, kv_heads, head_dim),
            preferred_element_type=F32,
        )
        * scaling
    )
    valid = (jnp.arange(longest, dtype=jnp.int32)[None, :] < cached_length[:, None])[
        :, None, None, :
    ]
    scores = jnp.where(valid, scores, -1e30)
    highest = jnp.maximum(jnp.max(scores, axis=-1), own_score)
    exponent = jnp.where(valid, jnp.exp(scores - highest[..., None]), 0.0)
    own_exp = jnp.exp(own_score - highest)
    sum_exp = jnp.sum(exponent, axis=-1) + own_exp
    weights = (exponent / sum_exp[..., None]).astype(BF16)
    own_weight = (own_exp / sum_exp).astype(BF16)
    result = jnp.einsum("rkgl,rkld->rkgd", weights, stored_values, preferred_element_type=F32)
    own_value = fresh_value.reshape(requests, kv_heads, 1, head_dim).astype(F32)
    result = result + own_weight.astype(F32)[..., None] * own_value
    return result.reshape(requests, -1).astype(BF16)


def per_device_any(
    query,
    fresh_key,
    fresh_value,
    stored_keys,
    stored_values,
    cached_length,
    request_adapter,
    rank_per_adapter,
    output_weight,
    adapter_down_weight,
    adapter_up_weight,
):
    attended = attend(query, fresh_key, fresh_value, stored_keys, stored_values, cached_length)
    batch_count = lax.axis_size("batch")
    local, _, rank_span = adapter_down_weight.shape
    head_rows = lax.all_to_all(attended, "tensor", split_axis=1, concat_axis=0, tiled=True)
    row_count = head_rows.shape[0]
    products = jnp.dot(head_rows, output_weight, preferred_element_type=F32)
    base = lax.psum_scatter(
        products.astype(BF16), "tensor", scatter_dimension=1, tiled=True
    ).astype(F32)
    all_rows = lax.all_gather(head_rows, "batch", axis=0, tiled=True)
    ids = lax.all_gather(request_adapter, ("batch", "tensor"), axis=0, tiled=True)
    slot = ids - lax.axis_index("batch") * local
    one_hot = slot[:, None] == jnp.arange(local, dtype=jnp.int32)[None, :]
    low_every = jnp.einsum("rk,skj->rsj", all_rows, adapter_down_weight, preferred_element_type=F32)
    low = jnp.sum(jnp.where(one_hot[:, :, None], low_every, 0.0), axis=1)
    low = lax.psum(low.astype(BF16), "tensor").astype(F32)
    adapter_count = rank_per_adapter.shape[0]
    picked = ids[:, None] == jnp.arange(adapter_count, dtype=jnp.int32)[None, :]
    row_rank = jnp.sum(jnp.where(picked, rank_per_adapter[None, :], 0), axis=1)[:, None]
    kept = jnp.arange(rank_span, dtype=jnp.int32)[None, :] < row_rank
    delta = jnp.where(kept, low * (ADAPTER_SCALE / row_rank.astype(F32)), 0.0).astype(BF16)
    widened = jnp.where(one_hot[:, :, None], delta[:, None, :], jnp.zeros((), BF16))
    adapted = jnp.dot(
        widened.reshape(ids.shape[0], local * rank_span),
        adapter_up_weight.reshape(local * rank_span, -1),
        preferred_element_type=F32,
    ).astype(BF16)
    adapted = lax.all_to_all(
        adapted.reshape(batch_count, row_count, -1), "batch", split_axis=0, concat_axis=0, tiled=True
    )
    adapted = jnp.sum(adapted.astype(F32), axis=0)
    return (base + adapted).astype(BF16)


def solution(mesh):
    in_specs = (
        P(("group", "batch", "tensor"), None),
        P(("group", "batch", "tensor"), None),
        P(("group", "batch", "tensor"), None),
        P(("group", "batch", "tensor"), None, None, None),
        P(("group", "batch", "tensor"), None, None, None),
        P(("group", "batch", "tensor")),
        P(("group", "batch", "tensor")),
        P(),
        P("tensor", None),
        P("batch", "tensor", None),
        P("batch", None, "tensor"),
    )
    out_specs = P(("group", "batch"), "tensor")

    def whole(*arrays):
        tensor_count, batch_count = mesh.shape["tensor"], mesh.shape["batch"]
        four = tensor_count == batch_count == arrays[3].shape[1] == 4
        body = per_device_four if four else per_device_any
        return jax.shard_map(
            body, mesh=mesh, in_specs=in_specs, out_specs=out_specs, check_vma=False
        )(*arrays)

    return whole
```

```python
import functools
import math

import jax
import jax.numpy as jnp
from jax import lax
from jax.experimental import pallas as pl
from jax.experimental.pallas import tpu as pltpu
from jax.sharding import PartitionSpec as P

ADAPTER_SCALE = 16.0
F32 = jnp.float32
BF16 = jnp.bfloat16
LANES = 128
MIB = 1024 * 1024


def params(grid_rank=0, vmem=24 * MIB):
    if grid_rank:
        return pltpu.CompilerParams(
            dimension_semantics=("arbitrary",) * grid_rank, vmem_limit_bytes=vmem
        )
    return pltpu.CompilerParams(vmem_limit_bytes=vmem)


def cost(flops, nbytes):
    return pl.CostEstimate(flops=flops, bytes_accessed=nbytes, transcendentals=0)


def sds(shape, dtype=BF16):
    return jax.ShapeDtypeStruct(shape, dtype)


def column_of(ref, count):
    rows = lax.broadcasted_iota(jnp.int32, (count, LANES), 0)
    out = jnp.full((count, LANES), ref[0], jnp.int32)
    for i in range(1, count):
        out = jnp.where(rows == i, ref[i], out)
    return out


def attend_kernel(*refs, kv):
    length_hbm, adapter_hbm, q_hbm, fk_hbm, fv_hbm, k_hbm, v_hbm = refs[:7]
    outs = refs[7 : 7 + kv]
    length, adapter, q_buf, fk_buf, fv_buf, k_buf, v_buf, small, big = refs[7 + kv :]
    requests, _, longest, dim = k_hbm.shape
    width = q_hbm.shape[1] // kv
    group = width // dim
    rows = group * requests
    scaling = 1.0 / math.sqrt(dim)
    me = lax.axis_index("tensor")
    order = tuple(range(kv - 1, -1, -1))

    ready = [
        pltpu.make_async_copy(source, target, small.at[i])
        for i, (source, target) in enumerate(
            (
                (q_hbm, q_buf),
                (fk_hbm, fk_buf),
                (fv_hbm, fv_buf),
                (length_hbm, length),
                (adapter_hbm, adapter),
            )
        )
    ]
    keys_in = {}
    values_in = {}
    for r in order:
        head = jnp.bitwise_xor(me, r)
        keys_in[r] = pltpu.make_async_copy(k_hbm.at[:, head], k_buf.at[r], big.at[0, r])
        values_in[r] = pltpu.make_async_copy(v_hbm.at[:, head], v_buf.at[r], big.at[1, r])
    for copy in ready:
        copy.start()
    for r in order:
        keys_in[r].start()
        values_in[r].start()
    for copy in ready:
        copy.wait()

    request = lax.rem(lax.broadcasted_iota(jnp.int32, (rows, longest), 0), requests)
    lengths = jnp.concatenate([column_of(length, requests)] * group, axis=0)
    valid = lax.broadcasted_iota(jnp.int32, (rows, longest), 1) < lengths
    ids = column_of(adapter, requests).astype(F32)
    for r in order:
        head = jnp.bitwise_xor(me, r)
        mine = pl.ds(pl.multiple_of(head * dim, dim), dim)
        q32 = q_buf[:, pl.ds(pl.multiple_of(head * width, width), width)].astype(F32)
        queries = jnp.concatenate([q32[:, h * dim : (h + 1) * dim] for h in range(group)], axis=0)
        fresh_key = jnp.concatenate([fk_buf[:, mine].astype(F32)] * group, axis=0)
        fresh_value = jnp.concatenate([fv_buf[:, mine].astype(F32)] * group, axis=0)
        own = jnp.sum(queries * fresh_key, axis=1, keepdims=True) * scaling
        keys_in[r].wait()
        every = lax.dot_general(
            queries.astype(BF16),
            k_buf[r].reshape(requests * longest, dim),
            (((1,), (1,)), ((), ())),
            preferred_element_type=F32,
        )
        scores = every[:, :longest]
        for i in range(1, requests):
            scores = jnp.where(request == i, every[:, i * longest : (i + 1) * longest], scores)
        scores = jnp.where(valid, scores * scaling, -1e30)
        highest = jnp.maximum(jnp.max(scores, axis=1, keepdims=True), own)
        exponent = jnp.where(valid, jnp.exp(scores - highest), 0.0)
        own_exp = jnp.exp(own - highest)
        total = jnp.sum(exponent, axis=1, keepdims=True) + own_exp
        weights = exponent / total
        own_weight = (own_exp / total).astype(BF16).astype(F32)
        spread = jnp.concatenate(
            [jnp.where(request == i, weights, 0.0) for i in range(requests)], axis=1
        ).astype(BF16)
        values_in[r].wait()
        result = (
            jnp.dot(
                spread, v_buf[r].reshape(requests * longest, dim), preferred_element_type=F32
            )
            + own_weight * fresh_value
        )
        pieces = [result[h * requests : (h + 1) * requests] for h in range(group)]
        outs[r][...] = jnp.concatenate(pieces + [ids], axis=1).astype(BF16)


def attend_blocks(length, adapter, query, fresh_key, fresh_value, keys, values):
    requests, kv, longest, dim = keys.shape
    width = query.shape[1] // kv
    hbm = pl.BlockSpec(memory_space=pltpu.HBM)
    return pl.pallas_call(
        functools.partial(attend_kernel, kv=kv),
        in_specs=[hbm] * 7,
        out_specs=[pl.BlockSpec(memory_space=pltpu.VMEM)] * kv,
        out_shape=[sds((requests, width + LANES))] * kv,
        scratch_shapes=[
            pltpu.SMEM(length.shape, jnp.int32),
            pltpu.SMEM(adapter.shape, jnp.int32),
            pltpu.VMEM(query.shape, BF16),
            pltpu.VMEM(fresh_key.shape, BF16),
            pltpu.VMEM(fresh_value.shape, BF16),
            pltpu.VMEM((kv, requests, longest, dim), BF16),
            pltpu.VMEM((kv, requests, longest, dim), BF16),
            pltpu.SemaphoreType.DMA((5,)),
            pltpu.SemaphoreType.DMA((2, kv)),
        ],
        compiler_params=params(),
        cost_estimate=cost(2**31, 2 * keys.size * 2),
        name="attend",
    )(*[pltpu.with_memory_space_constraint(x, pltpu.HBM) for x in (length, adapter, query, fresh_key, fresh_value, keys, values)])


def route_kernel(x0, x1, x2, x3, rows_ref, pick_ref, c0, c1, c2, c3, held, *, local, cap):
    me, mine = lax.axis_index("tensor"), lax.axis_index("batch")
    count = x0.shape[0]
    for r, x in enumerate((x0, x1, x2, x3)):
        held[pl.ds(pl.multiple_of(jnp.bitwise_xor(me, r) * count, count), count), :] = x[
            ...
        ].astype(F32)
    every = held[...]
    packed = every.astype(BF16)
    rows, wide = every.shape
    width = wide - LANES
    rows_ref[...] = packed[:, :width]
    adapter = every[:, width:].astype(jnp.int32)
    lane = lax.broadcasted_iota(jnp.int32, (rows, LANES), 1)
    part, slot = lax.div(lane, cap), lax.rem(lane, cap)
    first = jnp.bitwise_xor(mine, part) * local
    held_there = (adapter >= first) & (adapter < first + local) & (part < 4)
    held_f = held_there.astype(F32)
    lower = lax.broadcasted_iota(jnp.int32, (rows, rows), 0) >= lax.broadcasted_iota(
        jnp.int32, (rows, rows), 1
    )
    place_in = jnp.dot(
        lower.astype(F32).astype(BF16), held_f.astype(BF16), preferred_element_type=F32
    )
    pick = jnp.where(held_there & (place_in == (slot + 1).astype(F32)), 1.0, 0.0).astype(BF16)
    pick_ref[...] = pick
    chosen = lax.dot_general(
        pick, packed, (((0,), (0,)), ((), ())), preferred_element_type=F32
    ).astype(BF16)
    for r, c in enumerate((c0, c1, c2, c3)):
        c[...] = chosen[r * cap : (r + 1) * cap]


def route(blocks, local, cap):
    count, wide = blocks[0].shape
    rows = count * len(blocks)
    vmem = pl.BlockSpec(memory_space=pltpu.VMEM)
    return pl.pallas_call(
        functools.partial(route_kernel, local=local, cap=cap),
        in_specs=[vmem] * 4,
        out_specs=[vmem] * 6,
        out_shape=[sds((rows, wide - LANES)), sds((rows, LANES))] + [sds((cap, wide))] * 4,
        scratch_shapes=[pltpu.VMEM((rows, wide), F32)],
        compiler_params=params(),
        cost_estimate=cost(2**20, rows * wide * 8),
        name="route",
    )(*blocks)


def project_kernel(*refs, which, tile, add, after):
    rows_ref, w_hbm = refs[:2]
    addend = refs[2] if add else None
    skip = 2 + add + after
    outs = refs[skip : skip + len(which)]
    buf, sems = refs[skip + len(which) :]
    width = outs[0].shape[1]
    tiles = width // tile
    me = lax.axis_index("tensor")
    copies = []
    for k, r in enumerate(which):
        start = jnp.bitwise_xor(me, r) * width
        for j in range(tiles):
            at = pl.ds(pl.multiple_of(start + j * tile, tile), tile)
            n = k * tiles + j
            copies.append(pltpu.make_async_copy(w_hbm.at[:, at], buf.at[n], sems.at[n]))
    for copy in copies:
        copy.start()
    rows = rows_ref[...]
    for k, out in enumerate(outs):
        for j in range(tiles):
            n = k * tiles + j
            copies[n].wait()
            product = jnp.dot(rows, buf[n], preferred_element_type=F32)
            span = slice(j * tile, (j + 1) * tile)
            if add:
                product = product + addend[:, span].astype(F32)
            out[:, span] = product.astype(BF16)


def project(rows, weight, width, which, addend=None, after=None, tile=512):
    count, depth = rows.shape
    tiles = width // tile
    parts = len(which)
    vmem = pl.BlockSpec(memory_space=pltpu.VMEM)
    in_specs = [vmem, pl.BlockSpec(memory_space=pltpu.HBM)]
    operands = [rows, pltpu.with_memory_space_constraint(weight, pltpu.HBM)]
    if addend is not None:
        in_specs.append(vmem)
        operands.append(addend)
    if after is not None:
        in_specs.append(pl.BlockSpec(memory_space=pl.ANY))
        operands.append(after)
    return pl.pallas_call(
        functools.partial(
            project_kernel,
            which=which,
            tile=tile,
            add=addend is not None,
            after=after is not None,
        ),
        in_specs=in_specs,
        out_specs=[vmem] * parts,
        out_shape=[sds((count, width))] * parts,
        scratch_shapes=[
            pltpu.VMEM((parts * tiles, depth, tile), BF16),
            pltpu.SemaphoreType.DMA((parts * tiles,)),
        ],
        compiler_params=params(),
        cost_estimate=cost(2 * count * depth * width * parts, depth * width * 2 * parts),
        name="project",
    )(*operands)


def down_kernel(c0, c1, c2, c3, down_ref, low_ref, slot_ref):
    local, width, rank = down_ref.shape
    chosen = jnp.concatenate([c[...] for c in (c0, c1, c2, c3)], axis=0)
    values = chosen[:, :width]
    slot = chosen[:, width:].astype(F32).astype(jnp.int32) - lax.axis_index("batch") * local
    low = jnp.zeros((chosen.shape[0], rank), F32)
    for a in range(local):
        product = jnp.dot(values, down_ref[a], preferred_element_type=F32)
        low = jnp.where(slot == a, product, low)
    low_ref[...] = low.astype(BF16)
    slot_ref[...] = slot


def down(chosen, weight):
    local, width, rank = weight.shape
    rows = chosen[0].shape[0] * len(chosen)
    vmem = pl.BlockSpec(memory_space=pltpu.VMEM)
    return pl.pallas_call(
        down_kernel,
        in_specs=[vmem] * 5,
        out_specs=[vmem] * 2,
        out_shape=[sds((rows, rank)), sds((rows, rank), jnp.int32)],
        compiler_params=params(),
        cost_estimate=cost(2**34, weight.size * 2),
        name="down",
    )(*chosen, weight)


def up_kernel(ranks, l0, l1, l2, l3, slot_ref, up_ref, *outs):
    local = up_ref.shape[0]
    low = l0[...].astype(F32)
    for share in (l1, l2, l3):
        low = low + share[...].astype(F32)
    slot = slot_ref[...]
    lane = lax.broadcasted_iota(jnp.int32, low.shape, 1)
    total = None
    for a in range(local):
        rank = ranks[lax.axis_index("batch") * local + a]
        factor = ADAPTER_SCALE / jnp.full(low.shape, rank, jnp.int32).astype(F32)
        kept = jnp.where((slot == a) & (lane < rank), low * factor, 0.0).astype(BF16)
        product = jnp.dot(kept, up_ref[a], preferred_element_type=F32)
        total = product if total is None else total + product
    adapted = total.astype(BF16)
    cap = outs[0].shape[0]
    for r, out in enumerate(outs):
        out[...] = adapted[r * cap : (r + 1) * cap]


def up(ranks, shares, slot, weight, parts, tile=512):
    local, rank, width = weight.shape
    rows = slot.shape[0]
    cap = rows // parts
    tiles = width // tile
    whole = pl.BlockSpec((rows, rank), lambda j, *_: (0, 0))
    return pl.pallas_call(
        up_kernel,
        grid_spec=pltpu.PrefetchScalarGridSpec(
            num_scalar_prefetch=1,
            grid=(tiles,),
            in_specs=[whole] * 5 + [pl.BlockSpec((local, rank, tile), lambda j, *_: (0, 0, j))],
            out_specs=[pl.BlockSpec((cap, tile), lambda j, *_: (0, j))] * parts,
        ),
        out_shape=[sds((cap, width))] * parts,
        compiler_params=params(1),
        cost_estimate=cost(2**34, weight.size * 2),
        name="up",
    )(ranks, *shares, slot, weight)


def finish_kernel(pick_ref, y0, y1, y2, a0, a1, a2, a3, out):
    rows = jnp.concatenate([a[...] for a in (a0, a1, a2, a3)], axis=0)
    pick = pick_ref[...][:, : rows.shape[0]]
    adapted = jnp.dot(pick, rows, preferred_element_type=F32)
    base = y0[...].astype(F32) + y1[...].astype(F32) + y2[...].astype(F32)
    out[...] = (base + adapted).astype(BF16)


def finish(pick, shares, adapted):
    vmem = pl.BlockSpec(memory_space=pltpu.VMEM)
    return pl.pallas_call(
        finish_kernel,
        in_specs=[vmem] * 8,
        out_specs=vmem,
        out_shape=sds(shares[0].shape),
        compiler_params=params(),
        cost_estimate=cost(2**24, shares[0].size * 16),
        name="finish",
    )(pick, *shares, *adapted)


def across(value, axis, r):
    n = lax.axis_size(axis)
    return lax.ppermute(value, axis, [(i, i ^ r) for i in range(n)])


def per_device_four(
    query,
    fresh_key,
    fresh_value,
    stored_keys,
    stored_values,
    cached_length,
    request_adapter,
    rank_per_adapter,
    output_weight,
    adapter_down_weight,
    adapter_up_weight,
):
    tensor_count = lax.axis_size("tensor")
    batch_count = lax.axis_size("batch")
    local = adapter_down_weight.shape[0]
    width = adapter_up_weight.shape[2]
    requests = query.shape[0]
    cap = 2 * requests * tensor_count // batch_count
    blocks = attend_blocks(
        cached_length,
        request_adapter,
        query,
        fresh_key,
        fresh_value,
        stored_keys,
        stored_values,
    )
    blocks = [blocks[0]] + [across(blocks[r], "tensor", r) for r in (1, 2, 3)]
    rows, pick, *chosen = route(blocks, local, cap)

    gathered = [chosen[0]] + [across(chosen[r], "batch", r) for r in (1, 2, 3)]
    far, near = project(rows, output_weight, width, (3, 1))
    far_in = across(far, "tensor", 1)
    near_in = across(near, "tensor", 1)

    low, slot = down(gathered, adapter_down_weight)
    shares = [low] + [across(low, "tensor", r) for r in (1, 2, 3)]
    (cross,) = project(rows, output_weight, width, (2,), addend=far_in)
    (mine,) = project(rows, output_weight, width, (0,))
    cross_in = across(cross, "tensor", 2)

    lifted = up(rank_per_adapter, shares, slot, adapter_up_weight, batch_count)
    lifted = [lifted[0]] + [across(lifted[r], "batch", r) for r in (1, 2, 3)]
    return finish(pick, (mine, near_in, cross_in), lifted)


def attend(query, fresh_key, fresh_value, stored_keys, stored_values, cached_length):
    requests = query.shape[0]
    kv_heads, longest, head_dim = stored_keys.shape[1:]
    group_size = query.shape[1] // (kv_heads * head_dim)
    queries = query.reshape(requests, kv_heads, group_size, head_dim)
    scaling = 1.0 / math.sqrt(head_dim)
    scores = (
        jnp.einsum("rkgd,rkld->rkgl", queries, stored_keys, preferred_element_type=F32) * scaling
    )
    own_score = (
        jnp.einsum(
            "rkgd,rkd->rkg",
            queries,
            fresh_key.reshape(requests, kv_heads, head_dim),
            preferred_element_type=F32,
        )
        * scaling
    )
    valid = (jnp.arange(longest, dtype=jnp.int32)[None, :] < cached_length[:, None])[
        :, None, None, :
    ]
    scores = jnp.where(valid, scores, -1e30)
    highest = jnp.maximum(jnp.max(scores, axis=-1), own_score)
    exponent = jnp.where(valid, jnp.exp(scores - highest[..., None]), 0.0)
    own_exp = jnp.exp(own_score - highest)
    sum_exp = jnp.sum(exponent, axis=-1) + own_exp
    weights = (exponent / sum_exp[..., None]).astype(BF16)
    own_weight = (own_exp / sum_exp).astype(BF16)
    result = jnp.einsum("rkgl,rkld->rkgd", weights, stored_values, preferred_element_type=F32)
    own_value = fresh_value.reshape(requests, kv_heads, 1, head_dim).astype(F32)
    result = result + own_weight.astype(F32)[..., None] * own_value
    return result.reshape(requests, -1).astype(BF16)


def per_device_any(
    query,
    fresh_key,
    fresh_value,
    stored_keys,
    stored_values,
    cached_length,
    request_adapter,
    rank_per_adapter,
    output_weight,
    adapter_down_weight,
    adapter_up_weight,
):
    attended = attend(query, fresh_key, fresh_value, stored_keys, stored_values, cached_length)
    batch_count = lax.axis_size("batch")
    local, _, rank_span = adapter_down_weight.shape
    head_rows = lax.all_to_all(attended, "tensor", split_axis=1, concat_axis=0, tiled=True)
    row_count = head_rows.shape[0]
    products = jnp.dot(head_rows, output_weight, preferred_element_type=F32)
    base = lax.psum_scatter(
        products.astype(BF16), "tensor", scatter_dimension=1, tiled=True
    ).astype(F32)
    all_rows = lax.all_gather(head_rows, "batch", axis=0, tiled=True)
    ids = lax.all_gather(request_adapter, ("batch", "tensor"), axis=0, tiled=True)
    slot = ids - lax.axis_index("batch") * local
    one_hot = slot[:, None] == jnp.arange(local, dtype=jnp.int32)[None, :]
    low_every = jnp.einsum("rk,skj->rsj", all_rows, adapter_down_weight, preferred_element_type=F32)
    low = jnp.sum(jnp.where(one_hot[:, :, None], low_every, 0.0), axis=1)
    low = lax.psum(low.astype(BF16), "tensor").astype(F32)
    adapter_count = rank_per_adapter.shape[0]
    picked = ids[:, None] == jnp.arange(adapter_count, dtype=jnp.int32)[None, :]
    row_rank = jnp.sum(jnp.where(picked, rank_per_adapter[None, :], 0), axis=1)[:, None]
    kept = jnp.arange(rank_span, dtype=jnp.int32)[None, :] < row_rank
    delta = jnp.where(kept, low * (ADAPTER_SCALE / row_rank.astype(F32)), 0.0).astype(BF16)
    widened = jnp.where(one_hot[:, :, None], delta[:, None, :], jnp.zeros((), BF16))
    adapted = jnp.dot(
        widened.reshape(ids.shape[0], local * rank_span),
        adapter_up_weight.reshape(local * rank_span, -1),
        preferred_element_type=F32,
    ).astype(BF16)
    adapted = lax.all_to_all(
        adapted.reshape(batch_count, row_count, -1), "batch", split_axis=0, concat_axis=0, tiled=True
    )
    adapted = jnp.sum(adapted.astype(F32), axis=0)
    return (base + adapted).astype(BF16)


def solution(mesh):
    in_specs = (
        P(("group", "batch", "tensor"), None),
        P(("group", "batch", "tensor"), None),
        P(("group", "batch", "tensor"), None),
        P(("group", "batch", "tensor"), None, None, None),
        P(("group", "batch", "tensor"), None, None, None),
        P(("group", "batch", "tensor")),
        P(("group", "batch", "tensor")),
        P(),
        P("tensor", None),
        P("batch", "tensor", None),
        P("batch", None, "tensor"),
    )
    out_specs = P(("group", "batch"), "tensor")

    def whole(*arrays):
        tensor_count, batch_count = mesh.shape["tensor"], mesh.shape["batch"]
        four = tensor_count == batch_count == arrays[3].shape[1] == 4
        body = per_device_four if four else per_device_any
        return jax.shard_map(
            body, mesh=mesh, in_specs=in_specs, out_specs=out_specs, check_vma=False
        )(*arrays)

    return whole
```

```python
import functools
import math

import jax
import jax.numpy as jnp
from jax import lax
from jax.experimental import pallas as pl
from jax.experimental.pallas import tpu as pltpu
from jax.sharding import PartitionSpec as P

ADAPTER_SCALE = 16.0
F32 = jnp.float32
BF16 = jnp.bfloat16
LANES = 128
MIB = 1024 * 1024


def params(grid_rank=0, vmem=24 * MIB):
    if grid_rank:
        return pltpu.CompilerParams(
            dimension_semantics=("arbitrary",) * grid_rank, vmem_limit_bytes=vmem
        )
    return pltpu.CompilerParams(vmem_limit_bytes=vmem)


def cost(flops, nbytes):
    return pl.CostEstimate(flops=flops, bytes_accessed=nbytes, transcendentals=0)


def sds(shape, dtype=BF16):
    return jax.ShapeDtypeStruct(shape, dtype)


def column_of(ref, count):
    rows = lax.broadcasted_iota(jnp.int32, (count, LANES), 0)
    out = jnp.full((count, LANES), ref[0], jnp.int32)
    for i in range(1, count):
        out = jnp.where(rows == i, ref[i], out)
    return out


def attend_kernel(*refs, kv):
    length_hbm, adapter_hbm, q_hbm, fk_hbm, fv_hbm, k_hbm, v_hbm = refs[:7]
    outs = refs[7 : 7 + kv]
    length, adapter, q_buf, fk_buf, fv_buf, k_buf, v_buf, small, big = refs[7 + kv :]
    requests, _, longest, dim = k_hbm.shape
    width = q_hbm.shape[1] // kv
    group = width // dim
    rows = group * requests
    scaling = 1.0 / math.sqrt(dim)
    me = lax.axis_index("tensor")
    order = tuple(range(kv - 1, -1, -1))

    ready = [
        pltpu.make_async_copy(source, target, small.at[i])
        for i, (source, target) in enumerate(
            (
                (q_hbm, q_buf),
                (fk_hbm, fk_buf),
                (fv_hbm, fv_buf),
                (length_hbm, length),
                (adapter_hbm, adapter),
            )
        )
    ]
    keys_in = {}
    values_in = {}
    for r in order:
        head = jnp.bitwise_xor(me, r)
        keys_in[r] = pltpu.make_async_copy(k_hbm.at[:, head], k_buf.at[r], big.at[0, r])
        values_in[r] = pltpu.make_async_copy(v_hbm.at[:, head], v_buf.at[r], big.at[1, r])
    for copy in ready:
        copy.start()
    for r in order:
        keys_in[r].start()
        values_in[r].start()
    for copy in ready:
        copy.wait()

    request = lax.rem(lax.broadcasted_iota(jnp.int32, (rows, longest), 0), requests)
    lengths = jnp.concatenate([column_of(length, requests)] * group, axis=0)
    valid = lax.broadcasted_iota(jnp.int32, (rows, longest), 1) < lengths
    ids = column_of(adapter, requests).astype(F32)
    scores, own, fresh_value = {}, {}, {}
    for r in order:
        head = jnp.bitwise_xor(me, r)
        mine = pl.ds(pl.multiple_of(head * dim, dim), dim)
        q32 = q_buf[:, pl.ds(pl.multiple_of(head * width, width), width)].astype(F32)
        queries = jnp.concatenate([q32[:, h * dim : (h + 1) * dim] for h in range(group)], axis=0)
        fresh_key = jnp.concatenate([fk_buf[:, mine].astype(F32)] * group, axis=0)
        fresh_value[r] = jnp.concatenate([fv_buf[:, mine].astype(F32)] * group, axis=0)
        own[r] = jnp.sum(queries * fresh_key, axis=1, keepdims=True) * scaling
        scores[r] = queries.astype(BF16)
    for r in order:
        keys_in[r].wait()
    for r in order:
        every = lax.dot_general(
            scores[r],
            k_buf[r].reshape(requests * longest, dim),
            (((1,), (1,)), ((), ())),
            preferred_element_type=F32,
        )
        picked = every[:, :longest]
        for i in range(1, requests):
            picked = jnp.where(request == i, every[:, i * longest : (i + 1) * longest], picked)
        scores[r] = jnp.where(valid, picked * scaling, -1e30)
    highest = {r: jnp.maximum(jnp.max(scores[r], axis=1, keepdims=True), own[r]) for r in order}
    exponent = {r: jnp.where(valid, jnp.exp(scores[r] - highest[r]), 0.0) for r in order}
    own_exp = {r: jnp.exp(own[r] - highest[r]) for r in order}
    inverse = {
        r: 1.0 / (jnp.sum(exponent[r], axis=1, keepdims=True) + own_exp[r]) for r in order
    }
    spread = {}
    for r in order:
        weights = exponent[r] * inverse[r]
        spread[r] = jnp.concatenate(
            [jnp.where(request == i, weights, 0.0) for i in range(requests)], axis=1
        ).astype(BF16)
    for r in order:
        values_in[r].wait()
    for r in order:
        own_weight = (own_exp[r] * inverse[r]).astype(BF16).astype(F32)
        result = (
            jnp.dot(
                spread[r], v_buf[r].reshape(requests * longest, dim), preferred_element_type=F32
            )
            + own_weight * fresh_value[r]
        )
        pieces = [result[h * requests : (h + 1) * requests] for h in range(group)]
        outs[r][...] = jnp.concatenate(pieces + [ids], axis=1).astype(BF16)


def attend_blocks(length, adapter, query, fresh_key, fresh_value, keys, values):
    requests, kv, longest, dim = keys.shape
    width = query.shape[1] // kv
    hbm = pl.BlockSpec(memory_space=pltpu.HBM)
    return pl.pallas_call(
        functools.partial(attend_kernel, kv=kv),
        in_specs=[hbm] * 7,
        out_specs=[pl.BlockSpec(memory_space=pltpu.VMEM)] * kv,
        out_shape=[sds((requests, width + LANES))] * kv,
        scratch_shapes=[
            pltpu.SMEM(length.shape, jnp.int32),
            pltpu.SMEM(adapter.shape, jnp.int32),
            pltpu.VMEM(query.shape, BF16),
            pltpu.VMEM(fresh_key.shape, BF16),
            pltpu.VMEM(fresh_value.shape, BF16),
            pltpu.VMEM((kv, requests, longest, dim), BF16),
            pltpu.VMEM((kv, requests, longest, dim), BF16),
            pltpu.SemaphoreType.DMA((5,)),
            pltpu.SemaphoreType.DMA((2, kv)),
        ],
        compiler_params=params(),
        cost_estimate=cost(2**31, 2 * keys.size * 2),
        name="attend",
    )(*[pltpu.with_memory_space_constraint(x, pltpu.HBM) for x in (length, adapter, query, fresh_key, fresh_value, keys, values)])


def route_kernel(x0, x1, x2, x3, rows_ref, pick_ref, c0, c1, c2, c3, held, *, local, cap):
    me, mine = lax.axis_index("tensor"), lax.axis_index("batch")
    count = x0.shape[0]
    for r, x in enumerate((x0, x1, x2, x3)):
        held[pl.ds(pl.multiple_of(jnp.bitwise_xor(me, r) * count, count), count), :] = x[
            ...
        ].astype(F32)
    every = held[...]
    packed = every.astype(BF16)
    rows, wide = every.shape
    width = wide - LANES
    rows_ref[...] = packed[:, :width]
    adapter = every[:, width:].astype(jnp.int32)
    lane = lax.broadcasted_iota(jnp.int32, (rows, LANES), 1)
    part, slot = lax.div(lane, cap), lax.rem(lane, cap)
    first = jnp.bitwise_xor(mine, part) * local
    held_there = (adapter >= first) & (adapter < first + local) & (part < 4)
    held_f = held_there.astype(F32)
    lower = lax.broadcasted_iota(jnp.int32, (rows, rows), 0) >= lax.broadcasted_iota(
        jnp.int32, (rows, rows), 1
    )
    place_in = jnp.dot(
        lower.astype(F32).astype(BF16), held_f.astype(BF16), preferred_element_type=F32
    )
    pick = jnp.where(held_there & (place_in == (slot + 1).astype(F32)), 1.0, 0.0).astype(BF16)
    pick_ref[...] = pick
    chosen = lax.dot_general(
        pick, packed, (((0,), (0,)), ((), ())), preferred_element_type=F32
    ).astype(BF16)
    for r, c in enumerate((c0, c1, c2, c3)):
        c[...] = chosen[r * cap : (r + 1) * cap]


def route(blocks, local, cap):
    count, wide = blocks[0].shape
    rows = count * len(blocks)
    vmem = pl.BlockSpec(memory_space=pltpu.VMEM)
    return pl.pallas_call(
        functools.partial(route_kernel, local=local, cap=cap),
        in_specs=[vmem] * 4,
        out_specs=[vmem] * 6,
        out_shape=[sds((rows, wide - LANES)), sds((rows, LANES))] + [sds((cap, wide))] * 4,
        scratch_shapes=[pltpu.VMEM((rows, wide), F32)],
        compiler_params=params(),
        cost_estimate=cost(2**20, rows * wide * 8),
        name="route",
    )(*blocks)


def project_kernel(*refs, which, tile, add, after):
    rows_ref, w_hbm = refs[:2]
    addend = refs[2] if add else None
    skip = 2 + add + after
    outs = refs[skip : skip + len(which)]
    buf, sems = refs[skip + len(which) :]
    width = outs[0].shape[1]
    tiles = width // tile
    me = lax.axis_index("tensor")
    copies = []
    for k, r in enumerate(which):
        start = jnp.bitwise_xor(me, r) * width
        for j in range(tiles):
            at = pl.ds(pl.multiple_of(start + j * tile, tile), tile)
            n = k * tiles + j
            copies.append(pltpu.make_async_copy(w_hbm.at[:, at], buf.at[n], sems.at[n]))
    for copy in copies:
        copy.start()
    rows = rows_ref[...]
    for k, out in enumerate(outs):
        for j in range(tiles):
            n = k * tiles + j
            copies[n].wait()
            product = jnp.dot(rows, buf[n], preferred_element_type=F32)
            span = slice(j * tile, (j + 1) * tile)
            if add:
                product = product + addend[:, span].astype(F32)
            out[:, span] = product.astype(BF16)


def project(rows, weight, width, which, addend=None, after=None, tile=512):
    count, depth = rows.shape
    tiles = width // tile
    parts = len(which)
    vmem = pl.BlockSpec(memory_space=pltpu.VMEM)
    in_specs = [vmem, pl.BlockSpec(memory_space=pltpu.HBM)]
    operands = [rows, pltpu.with_memory_space_constraint(weight, pltpu.HBM)]
    if addend is not None:
        in_specs.append(vmem)
        operands.append(addend)
    if after is not None:
        in_specs.append(pl.BlockSpec(memory_space=pl.ANY))
        operands.append(after)
    return pl.pallas_call(
        functools.partial(
            project_kernel,
            which=which,
            tile=tile,
            add=addend is not None,
            after=after is not None,
        ),
        in_specs=in_specs,
        out_specs=[vmem] * parts,
        out_shape=[sds((count, width))] * parts,
        scratch_shapes=[
            pltpu.VMEM((parts * tiles, depth, tile), BF16),
            pltpu.SemaphoreType.DMA((parts * tiles,)),
        ],
        compiler_params=params(),
        cost_estimate=cost(2 * count * depth * width * parts, depth * width * 2 * parts),
        name="project",
    )(*operands)


def down_kernel(c0, c1, c2, c3, down_ref, low_ref, slot_ref):
    local, width, rank = down_ref.shape
    chosen = jnp.concatenate([c[...] for c in (c0, c1, c2, c3)], axis=0)
    values = chosen[:, :width]
    slot = chosen[:, width:].astype(F32).astype(jnp.int32) - lax.axis_index("batch") * local
    low = jnp.zeros((chosen.shape[0], rank), F32)
    for a in range(local):
        product = jnp.dot(values, down_ref[a], preferred_element_type=F32)
        low = jnp.where(slot == a, product, low)
    low_ref[...] = low.astype(BF16)
    slot_ref[...] = slot


def down(chosen, weight):
    local, width, rank = weight.shape
    rows = chosen[0].shape[0] * len(chosen)
    vmem = pl.BlockSpec(memory_space=pltpu.VMEM)
    return pl.pallas_call(
        down_kernel,
        in_specs=[vmem] * 5,
        out_specs=[vmem] * 2,
        out_shape=[sds((rows, rank)), sds((rows, rank), jnp.int32)],
        compiler_params=params(),
        cost_estimate=cost(2**34, weight.size * 2),
        name="down",
    )(*chosen, weight)


def up_kernel(ranks, l0, l1, l2, l3, slot_ref, up_ref, *outs, tile):
    local, _, width = up_ref.shape
    low = l0[...].astype(F32)
    for share in (l1, l2, l3):
        low = low + share[...].astype(F32)
    slot = slot_ref[...]
    lane = lax.broadcasted_iota(jnp.int32, low.shape, 1)
    kept = []
    for a in range(local):
        rank = ranks[lax.axis_index("batch") * local + a]
        factor = ADAPTER_SCALE / jnp.full(low.shape, rank, jnp.int32).astype(F32)
        kept.append(jnp.where((slot == a) & (lane < rank), low * factor, 0.0).astype(BF16))
    cap = outs[0].shape[0]
    for start in range(0, width, tile):
        span = slice(start, start + tile)
        total = jnp.dot(kept[0], up_ref[0, :, span], preferred_element_type=F32)
        for a in range(1, local):
            total = total + jnp.dot(kept[a], up_ref[a, :, span], preferred_element_type=F32)
        adapted = total.astype(BF16)
        for r, out in enumerate(outs):
            out[:, span] = adapted[r * cap : (r + 1) * cap]


def up(ranks, shares, slot, weight, parts, tile=512):
    local, rank, width = weight.shape
    rows = slot.shape[0]
    cap = rows // parts
    vmem = pl.BlockSpec(memory_space=pltpu.VMEM)
    return pl.pallas_call(
        functools.partial(up_kernel, tile=tile),
        in_specs=[pl.BlockSpec(memory_space=pltpu.SMEM)] + [vmem] * 6,
        out_specs=[vmem] * parts,
        out_shape=[sds((cap, width))] * parts,
        compiler_params=params(),
        cost_estimate=cost(2**34, weight.size * 2),
        name="up",
    )(ranks, *shares, slot, weight)


def finish_kernel(pick_ref, y0, y1, y2, a0, a1, a2, a3, out):
    rows = jnp.concatenate([a[...] for a in (a0, a1, a2, a3)], axis=0)
    pick = pick_ref[...][:, : rows.shape[0]]
    adapted = jnp.dot(pick, rows, preferred_element_type=F32)
    base = y0[...].astype(F32) + y1[...].astype(F32) + y2[...].astype(F32)
    out[...] = (base + adapted).astype(BF16)


def finish(pick, shares, adapted):
    vmem = pl.BlockSpec(memory_space=pltpu.VMEM)
    return pl.pallas_call(
        finish_kernel,
        in_specs=[vmem] * 8,
        out_specs=vmem,
        out_shape=sds(shares[0].shape),
        compiler_params=params(),
        cost_estimate=cost(2**24, shares[0].size * 16),
        name="finish",
    )(pick, *shares, *adapted)


def across(value, axis, r):
    n = lax.axis_size(axis)
    return lax.ppermute(value, axis, [(i, i ^ r) for i in range(n)])


def per_device_four(
    query,
    fresh_key,
    fresh_value,
    stored_keys,
    stored_values,
    cached_length,
    request_adapter,
    rank_per_adapter,
    output_weight,
    adapter_down_weight,
    adapter_up_weight,
):
    tensor_count = lax.axis_size("tensor")
    batch_count = lax.axis_size("batch")
    local = adapter_down_weight.shape[0]
    width = adapter_up_weight.shape[2]
    requests = query.shape[0]
    cap = 2 * requests * tensor_count // batch_count
    blocks = attend_blocks(
        cached_length,
        request_adapter,
        query,
        fresh_key,
        fresh_value,
        stored_keys,
        stored_values,
    )
    blocks = [blocks[0]] + [across(blocks[r], "tensor", r) for r in (1, 2, 3)]
    rows, pick, *chosen = route(blocks, local, cap)

    gathered = [chosen[0]] + [across(chosen[r], "batch", r) for r in (1, 2, 3)]
    far, near = project(rows, output_weight, width, (3, 1))
    far_in = across(far, "tensor", 1)
    near_in = across(near, "tensor", 1)

    low, slot = down(gathered, adapter_down_weight)
    shares = [low] + [across(low, "tensor", r) for r in (1, 2, 3)]
    (cross,) = project(rows, output_weight, width, (2,), addend=far_in)
    (mine,) = project(rows, output_weight, width, (0,))
    cross_in = across(cross, "tensor", 2)

    lifted = up(rank_per_adapter, shares, slot, adapter_up_weight, batch_count)
    lifted = [lifted[0]] + [across(lifted[r], "batch", r) for r in (1, 2, 3)]
    return finish(pick, (mine, near_in, cross_in), lifted)


def attend(query, fresh_key, fresh_value, stored_keys, stored_values, cached_length):
    requests = query.shape[0]
    kv_heads, longest, head_dim = stored_keys.shape[1:]
    group_size = query.shape[1] // (kv_heads * head_dim)
    queries = query.reshape(requests, kv_heads, group_size, head_dim)
    scaling = 1.0 / math.sqrt(head_dim)
    scores = (
        jnp.einsum("rkgd,rkld->rkgl", queries, stored_keys, preferred_element_type=F32) * scaling
    )
    own_score = (
        jnp.einsum(
            "rkgd,rkd->rkg",
            queries,
            fresh_key.reshape(requests, kv_heads, head_dim),
            preferred_element_type=F32,
        )
        * scaling
    )
    valid = (jnp.arange(longest, dtype=jnp.int32)[None, :] < cached_length[:, None])[
        :, None, None, :
    ]
    scores = jnp.where(valid, scores, -1e30)
    highest = jnp.maximum(jnp.max(scores, axis=-1), own_score)
    exponent = jnp.where(valid, jnp.exp(scores - highest[..., None]), 0.0)
    own_exp = jnp.exp(own_score - highest)
    sum_exp = jnp.sum(exponent, axis=-1) + own_exp
    weights = (exponent / sum_exp[..., None]).astype(BF16)
    own_weight = (own_exp / sum_exp).astype(BF16)
    result = jnp.einsum("rkgl,rkld->rkgd", weights, stored_values, preferred_element_type=F32)
    own_value = fresh_value.reshape(requests, kv_heads, 1, head_dim).astype(F32)
    result = result + own_weight.astype(F32)[..., None] * own_value
    return result.reshape(requests, -1).astype(BF16)


def per_device_any(
    query,
    fresh_key,
    fresh_value,
    stored_keys,
    stored_values,
    cached_length,
    request_adapter,
    rank_per_adapter,
    output_weight,
    adapter_down_weight,
    adapter_up_weight,
):
    attended = attend(query, fresh_key, fresh_value, stored_keys, stored_values, cached_length)
    batch_count = lax.axis_size("batch")
    local, _, rank_span = adapter_down_weight.shape
    head_rows = lax.all_to_all(attended, "tensor", split_axis=1, concat_axis=0, tiled=True)
    row_count = head_rows.shape[0]
    products = jnp.dot(head_rows, output_weight, preferred_element_type=F32)
    base = lax.psum_scatter(
        products.astype(BF16), "tensor", scatter_dimension=1, tiled=True
    ).astype(F32)
    all_rows = lax.all_gather(head_rows, "batch", axis=0, tiled=True)
    ids = lax.all_gather(request_adapter, ("batch", "tensor"), axis=0, tiled=True)
    slot = ids - lax.axis_index("batch") * local
    one_hot = slot[:, None] == jnp.arange(local, dtype=jnp.int32)[None, :]
    low_every = jnp.einsum("rk,skj->rsj", all_rows, adapter_down_weight, preferred_element_type=F32)
    low = jnp.sum(jnp.where(one_hot[:, :, None], low_every, 0.0), axis=1)
    low = lax.psum(low.astype(BF16), "tensor").astype(F32)
    adapter_count = rank_per_adapter.shape[0]
    picked = ids[:, None] == jnp.arange(adapter_count, dtype=jnp.int32)[None, :]
    row_rank = jnp.sum(jnp.where(picked, rank_per_adapter[None, :], 0), axis=1)[:, None]
    kept = jnp.arange(rank_span, dtype=jnp.int32)[None, :] < row_rank
    delta = jnp.where(kept, low * (ADAPTER_SCALE / row_rank.astype(F32)), 0.0).astype(BF16)
    widened = jnp.where(one_hot[:, :, None], delta[:, None, :], jnp.zeros((), BF16))
    adapted = jnp.dot(
        widened.reshape(ids.shape[0], local * rank_span),
        adapter_up_weight.reshape(local * rank_span, -1),
        preferred_element_type=F32,
    ).astype(BF16)
    adapted = lax.all_to_all(
        adapted.reshape(batch_count, row_count, -1), "batch", split_axis=0, concat_axis=0, tiled=True
    )
    adapted = jnp.sum(adapted.astype(F32), axis=0)
    return (base + adapted).astype(BF16)


def solution(mesh):
    in_specs = (
        P(("group", "batch", "tensor"), None),
        P(("group", "batch", "tensor"), None),
        P(("group", "batch", "tensor"), None),
        P(("group", "batch", "tensor"), None, None, None),
        P(("group", "batch", "tensor"), None, None, None),
        P(("group", "batch", "tensor")),
        P(("group", "batch", "tensor")),
        P(),
        P("tensor", None),
        P("batch", "tensor", None),
        P("batch", None, "tensor"),
    )
    out_specs = P(("group", "batch"), "tensor")

    def whole(*arrays):
        tensor_count, batch_count = mesh.shape["tensor"], mesh.shape["batch"]
        four = tensor_count == batch_count == arrays[3].shape[1] == 4
        body = per_device_four if four else per_device_any
        return jax.shard_map(
            body, mesh=mesh, in_specs=in_specs, out_specs=out_specs, check_vma=False
        )(*arrays)

    return whole
```

```python
import functools
import math

import jax
import jax.numpy as jnp
from jax import lax
from jax.experimental import pallas as pl
from jax.experimental.pallas import tpu as pltpu
from jax.sharding import PartitionSpec as P

ADAPTER_SCALE = 16.0
F32 = jnp.float32
BF16 = jnp.bfloat16
LANES = 128
MIB = 1024 * 1024


def params(grid_rank=0, vmem=24 * MIB):
    if grid_rank:
        return pltpu.CompilerParams(
            dimension_semantics=("arbitrary",) * grid_rank, vmem_limit_bytes=vmem
        )
    return pltpu.CompilerParams(vmem_limit_bytes=vmem)


def cost(flops, nbytes):
    return pl.CostEstimate(flops=flops, bytes_accessed=nbytes, transcendentals=0)


def sds(shape, dtype=BF16):
    return jax.ShapeDtypeStruct(shape, dtype)


def column_of(ref, count):
    rows = lax.broadcasted_iota(jnp.int32, (count, LANES), 0)
    out = jnp.full((count, LANES), ref[0], jnp.int32)
    for i in range(1, count):
        out = jnp.where(rows == i, ref[i], out)
    return out


def attend_kernel(*refs, kv):
    length_hbm, adapter_hbm, q_hbm, fk_hbm, fv_hbm, k_hbm, v_hbm = refs[:7]
    outs = refs[7 : 7 + kv]
    length, adapter, q_buf, fk_buf, fv_buf, k_buf, v_buf, small, big = refs[7 + kv :]
    requests, _, longest, dim = k_hbm.shape
    width = q_hbm.shape[1] // kv
    group = width // dim
    rows = group * requests
    scaling = 1.0 / math.sqrt(dim)
    me = lax.axis_index("tensor")
    order = tuple(range(kv - 1, -1, -1))

    ready = [
        pltpu.make_async_copy(source, target, small.at[i])
        for i, (source, target) in enumerate(
            (
                (q_hbm, q_buf),
                (fk_hbm, fk_buf),
                (fv_hbm, fv_buf),
                (length_hbm, length),
                (adapter_hbm, adapter),
            )
        )
    ]
    keys_in = {}
    values_in = {}
    for r in order:
        head = jnp.bitwise_xor(me, r)
        keys_in[r] = pltpu.make_async_copy(k_hbm.at[:, head], k_buf.at[r], big.at[0, r])
        values_in[r] = pltpu.make_async_copy(v_hbm.at[:, head], v_buf.at[r], big.at[1, r])
    for copy in ready:
        copy.start()
    for r in order:
        keys_in[r].start()
        values_in[r].start()
    for copy in ready:
        copy.wait()

    request = lax.rem(lax.broadcasted_iota(jnp.int32, (rows, longest), 0), requests)
    lengths = jnp.concatenate([column_of(length, requests)] * group, axis=0)
    valid = lax.broadcasted_iota(jnp.int32, (rows, longest), 1) < lengths
    ids = column_of(adapter, requests).astype(F32)
    scores, own, fresh_value = {}, {}, {}
    for r in order:
        head = jnp.bitwise_xor(me, r)
        mine = pl.ds(pl.multiple_of(head * dim, dim), dim)
        q32 = q_buf[:, pl.ds(pl.multiple_of(head * width, width), width)].astype(F32)
        queries = jnp.concatenate([q32[:, h * dim : (h + 1) * dim] for h in range(group)], axis=0)
        fresh_key = jnp.concatenate([fk_buf[:, mine].astype(F32)] * group, axis=0)
        fresh_value[r] = jnp.concatenate([fv_buf[:, mine].astype(F32)] * group, axis=0)
        own[r] = jnp.sum(queries * fresh_key, axis=1, keepdims=True) * scaling
        scores[r] = queries.astype(BF16)
    for r in order:
        keys_in[r].wait()
    for r in order:
        every = lax.dot_general(
            scores[r],
            k_buf[r].reshape(requests * longest, dim),
            (((1,), (1,)), ((), ())),
            preferred_element_type=F32,
        )
        picked = every[:, :longest]
        for i in range(1, requests):
            picked = jnp.where(request == i, every[:, i * longest : (i + 1) * longest], picked)
        scores[r] = jnp.where(valid, picked * scaling, -1e30)
    highest = {r: jnp.maximum(jnp.max(scores[r], axis=1, keepdims=True), own[r]) for r in order}
    exponent = {r: jnp.where(valid, jnp.exp(scores[r] - highest[r]), 0.0) for r in order}
    own_exp = {r: jnp.exp(own[r] - highest[r]) for r in order}
    inverse = {
        r: 1.0 / (jnp.sum(exponent[r], axis=1, keepdims=True) + own_exp[r]) for r in order
    }
    spread = {}
    for r in order:
        weights = exponent[r] * inverse[r]
        spread[r] = jnp.concatenate(
            [jnp.where(request == i, weights, 0.0) for i in range(requests)], axis=1
        ).astype(BF16)
    for r in order:
        values_in[r].wait()
    for r in order:
        own_weight = (own_exp[r] * inverse[r]).astype(BF16).astype(F32)
        result = (
            jnp.dot(
                spread[r], v_buf[r].reshape(requests * longest, dim), preferred_element_type=F32
            )
            + own_weight * fresh_value[r]
        )
        pieces = [result[h * requests : (h + 1) * requests] for h in range(group)]
        outs[kv - 1 - r][...] = jnp.concatenate(pieces + [ids], axis=1).astype(BF16)


def attend_blocks(length, adapter, query, fresh_key, fresh_value, keys, values):
    requests, kv, longest, dim = keys.shape
    width = query.shape[1] // kv
    hbm = pl.BlockSpec(memory_space=pltpu.HBM)
    return pl.pallas_call(
        functools.partial(attend_kernel, kv=kv),
        in_specs=[hbm] * 7,
        out_specs=[pl.BlockSpec(memory_space=pltpu.VMEM)] * kv,
        out_shape=[sds((requests, width + LANES))] * kv,
        scratch_shapes=[
            pltpu.SMEM(length.shape, jnp.int32),
            pltpu.SMEM(adapter.shape, jnp.int32),
            pltpu.VMEM(query.shape, BF16),
            pltpu.VMEM(fresh_key.shape, BF16),
            pltpu.VMEM(fresh_value.shape, BF16),
            pltpu.VMEM((kv, requests, longest, dim), BF16),
            pltpu.VMEM((kv, requests, longest, dim), BF16),
            pltpu.SemaphoreType.DMA((5,)),
            pltpu.SemaphoreType.DMA((2, kv)),
        ],
        compiler_params=params(),
        cost_estimate=cost(2**31, 2 * keys.size * 2),
        name="attend",
    )(*[pltpu.with_memory_space_constraint(x, pltpu.HBM) for x in (length, adapter, query, fresh_key, fresh_value, keys, values)])


def route_kernel(x0, x1, x2, x3, rows_ref, pick_ref, c0, c1, c2, c3, held, *, local, cap):
    me, mine = lax.axis_index("tensor"), lax.axis_index("batch")
    count = x0.shape[0]
    for r, x in zip((3, 2, 1, 0), (x0, x1, x2, x3)):
        held[pl.ds(pl.multiple_of(jnp.bitwise_xor(me, r) * count, count), count), :] = x[
            ...
        ].astype(F32)
    every = held[...]
    packed = every.astype(BF16)
    rows, wide = every.shape
    width = wide - LANES
    rows_ref[...] = packed[:, :width]
    adapter = every[:, width:].astype(jnp.int32)
    lane = lax.broadcasted_iota(jnp.int32, (rows, LANES), 1)
    part, slot = lax.div(lane, cap), lax.rem(lane, cap)
    first = jnp.bitwise_xor(mine, part) * local
    held_there = (adapter >= first) & (adapter < first + local) & (part < 4)
    held_f = held_there.astype(F32)
    lower = lax.broadcasted_iota(jnp.int32, (rows, rows), 0) >= lax.broadcasted_iota(
        jnp.int32, (rows, rows), 1
    )
    place_in = jnp.dot(
        lower.astype(F32).astype(BF16), held_f.astype(BF16), preferred_element_type=F32
    )
    pick = jnp.where(held_there & (place_in == (slot + 1).astype(F32)), 1.0, 0.0).astype(BF16)
    pick_ref[...] = pick
    chosen = lax.dot_general(
        pick, packed, (((0,), (0,)), ((), ())), preferred_element_type=F32
    ).astype(BF16)
    for r, c in enumerate((c0, c1, c2, c3)):
        c[...] = chosen[r * cap : (r + 1) * cap]


def route(blocks, local, cap):
    count, wide = blocks[0].shape
    rows = count * len(blocks)
    vmem = pl.BlockSpec(memory_space=pltpu.VMEM)
    return pl.pallas_call(
        functools.partial(route_kernel, local=local, cap=cap),
        in_specs=[vmem] * 4,
        out_specs=[vmem] * 6,
        out_shape=[sds((rows, wide - LANES)), sds((rows, LANES))] + [sds((cap, wide))] * 4,
        scratch_shapes=[pltpu.VMEM((rows, wide), F32)],
        compiler_params=params(),
        cost_estimate=cost(2**20, rows * wide * 8),
        name="route",
    )(*blocks)


def project_kernel(*refs, which, tile, add, after):
    rows_ref, w_hbm = refs[:2]
    addend = refs[2] if add else None
    skip = 2 + add + after
    outs = refs[skip : skip + len(which)]
    buf, sems = refs[skip + len(which) :]
    width = outs[0].shape[1]
    tiles = width // tile
    me = lax.axis_index("tensor")
    copies = []
    for k, r in enumerate(which):
        start = jnp.bitwise_xor(me, r) * width
        for j in range(tiles):
            at = pl.ds(pl.multiple_of(start + j * tile, tile), tile)
            n = k * tiles + j
            copies.append(pltpu.make_async_copy(w_hbm.at[:, at], buf.at[n], sems.at[n]))
    for copy in copies:
        copy.start()
    rows = rows_ref[...]
    for k, out in enumerate(outs):
        for j in range(tiles):
            n = k * tiles + j
            copies[n].wait()
            product = jnp.dot(rows, buf[n], preferred_element_type=F32)
            span = slice(j * tile, (j + 1) * tile)
            if add:
                product = product + addend[:, span].astype(F32)
            out[:, span] = product.astype(BF16)


def project(rows, weight, width, which, addend=None, after=None, tile=512):
    count, depth = rows.shape
    tiles = width // tile
    parts = len(which)
    vmem = pl.BlockSpec(memory_space=pltpu.VMEM)
    in_specs = [vmem, pl.BlockSpec(memory_space=pltpu.HBM)]
    operands = [rows, pltpu.with_memory_space_constraint(weight, pltpu.HBM)]
    if addend is not None:
        in_specs.append(vmem)
        operands.append(addend)
    if after is not None:
        in_specs.append(pl.BlockSpec(memory_space=pl.ANY))
        operands.append(after)
    return pl.pallas_call(
        functools.partial(
            project_kernel,
            which=which,
            tile=tile,
            add=addend is not None,
            after=after is not None,
        ),
        in_specs=in_specs,
        out_specs=[vmem] * parts,
        out_shape=[sds((count, width))] * parts,
        scratch_shapes=[
            pltpu.VMEM((parts * tiles, depth, tile), BF16),
            pltpu.SemaphoreType.DMA((parts * tiles,)),
        ],
        compiler_params=params(),
        cost_estimate=cost(2 * count * depth * width * parts, depth * width * 2 * parts),
        name="project",
    )(*operands)


def down_kernel(c0, c1, c2, c3, down_ref, low_ref, slot_ref):
    local, width, rank = down_ref.shape
    chosen = jnp.concatenate([c[...] for c in (c0, c1, c2, c3)], axis=0)
    values = chosen[:, :width]
    slot = chosen[:, width:].astype(F32).astype(jnp.int32) - lax.axis_index("batch") * local
    low = jnp.zeros((chosen.shape[0], rank), F32)
    for a in range(local):
        product = jnp.dot(values, down_ref[a], preferred_element_type=F32)
        low = jnp.where(slot == a, product, low)
    low_ref[...] = low.astype(BF16)
    slot_ref[...] = slot


def down(chosen, weight):
    local, width, rank = weight.shape
    rows = chosen[0].shape[0] * len(chosen)
    vmem = pl.BlockSpec(memory_space=pltpu.VMEM)
    return pl.pallas_call(
        down_kernel,
        in_specs=[vmem] * 5,
        out_specs=[vmem] * 2,
        out_shape=[sds((rows, rank)), sds((rows, rank), jnp.int32)],
        compiler_params=params(),
        cost_estimate=cost(2**34, weight.size * 2),
        name="down",
    )(*chosen, weight)


def up_kernel(ranks, l0, l1, l2, l3, slot_ref, up_ref, *outs, tile):
    local, _, width = up_ref.shape
    low = l0[...].astype(F32)
    for share in (l1, l2, l3):
        low = low + share[...].astype(F32)
    slot = slot_ref[...]
    lane = lax.broadcasted_iota(jnp.int32, low.shape, 1)
    kept = []
    for a in range(local):
        rank = ranks[lax.axis_index("batch") * local + a]
        factor = ADAPTER_SCALE / jnp.full(low.shape, rank, jnp.int32).astype(F32)
        kept.append(jnp.where((slot == a) & (lane < rank), low * factor, 0.0).astype(BF16))
    cap = outs[0].shape[0]
    for start in range(0, width, tile):
        span = slice(start, start + tile)
        total = jnp.dot(kept[0], up_ref[0, :, span], preferred_element_type=F32)
        for a in range(1, local):
            total = total + jnp.dot(kept[a], up_ref[a, :, span], preferred_element_type=F32)
        adapted = total.astype(BF16)
        for r, out in enumerate(outs):
            out[:, span] = adapted[r * cap : (r + 1) * cap]


def up(ranks, shares, slot, weight, parts, tile=512):
    local, rank, width = weight.shape
    rows = slot.shape[0]
    cap = rows // parts
    vmem = pl.BlockSpec(memory_space=pltpu.VMEM)
    return pl.pallas_call(
        functools.partial(up_kernel, tile=tile),
        in_specs=[pl.BlockSpec(memory_space=pltpu.SMEM)] + [vmem] * 6,
        out_specs=[vmem] * parts,
        out_shape=[sds((cap, width))] * parts,
        compiler_params=params(),
        cost_estimate=cost(2**34, weight.size * 2),
        name="up",
    )(ranks, *shares, slot, weight)


def finish_kernel(pick_ref, y0, y1, y2, a0, a1, a2, a3, out):
    rows = jnp.concatenate([a[...] for a in (a0, a1, a2, a3)], axis=0)
    pick = pick_ref[...][:, : rows.shape[0]]
    adapted = jnp.dot(pick, rows, preferred_element_type=F32)
    base = y0[...].astype(F32) + y1[...].astype(F32) + y2[...].astype(F32)
    out[...] = (base + adapted).astype(BF16)


def finish(pick, shares, adapted):
    vmem = pl.BlockSpec(memory_space=pltpu.VMEM)
    return pl.pallas_call(
        finish_kernel,
        in_specs=[vmem] * 8,
        out_specs=vmem,
        out_shape=sds(shares[0].shape),
        compiler_params=params(),
        cost_estimate=cost(2**24, shares[0].size * 16),
        name="finish",
    )(pick, *shares, *adapted)


def across(value, axis, r):
    n = lax.axis_size(axis)
    return lax.ppermute(value, axis, [(i, i ^ r) for i in range(n)])


def per_device_four(
    query,
    fresh_key,
    fresh_value,
    stored_keys,
    stored_values,
    cached_length,
    request_adapter,
    rank_per_adapter,
    output_weight,
    adapter_down_weight,
    adapter_up_weight,
):
    tensor_count = lax.axis_size("tensor")
    batch_count = lax.axis_size("batch")
    local = adapter_down_weight.shape[0]
    width = adapter_up_weight.shape[2]
    requests = query.shape[0]
    cap = 2 * requests * tensor_count // batch_count
    blocks = attend_blocks(
        cached_length,
        request_adapter,
        query,
        fresh_key,
        fresh_value,
        stored_keys,
        stored_values,
    )
    blocks = [across(blocks[3 - r], "tensor", r) for r in (3, 2, 1)] + [blocks[3]]
    rows, pick, *chosen = route(blocks, local, cap)

    gathered = [chosen[0]] + [across(chosen[r], "batch", r) for r in (1, 2, 3)]
    far, near = project(rows, output_weight, width, (3, 1))
    far_in = across(far, "tensor", 1)
    near_in = across(near, "tensor", 1)

    low, slot = down(gathered, adapter_down_weight)
    shares = [low] + [across(low, "tensor", r) for r in (1, 2, 3)]
    (cross,) = project(rows, output_weight, width, (2,), addend=far_in)
    (mine,) = project(rows, output_weight, width, (0,))
    cross_in = across(cross, "tensor", 2)

    lifted = up(rank_per_adapter, shares, slot, adapter_up_weight, batch_count)
    lifted = [lifted[0]] + [across(lifted[r], "batch", r) for r in (1, 2, 3)]
    return finish(pick, (mine, near_in, cross_in), lifted)


def attend(query, fresh_key, fresh_value, stored_keys, stored_values, cached_length):
    requests = query.shape[0]
    kv_heads, longest, head_dim = stored_keys.shape[1:]
    group_size = query.shape[1] // (kv_heads * head_dim)
    queries = query.reshape(requests, kv_heads, group_size, head_dim)
    scaling = 1.0 / math.sqrt(head_dim)
    scores = (
        jnp.einsum("rkgd,rkld->rkgl", queries, stored_keys, preferred_element_type=F32) * scaling
    )
    own_score = (
        jnp.einsum(
            "rkgd,rkd->rkg",
            queries,
            fresh_key.reshape(requests, kv_heads, head_dim),
            preferred_element_type=F32,
        )
        * scaling
    )
    valid = (jnp.arange(longest, dtype=jnp.int32)[None, :] < cached_length[:, None])[
        :, None, None, :
    ]
    scores = jnp.where(valid, scores, -1e30)
    highest = jnp.maximum(jnp.max(scores, axis=-1), own_score)
    exponent = jnp.where(valid, jnp.exp(scores - highest[..., None]), 0.0)
    own_exp = jnp.exp(own_score - highest)
    sum_exp = jnp.sum(exponent, axis=-1) + own_exp
    weights = (exponent / sum_exp[..., None]).astype(BF16)
    own_weight = (own_exp / sum_exp).astype(BF16)
    result = jnp.einsum("rkgl,rkld->rkgd", weights, stored_values, preferred_element_type=F32)
    own_value = fresh_value.reshape(requests, kv_heads, 1, head_dim).astype(F32)
    result = result + own_weight.astype(F32)[..., None] * own_value
    return result.reshape(requests, -1).astype(BF16)


def per_device_any(
    query,
    fresh_key,
    fresh_value,
    stored_keys,
    stored_values,
    cached_length,
    request_adapter,
    rank_per_adapter,
    output_weight,
    adapter_down_weight,
    adapter_up_weight,
):
    attended = attend(query, fresh_key, fresh_value, stored_keys, stored_values, cached_length)
    batch_count = lax.axis_size("batch")
    local, _, rank_span = adapter_down_weight.shape
    head_rows = lax.all_to_all(attended, "tensor", split_axis=1, concat_axis=0, tiled=True)
    row_count = head_rows.shape[0]
    products = jnp.dot(head_rows, output_weight, preferred_element_type=F32)
    base = lax.psum_scatter(
        products.astype(BF16), "tensor", scatter_dimension=1, tiled=True
    ).astype(F32)
    all_rows = lax.all_gather(head_rows, "batch", axis=0, tiled=True)
    ids = lax.all_gather(request_adapter, ("batch", "tensor"), axis=0, tiled=True)
    slot = ids - lax.axis_index("batch") * local
    one_hot = slot[:, None] == jnp.arange(local, dtype=jnp.int32)[None, :]
    low_every = jnp.einsum("rk,skj->rsj", all_rows, adapter_down_weight, preferred_element_type=F32)
    low = jnp.sum(jnp.where(one_hot[:, :, None], low_every, 0.0), axis=1)
    low = lax.psum(low.astype(BF16), "tensor").astype(F32)
    adapter_count = rank_per_adapter.shape[0]
    picked = ids[:, None] == jnp.arange(adapter_count, dtype=jnp.int32)[None, :]
    row_rank = jnp.sum(jnp.where(picked, rank_per_adapter[None, :], 0), axis=1)[:, None]
    kept = jnp.arange(rank_span, dtype=jnp.int32)[None, :] < row_rank
    delta = jnp.where(kept, low * (ADAPTER_SCALE / row_rank.astype(F32)), 0.0).astype(BF16)
    widened = jnp.where(one_hot[:, :, None], delta[:, None, :], jnp.zeros((), BF16))
    adapted = jnp.dot(
        widened.reshape(ids.shape[0], local * rank_span),
        adapter_up_weight.reshape(local * rank_span, -1),
        preferred_element_type=F32,
    ).astype(BF16)
    adapted = lax.all_to_all(
        adapted.reshape(batch_count, row_count, -1), "batch", split_axis=0, concat_axis=0, tiled=True
    )
    adapted = jnp.sum(adapted.astype(F32), axis=0)
    return (base + adapted).astype(BF16)


def solution(mesh):
    in_specs = (
        P(("group", "batch", "tensor"), None),
        P(("group", "batch", "tensor"), None),
        P(("group", "batch", "tensor"), None),
        P(("group", "batch", "tensor"), None, None, None),
        P(("group", "batch", "tensor"), None, None, None),
        P(("group", "batch", "tensor")),
        P(("group", "batch", "tensor")),
        P(),
        P("tensor", None),
        P("batch", "tensor", None),
        P("batch", None, "tensor"),
    )
    out_specs = P(("group", "batch"), "tensor")

    def whole(*arrays):
        tensor_count, batch_count = mesh.shape["tensor"], mesh.shape["batch"]
        four = tensor_count == batch_count == arrays[3].shape[1] == 4
        body = per_device_four if four else per_device_any
        return jax.shard_map(
            body, mesh=mesh, in_specs=in_specs, out_specs=out_specs, check_vma=False
        )(*arrays)

    return whole
```

```python
import functools
import math

import jax
import jax.numpy as jnp
from jax import lax
from jax.experimental import pallas as pl
from jax.experimental.pallas import tpu as pltpu
from jax.sharding import PartitionSpec as P

ADAPTER_SCALE = 16.0
F32 = jnp.float32
BF16 = jnp.bfloat16
LANES = 128
MIB = 1024 * 1024


def params(grid_rank=0, vmem=24 * MIB):
    if grid_rank:
        return pltpu.CompilerParams(
            dimension_semantics=("arbitrary",) * grid_rank, vmem_limit_bytes=vmem
        )
    return pltpu.CompilerParams(vmem_limit_bytes=vmem)


def cost(flops, nbytes):
    return pl.CostEstimate(flops=flops, bytes_accessed=nbytes, transcendentals=0)


def sds(shape, dtype=BF16):
    return jax.ShapeDtypeStruct(shape, dtype)


def column_of(ref, count):
    rows = lax.broadcasted_iota(jnp.int32, (count, LANES), 0)
    out = jnp.full((count, LANES), ref[0], jnp.int32)
    for i in range(1, count):
        out = jnp.where(rows == i, ref[i], out)
    return out


def attend_kernel(*refs, kv):
    length_hbm, adapter_hbm, q_hbm, fk_hbm, fv_hbm, k_hbm, v_hbm, w_hbm = refs[:8]
    outs = refs[8 : 8 + kv]
    far, cross = refs[8 + kv : 10 + kv]
    length, adapter, q_buf, fk_buf, fv_buf, k_buf, v_buf, small, big, ahead = refs[10 + kv :]
    requests, _, longest, dim = k_hbm.shape
    width = q_hbm.shape[1] // kv
    group = width // dim
    rows = group * requests
    scaling = 1.0 / math.sqrt(dim)
    me = lax.axis_index("tensor")
    order = tuple(range(kv - 1, -1, -1))

    ready = [
        pltpu.make_async_copy(source, target, small.at[i])
        for i, (source, target) in enumerate(
            (
                (q_hbm, q_buf),
                (fk_hbm, fk_buf),
                (fv_hbm, fv_buf),
                (length_hbm, length),
                (adapter_hbm, adapter),
            )
        )
    ]
    keys_in = {}
    values_in = {}
    for r in order:
        head = jnp.bitwise_xor(me, r)
        keys_in[r] = pltpu.make_async_copy(k_hbm.at[:, head], k_buf.at[r], big.at[0, r])
        values_in[r] = pltpu.make_async_copy(v_hbm.at[:, head], v_buf.at[r], big.at[1, r])
    for copy in ready:
        copy.start()
    for r in order:
        keys_in[r].start()
    for r in order:
        values_in[r].start()
    half = lax.rem(lax.axis_index("batch"), 2)
    part = w_hbm.shape[1] // (2 * kv)
    ahead_in = []
    for i, (r, target) in enumerate(((3, far), (2, cross))):
        at = pl.multiple_of((jnp.bitwise_xor(me, r) * 2 + half) * part, part)
        source = w_hbm.at[:, pl.ds(at, target.shape[1])]
        ahead_in.append(pltpu.make_async_copy(source, target, ahead.at[i]))
    for copy in ahead_in:
        copy.start()
    for copy in ready:
        copy.wait()

    request = lax.rem(lax.broadcasted_iota(jnp.int32, (rows, longest), 0), requests)
    lengths = jnp.concatenate([column_of(length, requests)] * group, axis=0)
    valid = lax.broadcasted_iota(jnp.int32, (rows, longest), 1) < lengths
    ids = column_of(adapter, requests).astype(F32)
    scores, own, fresh_value = {}, {}, {}
    for r in order:
        head = jnp.bitwise_xor(me, r)
        mine = pl.ds(pl.multiple_of(head * dim, dim), dim)
        q32 = q_buf[:, pl.ds(pl.multiple_of(head * width, width), width)].astype(F32)
        queries = jnp.concatenate([q32[:, h * dim : (h + 1) * dim] for h in range(group)], axis=0)
        fresh_key = jnp.concatenate([fk_buf[:, mine].astype(F32)] * group, axis=0)
        fresh_value[r] = jnp.concatenate([fv_buf[:, mine].astype(F32)] * group, axis=0)
        own[r] = jnp.sum(queries * fresh_key, axis=1, keepdims=True) * scaling
        scores[r] = queries.astype(BF16)
    for r in order:
        keys_in[r].wait()
    for r in order:
        every = lax.dot_general(
            scores[r],
            k_buf[r].reshape(requests * longest, dim),
            (((1,), (1,)), ((), ())),
            preferred_element_type=F32,
        )
        picked = every[:, :longest]
        for i in range(1, requests):
            picked = jnp.where(request == i, every[:, i * longest : (i + 1) * longest], picked)
        scores[r] = jnp.where(valid, picked * scaling, -1e30)
    highest = {r: jnp.maximum(jnp.max(scores[r], axis=1, keepdims=True), own[r]) for r in order}
    exponent = {r: jnp.where(valid, jnp.exp(scores[r] - highest[r]), 0.0) for r in order}
    own_exp = {r: jnp.exp(own[r] - highest[r]) for r in order}
    inverse = {
        r: 1.0 / (jnp.sum(exponent[r], axis=1, keepdims=True) + own_exp[r]) for r in order
    }
    spread = {}
    for r in order:
        weights = exponent[r] * inverse[r]
        spread[r] = jnp.concatenate(
            [jnp.where(request == i, weights, 0.0) for i in range(requests)], axis=1
        ).astype(BF16)
    for r in order:
        values_in[r].wait()
    for r in order:
        own_weight = (own_exp[r] * inverse[r]).astype(BF16).astype(F32)
        result = (
            jnp.dot(
                spread[r], v_buf[r].reshape(requests * longest, dim), preferred_element_type=F32
            )
            + own_weight * fresh_value[r]
        )
        pieces = [result[h * requests : (h + 1) * requests] for h in range(group)]
        outs[kv - 1 - r][...] = jnp.concatenate(pieces + [ids], axis=1).astype(BF16)
    for copy in ahead_in:
        copy.wait()


def attend_blocks(length, adapter, query, fresh_key, fresh_value, keys, values, weight):
    requests, kv, longest, dim = keys.shape
    width = query.shape[1] // kv
    hbm = pl.BlockSpec(memory_space=pltpu.HBM)
    return pl.pallas_call(
        functools.partial(attend_kernel, kv=kv),
        in_specs=[hbm] * 8,
        out_specs=[pl.BlockSpec(memory_space=pltpu.VMEM)] * (kv + 2),
        out_shape=[sds((requests, width + LANES))] * kv
        + [sds((weight.shape[0], weight.shape[1] // n)) for n in (4 * kv, 2 * kv)],
        scratch_shapes=[
            pltpu.SMEM(length.shape, jnp.int32),
            pltpu.SMEM(adapter.shape, jnp.int32),
            pltpu.VMEM(query.shape, BF16),
            pltpu.VMEM(fresh_key.shape, BF16),
            pltpu.VMEM(fresh_value.shape, BF16),
            pltpu.VMEM((kv, requests, longest, dim), BF16),
            pltpu.VMEM((kv, requests, longest, dim), BF16),
            pltpu.SemaphoreType.DMA((5,)),
            pltpu.SemaphoreType.DMA((2, kv)),
            pltpu.SemaphoreType.DMA((2,)),
        ],
        compiler_params=params(),
        cost_estimate=cost(2**31, 2 * keys.size * 2),
        name="attend",
    )(*[pltpu.with_memory_space_constraint(x, pltpu.HBM) for x in (length, adapter, query, fresh_key, fresh_value, keys, values, weight)])


def route_kernel(x0, x1, x2, x3, near_ref, pick_ref, c0, c2, c3, held, *, local, cap):
    me, mine = lax.axis_index("tensor"), lax.axis_index("batch")
    count = x0.shape[0]
    for r, x in zip((3, 2, 1, 0), (x0, x1, x2, x3)):
        held[pl.ds(pl.multiple_of(jnp.bitwise_xor(me, r) * count, count), count), :] = x[
            ...
        ].astype(F32)
    every = held[...]
    packed = every.astype(BF16)
    rows, wide = every.shape
    width = wide - LANES
    near_ref[:rows] = packed
    adapter = every[:, width:].astype(jnp.int32)
    lane = lax.broadcasted_iota(jnp.int32, (rows, LANES), 1)
    part, slot = lax.div(lane, cap), lax.rem(lane, cap)
    first = jnp.bitwise_xor(mine, part) * local
    held_there = (adapter >= first) & (adapter < first + local) & (part < 4)
    held_f = held_there.astype(F32)
    lower = lax.broadcasted_iota(jnp.int32, (rows, rows), 0) >= lax.broadcasted_iota(
        jnp.int32, (rows, rows), 1
    )
    place_in = jnp.dot(
        lower.astype(F32).astype(BF16), held_f.astype(BF16), preferred_element_type=F32
    )
    pick = jnp.where(held_there & (place_in == (slot + 1).astype(F32)), 1.0, 0.0).astype(BF16)
    pick_ref[...] = pick
    chosen = lax.dot_general(
        pick, packed, (((0,), (0,)), ((), ())), preferred_element_type=F32
    ).astype(BF16)
    for r, c in ((0, c0), (2, c2), (3, c3)):
        c[...] = chosen[r * cap : (r + 1) * cap]
    near_ref[rows:] = chosen[cap : 2 * cap]


def route(blocks, local, cap):
    count, wide = blocks[0].shape
    rows = count * len(blocks)
    vmem = pl.BlockSpec(memory_space=pltpu.VMEM)
    return pl.pallas_call(
        functools.partial(route_kernel, local=local, cap=cap),
        in_specs=[vmem] * 4,
        out_specs=[vmem] * 5,
        out_shape=[sds((rows + cap, wide)), sds((rows, LANES))] + [sds((cap, wide))] * 3,
        scratch_shapes=[pltpu.VMEM((rows, wide), F32)],
        compiler_params=params(),
        cost_estimate=cost(2**20, rows * wide * 8),
        name="route",
    )(*blocks)


def project_kernel(*refs, which, tile, leads, add, count):
    mine_ref, other_ref, w_hbm = refs[:3]
    refs = refs[3:]
    addend, refs = (refs[0], refs[1:]) if add else (None, refs)
    ready, refs = refs[0], refs[1:]
    outs, (buf, sems) = refs[: len(which)], refs[len(which) :]
    depth, width = w_hbm.shape[0], outs[0].shape[1]
    me, half = lax.axis_index("tensor"), lax.rem(lax.axis_index("batch"), 2)
    copies = {}
    for k, r in enumerate(which):
        start = (jnp.bitwise_xor(me, r) * 2 + half) * width
        for low in range(leads[k], width, tile):
            n = len(copies)
            at = pl.ds(pl.multiple_of(start + low, tile), tile)
            copies[k, low] = n, pltpu.make_async_copy(w_hbm.at[:, at], buf.at[n], sems.at[n])
    for _, copy in copies.values():
        copy.start()
    rows = jnp.concatenate([mine_ref[:count, :depth], other_ref[:count, :depth]], axis=0)
    for k in range(len(which)):
        for low in range(0, width, tile):
            span = slice(low, low + tile)
            if low < leads[k]:
                block = ready[:, span]
            else:
                n, copy = copies[k, low]
                copy.wait()
                block = buf[n]
            product = jnp.dot(rows, block, preferred_element_type=F32)
            if add:
                product = product + addend[:, span].astype(F32)
            outs[k][:, span] = product.astype(BF16)


def project(mine, other, count, weight, width, which, ready, addend=None, tile=512):
    depth = weight.shape[0]
    parts = len(which)
    leads = (ready.shape[1],) + (0,) * (parts - 1)
    pieces = max(1, (parts * width - sum(leads)) // tile)
    vmem = pl.BlockSpec(memory_space=pltpu.VMEM)
    in_specs = [vmem, vmem, pl.BlockSpec(memory_space=pltpu.HBM)]
    operands = [mine, other, pltpu.with_memory_space_constraint(weight, pltpu.HBM)]
    if addend is not None:
        in_specs.append(vmem)
        operands.append(addend)
    return pl.pallas_call(
        functools.partial(
            project_kernel,
            which=which,
            tile=tile,
            leads=leads,
            add=addend is not None,
            count=count,
        ),
        in_specs=in_specs + [vmem],
        out_specs=[vmem] * parts,
        out_shape=[sds((2 * count, width))] * parts,
        scratch_shapes=[
            pltpu.VMEM((pieces, depth, tile), BF16),
            pltpu.SemaphoreType.DMA((pieces,)),
        ],
        compiler_params=params(),
        cost_estimate=cost(4 * count * depth * width * parts, depth * width * 2 * parts),
        name="project",
    )(*operands, ready)


def down_kernel(c0, c1, c2, c3, down_ref, low_ref, slot_ref):
    local, width, rank = down_ref.shape
    cap = c0.shape[0]
    chosen = jnp.concatenate([c0[...], c1[c1.shape[0] - cap :], c2[...], c3[...]], axis=0)
    values = chosen[:, :width]
    slot = chosen[:, width:].astype(F32).astype(jnp.int32) - lax.axis_index("batch") * local
    low = jnp.zeros((chosen.shape[0], rank), F32)
    for a in range(local):
        product = jnp.dot(values, down_ref[a], preferred_element_type=F32)
        low = jnp.where(slot == a, product, low)
    low_ref[...] = low.astype(BF16)
    slot_ref[...] = slot


def down(chosen, weight):
    local, width, rank = weight.shape
    rows = chosen[0].shape[0] * len(chosen)
    vmem = pl.BlockSpec(memory_space=pltpu.VMEM)
    return pl.pallas_call(
        down_kernel,
        in_specs=[vmem] * 5,
        out_specs=[vmem] * 2,
        out_shape=[sds((rows, rank)), sds((rows, rank), jnp.int32)],
        compiler_params=params(),
        cost_estimate=cost(2**34, weight.size * 2),
        name="down",
    )(*chosen, weight)


def up_kernel(ranks, l0, l1, l2, l3, slot_ref, up_ref, *outs, tile):
    local, _, width = up_ref.shape
    low = l0[...].astype(F32)
    for share in (l1, l2, l3):
        low = low + share[...].astype(F32)
    slot = slot_ref[...]
    lane = lax.broadcasted_iota(jnp.int32, low.shape, 1)
    kept = []
    for a in range(local):
        rank = ranks[lax.axis_index("batch") * local + a]
        factor = ADAPTER_SCALE / jnp.full(low.shape, rank, jnp.int32).astype(F32)
        kept.append(jnp.where((slot == a) & (lane < rank), low * factor, 0.0).astype(BF16))
    cap = outs[0].shape[0]
    for start in range(0, width, tile):
        span = slice(start, start + tile)
        total = jnp.dot(kept[0], up_ref[0, :, span], preferred_element_type=F32)
        for a in range(1, local):
            total = total + jnp.dot(kept[a], up_ref[a, :, span], preferred_element_type=F32)
        adapted = total.astype(BF16)
        for r, out in enumerate(outs):
            out[:, span] = adapted[r * cap : (r + 1) * cap]


def up(ranks, shares, slot, weight, parts, tile=512):
    local, rank, width = weight.shape
    rows = slot.shape[0]
    cap = rows // parts
    vmem = pl.BlockSpec(memory_space=pltpu.VMEM)
    return pl.pallas_call(
        functools.partial(up_kernel, tile=tile),
        in_specs=[pl.BlockSpec(memory_space=pltpu.SMEM)] + [vmem] * 6,
        out_specs=[vmem] * parts,
        out_shape=[sds((cap, width))] * parts,
        compiler_params=params(),
        cost_estimate=cost(2**34, weight.size * 2),
        name="up",
    )(ranks, *shares, slot, weight)


def gather_kernel(y0, y1, y2, _, mine, theirs):
    count = mine.shape[0]
    total = y0[...].astype(F32) + y1[...].astype(F32) + y2[...].astype(F32)
    mine[...] = total[:count]
    theirs[...] = total[count:].astype(BF16)


def gather_base(shares, after):
    vmem = pl.BlockSpec(memory_space=pltpu.VMEM)
    count, width = shares[0].shape
    return pl.pallas_call(
        gather_kernel,
        in_specs=[vmem] * 3 + [pl.BlockSpec(memory_space=pl.ANY)],
        out_specs=[vmem] * 2,
        out_shape=[sds((count // 2, width), F32), sds((count // 2, width))],
        compiler_params=params(),
        cost_estimate=cost(2**20, shares[0].size * 12),
        name="gather_base",
    )(*shares, after)


def finish_kernel(pick_ref, m0, m1, a0, a1, a2, a3, out):
    width = m0.shape[1]
    half = lax.rem(lax.axis_index("batch"), 2)
    pick = pick_ref[...][:, : 4 * a0.shape[0]]
    for k, base in enumerate((m0, m1)):
        at = jnp.bitwise_xor(half, k) * width
        span = pl.ds(pl.multiple_of(at, width), width)
        rows = jnp.concatenate([a[:, span] for a in (a0, a1, a2, a3)], axis=0)
        adapted = jnp.dot(pick, rows, preferred_element_type=F32)
        out[:, span] = (base[...].astype(F32) + adapted).astype(BF16)


def finish(pick, shares, adapted):
    vmem = pl.BlockSpec(memory_space=pltpu.VMEM)
    count, width = shares[0].shape
    return pl.pallas_call(
        finish_kernel,
        in_specs=[vmem] * 7,
        out_specs=vmem,
        out_shape=sds((count, 2 * width)),
        compiler_params=params(),
        cost_estimate=cost(2**24, shares[0].size * 16),
        name="finish",
    )(pick, *shares, *adapted)


def across(value, axis, r):
    n = lax.axis_size(axis)
    return lax.ppermute(value, axis, [(i, i ^ r) for i in range(n)])


def per_device_four(
    query,
    fresh_key,
    fresh_value,
    stored_keys,
    stored_values,
    cached_length,
    request_adapter,
    rank_per_adapter,
    output_weight,
    adapter_down_weight,
    adapter_up_weight,
):
    tensor_count = lax.axis_size("tensor")
    batch_count = lax.axis_size("batch")
    local = adapter_down_weight.shape[0]
    width = adapter_up_weight.shape[2]
    requests = query.shape[0]
    cap = 2 * requests * tensor_count // batch_count
    *blocks, w_far, w_cross = attend_blocks(
        cached_length,
        request_adapter,
        query,
        fresh_key,
        fresh_value,
        stored_keys,
        stored_values,
        output_weight,
    )
    blocks = [across(blocks[3 - r], "tensor", r) for r in (3, 2, 1)] + [blocks[3]]
    near_rows, pick, *chosen = route(blocks, local, cap)
    count = requests * tensor_count
    other = across(near_rows, "batch", 1)
    gathered = [chosen[0], other] + [across(c, "batch", r) for c, r in zip(chosen[1:], (2, 3))]
    both = (near_rows, other, count, output_weight, width // 2)
    far, near, mine = project(*both, (3, 1, 0), w_far)
    far_in = across(far, "tensor", 1)
    near_in = across(near, "tensor", 1)

    low, slot = down(gathered, adapter_down_weight)
    shares = [low] + [across(low, "tensor", r) for r in (1, 2, 3)]
    (cross,) = project(*both, (2,), w_cross, addend=far_in)
    cross_in = across(cross, "tensor", 2)
    lifted = up(rank_per_adapter, shares, slot, adapter_up_weight, batch_count)
    lifted = [lifted[0]] + [across(lifted[r], "batch", r) for r in (1, 2, 3)]
    mine, theirs = gather_base((mine, near_in, cross_in), lifted[0])
    return finish(pick, (mine, across(theirs, "batch", 1)), lifted)


def attend(query, fresh_key, fresh_value, stored_keys, stored_values, cached_length):
    requests = query.shape[0]
    kv_heads, longest, head_dim = stored_keys.shape[1:]
    group_size = query.shape[1] // (kv_heads * head_dim)
    queries = query.reshape(requests, kv_heads, group_size, head_dim)
    scaling = 1.0 / math.sqrt(head_dim)
    scores = (
        jnp.einsum("rkgd,rkld->rkgl", queries, stored_keys, preferred_element_type=F32) * scaling
    )
    own_score = (
        jnp.einsum(
            "rkgd,rkd->rkg",
            queries,
            fresh_key.reshape(requests, kv_heads, head_dim),
            preferred_element_type=F32,
        )
        * scaling
    )
    valid = (jnp.arange(longest, dtype=jnp.int32)[None, :] < cached_length[:, None])[
        :, None, None, :
    ]
    scores = jnp.where(valid, scores, -1e30)
    highest = jnp.maximum(jnp.max(scores, axis=-1), own_score)
    exponent = jnp.where(valid, jnp.exp(scores - highest[..., None]), 0.0)
    own_exp = jnp.exp(own_score - highest)
    sum_exp = jnp.sum(exponent, axis=-1) + own_exp
    weights = (exponent / sum_exp[..., None]).astype(BF16)
    own_weight = (own_exp / sum_exp).astype(BF16)
    result = jnp.einsum("rkgl,rkld->rkgd", weights, stored_values, preferred_element_type=F32)
    own_value = fresh_value.reshape(requests, kv_heads, 1, head_dim).astype(F32)
    result = result + own_weight.astype(F32)[..., None] * own_value
    return result.reshape(requests, -1).astype(BF16)


def per_device_any(
    query,
    fresh_key,
    fresh_value,
    stored_keys,
    stored_values,
    cached_length,
    request_adapter,
    rank_per_adapter,
    output_weight,
    adapter_down_weight,
    adapter_up_weight,
):
    attended = attend(query, fresh_key, fresh_value, stored_keys, stored_values, cached_length)
    batch_count = lax.axis_size("batch")
    local, _, rank_span = adapter_down_weight.shape
    head_rows = lax.all_to_all(attended, "tensor", split_axis=1, concat_axis=0, tiled=True)
    row_count = head_rows.shape[0]
    products = jnp.dot(head_rows, output_weight, preferred_element_type=F32)
    base = lax.psum_scatter(
        products.astype(BF16), "tensor", scatter_dimension=1, tiled=True
    ).astype(F32)
    all_rows = lax.all_gather(head_rows, "batch", axis=0, tiled=True)
    ids = lax.all_gather(request_adapter, ("batch", "tensor"), axis=0, tiled=True)
    slot = ids - lax.axis_index("batch") * local
    one_hot = slot[:, None] == jnp.arange(local, dtype=jnp.int32)[None, :]
    low_every = jnp.einsum("rk,skj->rsj", all_rows, adapter_down_weight, preferred_element_type=F32)
    low = jnp.sum(jnp.where(one_hot[:, :, None], low_every, 0.0), axis=1)
    low = lax.psum(low.astype(BF16), "tensor").astype(F32)
    adapter_count = rank_per_adapter.shape[0]
    picked = ids[:, None] == jnp.arange(adapter_count, dtype=jnp.int32)[None, :]
    row_rank = jnp.sum(jnp.where(picked, rank_per_adapter[None, :], 0), axis=1)[:, None]
    kept = jnp.arange(rank_span, dtype=jnp.int32)[None, :] < row_rank
    delta = jnp.where(kept, low * (ADAPTER_SCALE / row_rank.astype(F32)), 0.0).astype(BF16)
    widened = jnp.where(one_hot[:, :, None], delta[:, None, :], jnp.zeros((), BF16))
    adapted = jnp.dot(
        widened.reshape(ids.shape[0], local * rank_span),
        adapter_up_weight.reshape(local * rank_span, -1),
        preferred_element_type=F32,
    ).astype(BF16)
    adapted = lax.all_to_all(
        adapted.reshape(batch_count, row_count, -1), "batch", split_axis=0, concat_axis=0, tiled=True
    )
    adapted = jnp.sum(adapted.astype(F32), axis=0)
    return (base + adapted).astype(BF16)


def solution(mesh):
    in_specs = (
        P(("group", "batch", "tensor"), None),
        P(("group", "batch", "tensor"), None),
        P(("group", "batch", "tensor"), None),
        P(("group", "batch", "tensor"), None, None, None),
        P(("group", "batch", "tensor"), None, None, None),
        P(("group", "batch", "tensor")),
        P(("group", "batch", "tensor")),
        P(),
        P("tensor", None),
        P("batch", "tensor", None),
        P("batch", None, "tensor"),
    )
    out_specs = P(("group", "batch"), "tensor")

    def whole(*arrays):
        tensor_count, batch_count = mesh.shape["tensor"], mesh.shape["batch"]
        four = tensor_count == batch_count == arrays[3].shape[1] == 4
        body = per_device_four if four else per_device_any
        return jax.shard_map(
            body, mesh=mesh, in_specs=in_specs, out_specs=out_specs, check_vma=False
        )(*arrays)

    return whole
```

```python
import functools
import math

import jax
import jax.numpy as jnp
from jax import lax
from jax.experimental import pallas as pl
from jax.experimental.pallas import tpu as pltpu
from jax.sharding import PartitionSpec as P

ADAPTER_SCALE = 16.0
F32 = jnp.float32
BF16 = jnp.bfloat16
LANES = 128
MIB = 1024 * 1024


def params(grid_rank=0, vmem=24 * MIB):
    if grid_rank:
        return pltpu.CompilerParams(
            dimension_semantics=("arbitrary",) * grid_rank, vmem_limit_bytes=vmem
        )
    return pltpu.CompilerParams(vmem_limit_bytes=vmem)


def cost(flops, nbytes):
    return pl.CostEstimate(flops=flops, bytes_accessed=nbytes, transcendentals=0)


def sds(shape, dtype=BF16):
    return jax.ShapeDtypeStruct(shape, dtype)


def column_of(ref, count):
    rows = lax.broadcasted_iota(jnp.int32, (count, LANES), 0)
    out = jnp.full((count, LANES), ref[0], jnp.int32)
    for i in range(1, count):
        out = jnp.where(rows == i, ref[i], out)
    return out


def attend_kernel(*refs, kv):
    length_hbm, adapter_hbm, q_hbm, fk_hbm, fv_hbm, k_hbm, v_hbm = refs[:7]
    outs = refs[7 : 7 + kv]
    length, adapter, q_buf, fk_buf, fv_buf, k_buf, v_buf, small, big = refs[7 + kv :]
    requests, _, longest, dim = k_hbm.shape
    width = q_hbm.shape[1] // kv
    group = width // dim
    rows = group * requests
    scaling = 1.0 / math.sqrt(dim)
    me = lax.axis_index("tensor")
    order = tuple(range(kv - 1, -1, -1))

    ready = [
        pltpu.make_async_copy(source, target, small.at[i])
        for i, (source, target) in enumerate(
            (
                (q_hbm, q_buf),
                (fk_hbm, fk_buf),
                (fv_hbm, fv_buf),
                (length_hbm, length),
                (adapter_hbm, adapter),
            )
        )
    ]
    keys_in = {}
    values_in = {}
    for r in order:
        head = jnp.bitwise_xor(me, r)
        keys_in[r] = pltpu.make_async_copy(k_hbm.at[:, head], k_buf.at[r], big.at[0, r])
        values_in[r] = pltpu.make_async_copy(v_hbm.at[:, head], v_buf.at[r], big.at[1, r])
    for copy in ready:
        copy.start()
    for r in order:
        keys_in[r].start()
    for r in order:
        values_in[r].start()
    for copy in ready:
        copy.wait()

    request = lax.rem(lax.broadcasted_iota(jnp.int32, (rows, longest), 0), requests)
    lengths = jnp.concatenate([column_of(length, requests)] * group, axis=0)
    valid = lax.broadcasted_iota(jnp.int32, (rows, longest), 1) < lengths
    ids = column_of(adapter, requests).astype(F32)
    scores, own, fresh_value = {}, {}, {}
    for r in order:
        head = jnp.bitwise_xor(me, r)
        mine = pl.ds(pl.multiple_of(head * dim, dim), dim)
        q32 = q_buf[:, pl.ds(pl.multiple_of(head * width, width), width)].astype(F32)
        queries = jnp.concatenate([q32[:, h * dim : (h + 1) * dim] for h in range(group)], axis=0)
        fresh_key = jnp.concatenate([fk_buf[:, mine].astype(F32)] * group, axis=0)
        fresh_value[r] = jnp.concatenate([fv_buf[:, mine].astype(F32)] * group, axis=0)
        own[r] = jnp.sum(queries * fresh_key, axis=1, keepdims=True) * scaling
        scores[r] = queries.astype(BF16)
    for r in order:
        keys_in[r].wait()
    for r in order:
        every = lax.dot_general(
            scores[r],
            k_buf[r].reshape(requests * longest, dim),
            (((1,), (1,)), ((), ())),
            preferred_element_type=F32,
        )
        picked = every[:, :longest]
        for i in range(1, requests):
            picked = jnp.where(request == i, every[:, i * longest : (i + 1) * longest], picked)
        scores[r] = jnp.where(valid, picked * scaling, -1e30)
    highest = {r: jnp.maximum(jnp.max(scores[r], axis=1, keepdims=True), own[r]) for r in order}
    exponent = {r: jnp.where(valid, jnp.exp(scores[r] - highest[r]), 0.0) for r in order}
    own_exp = {r: jnp.exp(own[r] - highest[r]) for r in order}
    inverse = {
        r: 1.0 / (jnp.sum(exponent[r], axis=1, keepdims=True) + own_exp[r]) for r in order
    }
    spread = {}
    for r in order:
        weights = exponent[r] * inverse[r]
        spread[r] = jnp.concatenate(
            [jnp.where(request == i, weights, 0.0) for i in range(requests)], axis=1
        ).astype(BF16)
    for r in order:
        values_in[r].wait()
    for r in order:
        own_weight = (own_exp[r] * inverse[r]).astype(BF16).astype(F32)
        result = (
            jnp.dot(
                spread[r], v_buf[r].reshape(requests * longest, dim), preferred_element_type=F32
            )
            + own_weight * fresh_value[r]
        )
        pieces = [result[h * requests : (h + 1) * requests] for h in range(group)]
        outs[kv - 1 - r][...] = jnp.concatenate(pieces + [ids], axis=1).astype(BF16)


def attend_blocks(length, adapter, query, fresh_key, fresh_value, keys, values):
    requests, kv, longest, dim = keys.shape
    width = query.shape[1] // kv
    hbm = pl.BlockSpec(memory_space=pltpu.HBM)
    return pl.pallas_call(
        functools.partial(attend_kernel, kv=kv),
        in_specs=[hbm] * 7,
        out_specs=[pl.BlockSpec(memory_space=pltpu.VMEM)] * kv,
        out_shape=[sds((requests, width + LANES))] * kv,
        scratch_shapes=[
            pltpu.SMEM(length.shape, jnp.int32),
            pltpu.SMEM(adapter.shape, jnp.int32),
            pltpu.VMEM(query.shape, BF16),
            pltpu.VMEM(fresh_key.shape, BF16),
            pltpu.VMEM(fresh_value.shape, BF16),
            pltpu.VMEM((kv, requests, longest, dim), BF16),
            pltpu.VMEM((kv, requests, longest, dim), BF16),
            pltpu.SemaphoreType.DMA((5,)),
            pltpu.SemaphoreType.DMA((2, kv)),
        ],
        compiler_params=params(),
        cost_estimate=cost(2**35, 2 * keys.size * 2),
        name="attend",
    )(*[pltpu.with_memory_space_constraint(x, pltpu.HBM) for x in (length, adapter, query, fresh_key, fresh_value, keys, values)])


def route_kernel(x0, x1, x2, x3, near_ref, pick_ref, c0, c2, c3, held, *, local, cap):
    me, mine = lax.axis_index("tensor"), lax.axis_index("batch")
    count = x0.shape[0]
    for r, x in zip((3, 2, 1, 0), (x0, x1, x2, x3)):
        held[pl.ds(pl.multiple_of(jnp.bitwise_xor(me, r) * count, count), count), :] = x[
            ...
        ].astype(F32)
    every = held[...]
    packed = every.astype(BF16)
    rows, wide = every.shape
    width = wide - LANES
    near_ref[:rows] = packed
    adapter = every[:, width:].astype(jnp.int32)
    lane = lax.broadcasted_iota(jnp.int32, (rows, LANES), 1)
    part, slot = lax.div(lane, cap), lax.rem(lane, cap)
    first = jnp.bitwise_xor(mine, part) * local
    held_there = (adapter >= first) & (adapter < first + local) & (part < 4)
    held_f = held_there.astype(F32)
    lower = lax.broadcasted_iota(jnp.int32, (rows, rows), 0) >= lax.broadcasted_iota(
        jnp.int32, (rows, rows), 1
    )
    place_in = jnp.dot(
        lower.astype(F32).astype(BF16), held_f.astype(BF16), preferred_element_type=F32
    )
    pick = jnp.where(held_there & (place_in == (slot + 1).astype(F32)), 1.0, 0.0).astype(BF16)
    pick_ref[...] = pick
    chosen = lax.dot_general(
        pick, packed, (((0,), (0,)), ((), ())), preferred_element_type=F32
    ).astype(BF16)
    for r, c in ((0, c0), (2, c2), (3, c3)):
        c[...] = chosen[r * cap : (r + 1) * cap]
    near_ref[rows:] = chosen[cap : 2 * cap]


def route(blocks, local, cap):
    count, wide = blocks[0].shape
    rows = count * len(blocks)
    vmem = pl.BlockSpec(memory_space=pltpu.VMEM)
    return pl.pallas_call(
        functools.partial(route_kernel, local=local, cap=cap),
        in_specs=[vmem] * 4,
        out_specs=[vmem] * 5,
        out_shape=[sds((rows + cap, wide)), sds((rows, LANES))] + [sds((cap, wide))] * 3,
        scratch_shapes=[pltpu.VMEM((rows, wide), F32)],
        compiler_params=params(),
        cost_estimate=cost(2**20, rows * wide * 8),
        name="route",
    )(*blocks)


def project_kernel(mine_ref, other_ref, w_ref, *refs, which, tile, add, count):
    addend, outs = (refs[0], refs[1:]) if add else (None, refs)
    depth, width = w_ref.shape[0], outs[0].shape[1]
    me, half = lax.axis_index("tensor"), lax.rem(lax.axis_index("batch"), 2)
    rows = jnp.concatenate([mine_ref[:count, :depth], other_ref[:count, :depth]], axis=0)
    for k, r in enumerate(which):
        start = (jnp.bitwise_xor(me, r) * 2 + half) * width
        for low in range(0, width, tile):
            at = pl.ds(pl.multiple_of(start + low, tile), tile)
            product = jnp.dot(rows, w_ref[:, at], preferred_element_type=F32)
            span = slice(low, low + tile)
            if add:
                product = product + addend[:, span].astype(F32)
            outs[k][:, span] = product.astype(BF16)


def project(mine, other, count, weight, width, which, addend=None, tile=512):
    depth = weight.shape[0]
    parts = len(which)
    vmem = pl.BlockSpec(memory_space=pltpu.VMEM)
    operands = [mine, other, weight] + ([] if addend is None else [addend])
    return pl.pallas_call(
        functools.partial(
            project_kernel, which=which, tile=tile, add=addend is not None, count=count
        ),
        in_specs=[vmem] * len(operands),
        out_specs=[vmem] * parts,
        out_shape=[sds((2 * count, width))] * parts,
        compiler_params=params(),
        cost_estimate=cost(4 * count * depth * width * parts, depth * width * 2 * parts),
        name="project",
    )(*operands)


def down_kernel(c0, c1, c2, c3, down_ref, low_ref, slot_ref):
    local, width, rank = down_ref.shape
    cap = c0.shape[0]
    chosen = jnp.concatenate([c0[...], c1[c1.shape[0] - cap :], c2[...], c3[...]], axis=0)
    values = chosen[:, :width]
    slot = chosen[:, width:].astype(F32).astype(jnp.int32) - lax.axis_index("batch") * local
    low = jnp.zeros((chosen.shape[0], rank), F32)
    for a in range(local):
        product = jnp.dot(values, down_ref[a], preferred_element_type=F32)
        low = jnp.where(slot == a, product, low)
    low_ref[...] = low.astype(BF16)
    slot_ref[...] = slot


def down(chosen, weight):
    local, width, rank = weight.shape
    rows = chosen[0].shape[0] * len(chosen)
    vmem = pl.BlockSpec(memory_space=pltpu.VMEM)
    return pl.pallas_call(
        down_kernel,
        in_specs=[vmem] * 5,
        out_specs=[vmem] * 2,
        out_shape=[sds((rows, rank)), sds((rows, rank), jnp.int32)],
        compiler_params=params(),
        cost_estimate=cost(2**34, weight.size * 2),
        name="down",
    )(*chosen, weight)


def up_kernel(ranks, l0, l1, l2, l3, slot_ref, up_ref, *outs, tile):
    local, _, width = up_ref.shape
    low = l0[...].astype(F32)
    for share in (l1, l2, l3):
        low = low + share[...].astype(F32)
    slot = slot_ref[...]
    lane = lax.broadcasted_iota(jnp.int32, low.shape, 1)
    kept = []
    for a in range(local):
        rank = ranks[lax.axis_index("batch") * local + a]
        factor = ADAPTER_SCALE / jnp.full(low.shape, rank, jnp.int32).astype(F32)
        kept.append(jnp.where((slot == a) & (lane < rank), low * factor, 0.0).astype(BF16))
    cap = outs[0].shape[0]
    for start in range(0, width, tile):
        span = slice(start, start + tile)
        total = jnp.dot(kept[0], up_ref[0, :, span], preferred_element_type=F32)
        for a in range(1, local):
            total = total + jnp.dot(kept[a], up_ref[a, :, span], preferred_element_type=F32)
        adapted = total.astype(BF16)
        for r, out in enumerate(outs):
            out[:, span] = adapted[r * cap : (r + 1) * cap]


def up(ranks, shares, slot, weight, parts, tile=512):
    local, rank, width = weight.shape
    rows = slot.shape[0]
    cap = rows // parts
    vmem = pl.BlockSpec(memory_space=pltpu.VMEM)
    return pl.pallas_call(
        functools.partial(up_kernel, tile=tile),
        in_specs=[pl.BlockSpec(memory_space=pltpu.SMEM)] + [vmem] * 6,
        out_specs=[vmem] * parts,
        out_shape=[sds((cap, width))] * parts,
        compiler_params=params(),
        cost_estimate=cost(2**34, weight.size * 2),
        name="up",
    )(ranks, *shares, slot, weight)


def gather_kernel(y0, y1, y2, _, mine, theirs):
    count = mine.shape[0]
    total = y0[...].astype(F32) + y1[...].astype(F32) + y2[...].astype(F32)
    mine[...] = total[:count]
    theirs[...] = total[count:].astype(BF16)


def gather_base(shares, after):
    vmem = pl.BlockSpec(memory_space=pltpu.VMEM)
    count, width = shares[0].shape
    return pl.pallas_call(
        gather_kernel,
        in_specs=[vmem] * 3 + [pl.BlockSpec(memory_space=pl.ANY)],
        out_specs=[vmem] * 2,
        out_shape=[sds((count // 2, width), F32), sds((count // 2, width))],
        compiler_params=params(),
        cost_estimate=cost(2**20, shares[0].size * 12),
        name="gather_base",
    )(*shares, after)


def finish_kernel(pick_ref, m0, m1, a0, a1, a2, a3, out):
    width = m0.shape[1]
    half = lax.rem(lax.axis_index("batch"), 2)
    pick = pick_ref[...][:, : 4 * a0.shape[0]]
    for k, base in enumerate((m0, m1)):
        at = jnp.bitwise_xor(half, k) * width
        span = pl.ds(pl.multiple_of(at, width), width)
        rows = jnp.concatenate([a[:, span] for a in (a0, a1, a2, a3)], axis=0)
        adapted = jnp.dot(pick, rows, preferred_element_type=F32)
        out[:, span] = (base[...].astype(F32) + adapted).astype(BF16)


def finish(pick, shares, adapted):
    vmem = pl.BlockSpec(memory_space=pltpu.VMEM)
    count, width = shares[0].shape
    return pl.pallas_call(
        finish_kernel,
        in_specs=[vmem] * 7,
        out_specs=vmem,
        out_shape=sds((count, 2 * width)),
        compiler_params=params(),
        cost_estimate=cost(2**24, shares[0].size * 16),
        name="finish",
    )(pick, *shares, *adapted)


def across(value, axis, r):
    n = lax.axis_size(axis)
    return lax.ppermute(value, axis, [(i, i ^ r) for i in range(n)])


def per_device_four(
    query,
    fresh_key,
    fresh_value,
    stored_keys,
    stored_values,
    cached_length,
    request_adapter,
    rank_per_adapter,
    output_weight,
    adapter_down_weight,
    adapter_up_weight,
):
    tensor_count = lax.axis_size("tensor")
    batch_count = lax.axis_size("batch")
    local = adapter_down_weight.shape[0]
    width = adapter_up_weight.shape[2]
    requests = query.shape[0]
    cap = 2 * requests * tensor_count // batch_count
    blocks = attend_blocks(
        cached_length,
        request_adapter,
        query,
        fresh_key,
        fresh_value,
        stored_keys,
        stored_values,
    )
    blocks = [across(blocks[3 - r], "tensor", r) for r in (3, 2, 1)] + [blocks[3]]
    near_rows, pick, *chosen = route(blocks, local, cap)
    count = requests * tensor_count
    other = across(near_rows, "batch", 1)
    gathered = [chosen[0], other] + [across(c, "batch", r) for c, r in zip(chosen[1:], (2, 3))]
    both = (near_rows, other, count, output_weight, width // 2)
    far, near, mine = project(*both, (3, 1, 0))
    far_in = across(far, "tensor", 1)
    near_in = across(near, "tensor", 1)

    low, slot = down(gathered, adapter_down_weight)
    shares = [low] + [across(low, "tensor", r) for r in (1, 2, 3)]
    (cross,) = project(*both, (2,), addend=far_in)
    cross_in = across(cross, "tensor", 2)
    lifted = up(rank_per_adapter, shares, slot, adapter_up_weight, batch_count)
    lifted = [lifted[0]] + [across(lifted[r], "batch", r) for r in (1, 2, 3)]
    mine, theirs = gather_base((mine, near_in, cross_in), lifted[0])
    return finish(pick, (mine, across(theirs, "batch", 1)), lifted)


def attend(query, fresh_key, fresh_value, stored_keys, stored_values, cached_length):
    requests = query.shape[0]
    kv_heads, longest, head_dim = stored_keys.shape[1:]
    group_size = query.shape[1] // (kv_heads * head_dim)
    queries = query.reshape(requests, kv_heads, group_size, head_dim)
    scaling = 1.0 / math.sqrt(head_dim)
    scores = (
        jnp.einsum("rkgd,rkld->rkgl", queries, stored_keys, preferred_element_type=F32) * scaling
    )
    own_score = (
        jnp.einsum(
            "rkgd,rkd->rkg",
            queries,
            fresh_key.reshape(requests, kv_heads, head_dim),
            preferred_element_type=F32,
        )
        * scaling
    )
    valid = (jnp.arange(longest, dtype=jnp.int32)[None, :] < cached_length[:, None])[
        :, None, None, :
    ]
    scores = jnp.where(valid, scores, -1e30)
    highest = jnp.maximum(jnp.max(scores, axis=-1), own_score)
    exponent = jnp.where(valid, jnp.exp(scores - highest[..., None]), 0.0)
    own_exp = jnp.exp(own_score - highest)
    sum_exp = jnp.sum(exponent, axis=-1) + own_exp
    weights = (exponent / sum_exp[..., None]).astype(BF16)
    own_weight = (own_exp / sum_exp).astype(BF16)
    result = jnp.einsum("rkgl,rkld->rkgd", weights, stored_values, preferred_element_type=F32)
    own_value = fresh_value.reshape(requests, kv_heads, 1, head_dim).astype(F32)
    result = result + own_weight.astype(F32)[..., None] * own_value
    return result.reshape(requests, -1).astype(BF16)


def per_device_any(
    query,
    fresh_key,
    fresh_value,
    stored_keys,
    stored_values,
    cached_length,
    request_adapter,
    rank_per_adapter,
    output_weight,
    adapter_down_weight,
    adapter_up_weight,
):
    attended = attend(query, fresh_key, fresh_value, stored_keys, stored_values, cached_length)
    batch_count = lax.axis_size("batch")
    local, _, rank_span = adapter_down_weight.shape
    head_rows = lax.all_to_all(attended, "tensor", split_axis=1, concat_axis=0, tiled=True)
    row_count = head_rows.shape[0]
    products = jnp.dot(head_rows, output_weight, preferred_element_type=F32)
    base = lax.psum_scatter(
        products.astype(BF16), "tensor", scatter_dimension=1, tiled=True
    ).astype(F32)
    all_rows = lax.all_gather(head_rows, "batch", axis=0, tiled=True)
    ids = lax.all_gather(request_adapter, ("batch", "tensor"), axis=0, tiled=True)
    slot = ids - lax.axis_index("batch") * local
    one_hot = slot[:, None] == jnp.arange(local, dtype=jnp.int32)[None, :]
    low_every = jnp.einsum("rk,skj->rsj", all_rows, adapter_down_weight, preferred_element_type=F32)
    low = jnp.sum(jnp.where(one_hot[:, :, None], low_every, 0.0), axis=1)
    low = lax.psum(low.astype(BF16), "tensor").astype(F32)
    adapter_count = rank_per_adapter.shape[0]
    picked = ids[:, None] == jnp.arange(adapter_count, dtype=jnp.int32)[None, :]
    row_rank = jnp.sum(jnp.where(picked, rank_per_adapter[None, :], 0), axis=1)[:, None]
    kept = jnp.arange(rank_span, dtype=jnp.int32)[None, :] < row_rank
    delta = jnp.where(kept, low * (ADAPTER_SCALE / row_rank.astype(F32)), 0.0).astype(BF16)
    widened = jnp.where(one_hot[:, :, None], delta[:, None, :], jnp.zeros((), BF16))
    adapted = jnp.dot(
        widened.reshape(ids.shape[0], local * rank_span),
        adapter_up_weight.reshape(local * rank_span, -1),
        preferred_element_type=F32,
    ).astype(BF16)
    adapted = lax.all_to_all(
        adapted.reshape(batch_count, row_count, -1), "batch", split_axis=0, concat_axis=0, tiled=True
    )
    adapted = jnp.sum(adapted.astype(F32), axis=0)
    return (base + adapted).astype(BF16)


def solution(mesh):
    in_specs = (
        P(("group", "batch", "tensor"), None),
        P(("group", "batch", "tensor"), None),
        P(("group", "batch", "tensor"), None),
        P(("group", "batch", "tensor"), None, None, None),
        P(("group", "batch", "tensor"), None, None, None),
        P(("group", "batch", "tensor")),
        P(("group", "batch", "tensor")),
        P(),
        P("tensor", None),
        P("batch", "tensor", None),
        P("batch", None, "tensor"),
    )
    out_specs = P(("group", "batch"), "tensor")

    def whole(*arrays):
        tensor_count, batch_count = mesh.shape["tensor"], mesh.shape["batch"]
        four = tensor_count == batch_count == arrays[3].shape[1] == 4
        body = per_device_four if four else per_device_any
        return jax.shard_map(
            body, mesh=mesh, in_specs=in_specs, out_specs=out_specs, check_vma=False
        )(*arrays)

    return whole
```

```python
import functools
import math

import jax
import jax.numpy as jnp
from jax import lax
from jax.experimental import pallas as pl
from jax.experimental.pallas import tpu as pltpu
from jax.sharding import PartitionSpec as P

ADAPTER_SCALE = 16.0
F32 = jnp.float32
BF16 = jnp.bfloat16
LANES = 128
MIB = 1024 * 1024


def params(grid_rank=0, vmem=24 * MIB):
    if grid_rank:
        return pltpu.CompilerParams(
            dimension_semantics=("arbitrary",) * grid_rank, vmem_limit_bytes=vmem
        )
    return pltpu.CompilerParams(vmem_limit_bytes=vmem)


def cost(flops, nbytes):
    return pl.CostEstimate(flops=flops, bytes_accessed=nbytes, transcendentals=0)


def sds(shape, dtype=BF16):
    return jax.ShapeDtypeStruct(shape, dtype)


def column_of(ref, count):
    rows = lax.broadcasted_iota(jnp.int32, (count, LANES), 0)
    out = jnp.full((count, LANES), ref[0], jnp.int32)
    for i in range(1, count):
        out = jnp.where(rows == i, ref[i], out)
    return out


def attend_kernel(*refs, kv):
    length_hbm, adapter_hbm, q_hbm, fk_hbm, fv_hbm, k_hbm, v_hbm = refs[:7]
    outs = refs[7 : 7 + kv]
    length, adapter, q_buf, fk_buf, fv_buf, k_buf, v_buf, small, big = refs[7 + kv :]
    requests, _, longest, dim = k_hbm.shape
    width = q_hbm.shape[1] // kv
    group = width // dim
    rows = group * requests
    scaling = 1.0 / math.sqrt(dim)
    me = lax.axis_index("tensor")
    order = tuple(range(kv - 1, -1, -1))

    ready = [
        pltpu.make_async_copy(source, target, small.at[i])
        for i, (source, target) in enumerate(
            (
                (q_hbm, q_buf),
                (fk_hbm, fk_buf),
                (fv_hbm, fv_buf),
                (length_hbm, length),
                (adapter_hbm, adapter),
            )
        )
    ]
    keys_in = {}
    values_in = {}
    for r in order:
        head = jnp.bitwise_xor(me, r)
        keys_in[r] = pltpu.make_async_copy(k_hbm.at[:, head], k_buf.at[r], big.at[0, r])
        values_in[r] = pltpu.make_async_copy(v_hbm.at[:, head], v_buf.at[r], big.at[1, r])
    for copy in ready:
        copy.start()
    for r in order:
        keys_in[r].start()
    for r in order:
        values_in[r].start()
    for copy in ready:
        copy.wait()

    request = lax.rem(lax.broadcasted_iota(jnp.int32, (rows, longest), 0), requests)
    lengths = jnp.concatenate([column_of(length, requests)] * group, axis=0)
    valid = lax.broadcasted_iota(jnp.int32, (rows, longest), 1) < lengths
    ids = column_of(adapter, requests).astype(F32)
    scores, own, fresh_value = {}, {}, {}
    for r in order:
        head = jnp.bitwise_xor(me, r)
        mine = pl.ds(pl.multiple_of(head * dim, dim), dim)
        q32 = q_buf[:, pl.ds(pl.multiple_of(head * width, width), width)].astype(F32)
        queries = jnp.concatenate([q32[:, h * dim : (h + 1) * dim] for h in range(group)], axis=0)
        fresh_key = jnp.concatenate([fk_buf[:, mine].astype(F32)] * group, axis=0)
        fresh_value[r] = jnp.concatenate([fv_buf[:, mine].astype(F32)] * group, axis=0)
        own[r] = jnp.sum(queries * fresh_key, axis=1, keepdims=True) * scaling
        scores[r] = queries.astype(BF16)
    for r in order:
        keys_in[r].wait()
    for r in order:
        every = lax.dot_general(
            scores[r],
            k_buf[r].reshape(requests * longest, dim),
            (((1,), (1,)), ((), ())),
            preferred_element_type=F32,
        )
        picked = every[:, :longest]
        for i in range(1, requests):
            picked = jnp.where(request == i, every[:, i * longest : (i + 1) * longest], picked)
        scores[r] = jnp.where(valid, picked * scaling, -1e30)
    highest = {r: jnp.maximum(jnp.max(scores[r], axis=1, keepdims=True), own[r]) for r in order}
    exponent = {r: jnp.where(valid, jnp.exp(scores[r] - highest[r]), 0.0) for r in order}
    own_exp = {r: jnp.exp(own[r] - highest[r]) for r in order}
    inverse = {
        r: 1.0 / (jnp.sum(exponent[r], axis=1, keepdims=True) + own_exp[r]) for r in order
    }
    spread = {}
    for r in order:
        weights = exponent[r] * inverse[r]
        spread[r] = jnp.concatenate(
            [jnp.where(request == i, weights, 0.0) for i in range(requests)], axis=1
        ).astype(BF16)
    for r in order:
        values_in[r].wait()
    for r in order:
        own_weight = (own_exp[r] * inverse[r]).astype(BF16).astype(F32)
        result = (
            jnp.dot(
                spread[r], v_buf[r].reshape(requests * longest, dim), preferred_element_type=F32
            )
            + own_weight * fresh_value[r]
        )
        pieces = [result[h * requests : (h + 1) * requests] for h in range(group)]
        outs[kv - 1 - r][...] = jnp.concatenate(pieces + [ids], axis=1).astype(BF16)


def attend_blocks(length, adapter, query, fresh_key, fresh_value, keys, values):
    requests, kv, longest, dim = keys.shape
    width = query.shape[1] // kv
    hbm = pl.BlockSpec(memory_space=pltpu.HBM)
    return pl.pallas_call(
        functools.partial(attend_kernel, kv=kv),
        in_specs=[hbm] * 7,
        out_specs=[pl.BlockSpec(memory_space=pltpu.VMEM)] * kv,
        out_shape=[sds((requests, width + LANES))] * kv,
        scratch_shapes=[
            pltpu.SMEM(length.shape, jnp.int32),
            pltpu.SMEM(adapter.shape, jnp.int32),
            pltpu.VMEM(query.shape, BF16),
            pltpu.VMEM(fresh_key.shape, BF16),
            pltpu.VMEM(fresh_value.shape, BF16),
            pltpu.VMEM((kv, requests, longest, dim), BF16),
            pltpu.VMEM((kv, requests, longest, dim), BF16),
            pltpu.SemaphoreType.DMA((5,)),
            pltpu.SemaphoreType.DMA((2, kv)),
        ],
        compiler_params=params(),
        cost_estimate=cost(2**35, 2 * keys.size * 2),
        name="attend",
    )(*[pltpu.with_memory_space_constraint(x, pltpu.HBM) for x in (length, adapter, query, fresh_key, fresh_value, keys, values)])


def route_kernel(x0, x1, x2, x3, rows_ref, pick_ref, c0, c1, c2, c3, held, *, local, cap):
    me, mine = lax.axis_index("tensor"), lax.axis_index("batch")
    count = x0.shape[0]
    for r, x in zip((3, 2, 1, 0), (x0, x1, x2, x3)):
        held[pl.ds(pl.multiple_of(jnp.bitwise_xor(me, r) * count, count), count), :] = x[
            ...
        ].astype(F32)
    every = held[...]
    packed = every.astype(BF16)
    rows, wide = every.shape
    width = wide - LANES
    rows_ref[...] = packed[:, :width]
    adapter = every[:, width:].astype(jnp.int32)
    lane = lax.broadcasted_iota(jnp.int32, (rows, LANES), 1)
    part, slot = lax.div(lane, cap), lax.rem(lane, cap)
    first = jnp.bitwise_xor(mine, part) * local
    held_there = (adapter >= first) & (adapter < first + local) & (part < 4)
    held_f = held_there.astype(F32)
    lower = lax.broadcasted_iota(jnp.int32, (rows, rows), 0) >= lax.broadcasted_iota(
        jnp.int32, (rows, rows), 1
    )
    place_in = jnp.dot(
        lower.astype(F32).astype(BF16), held_f.astype(BF16), preferred_element_type=F32
    )
    pick = jnp.where(held_there & (place_in == (slot + 1).astype(F32)), 1.0, 0.0).astype(BF16)
    pick_ref[...] = pick
    chosen = lax.dot_general(
        pick, packed, (((0,), (0,)), ((), ())), preferred_element_type=F32
    ).astype(BF16)
    for r, c in enumerate((c0, c1, c2, c3)):
        c[...] = chosen[r * cap : (r + 1) * cap]


def route(blocks, local, cap):
    count, wide = blocks[0].shape
    rows = count * len(blocks)
    vmem = pl.BlockSpec(memory_space=pltpu.VMEM)
    return pl.pallas_call(
        functools.partial(route_kernel, local=local, cap=cap),
        in_specs=[vmem] * 4,
        out_specs=[vmem] * 6,
        out_shape=[sds((rows, wide - LANES)), sds((rows, LANES))] + [sds((cap, wide))] * 4,
        scratch_shapes=[pltpu.VMEM((rows, wide), F32)],
        compiler_params=params(),
        cost_estimate=cost(2**20, rows * wide * 8),
        name="route",
    )(*blocks)


def project_kernel(rows_ref, w_ref, *refs, which, tile, add):
    addend, outs = (refs[0], refs[1:]) if add else (None, refs)
    width = outs[0].shape[1]
    me = lax.axis_index("tensor")
    rows = rows_ref[...]
    for k, r in enumerate(which):
        start = jnp.bitwise_xor(me, r) * width
        for low in range(0, width, tile):
            at = pl.ds(pl.multiple_of(start + low, tile), tile)
            product = jnp.dot(rows, w_ref[:, at], preferred_element_type=F32)
            span = slice(low, low + tile)
            if add and k == 0:
                product = product + addend[:, span].astype(F32)
            outs[k][:, span] = product.astype(BF16)


def project(rows, weight, width, which, addend=None, tile=512):
    count, depth = rows.shape
    parts = len(which)
    vmem = pl.BlockSpec(memory_space=pltpu.VMEM)
    operands = [rows, weight] + ([] if addend is None else [addend])
    return pl.pallas_call(
        functools.partial(project_kernel, which=which, tile=tile, add=addend is not None),
        in_specs=[vmem] * len(operands),
        out_specs=[vmem] * parts,
        out_shape=[sds((count, width))] * parts,
        compiler_params=params(),
        cost_estimate=cost(2 * count * depth * width * parts, depth * width * 2 * parts),
        name="project",
    )(*operands)


def down_kernel(c0, c1, c2, c3, down_ref, low_ref, slot_ref):
    local, width, rank = down_ref.shape
    chosen = jnp.concatenate([c[...] for c in (c0, c1, c2, c3)], axis=0)
    values = chosen[:, :width]
    slot = chosen[:, width:].astype(F32).astype(jnp.int32) - lax.axis_index("batch") * local
    low = jnp.zeros((chosen.shape[0], rank), F32)
    for a in range(local):
        product = jnp.dot(values, down_ref[a], preferred_element_type=F32)
        low = jnp.where(slot == a, product, low)
    low_ref[...] = low.astype(BF16)
    slot_ref[...] = slot


def down(chosen, weight):
    local, width, rank = weight.shape
    rows = chosen[0].shape[0] * len(chosen)
    vmem = pl.BlockSpec(memory_space=pltpu.VMEM)
    return pl.pallas_call(
        down_kernel,
        in_specs=[vmem] * 5,
        out_specs=[vmem] * 2,
        out_shape=[sds((rows, rank)), sds((rows, rank), jnp.int32)],
        compiler_params=params(),
        cost_estimate=cost(2**34, weight.size * 2),
        name="down",
    )(*chosen, weight)


def up_kernel(ranks, l0, l1, l2, l3, slot_ref, up_ref, *outs, tile):
    local, _, width = up_ref.shape
    low = l0[...].astype(F32)
    for share in (l1, l2, l3):
        low = low + share[...].astype(F32)
    slot = slot_ref[...]
    lane = lax.broadcasted_iota(jnp.int32, low.shape, 1)
    kept = []
    for a in range(local):
        rank = ranks[lax.axis_index("batch") * local + a]
        factor = ADAPTER_SCALE / jnp.full(low.shape, rank, jnp.int32).astype(F32)
        kept.append(jnp.where((slot == a) & (lane < rank), low * factor, 0.0).astype(BF16))
    cap = outs[0].shape[0]
    for start in range(0, width, tile):
        span = slice(start, start + tile)
        total = jnp.dot(kept[0], up_ref[0, :, span], preferred_element_type=F32)
        for a in range(1, local):
            total = total + jnp.dot(kept[a], up_ref[a, :, span], preferred_element_type=F32)
        adapted = total.astype(BF16)
        for r, out in zip((2, 3, 1, 0), outs):
            out[:, span] = adapted[r * cap : (r + 1) * cap]


def up(ranks, shares, slot, weight, parts, tile=512):
    local, rank, width = weight.shape
    rows = slot.shape[0]
    cap = rows // parts
    vmem = pl.BlockSpec(memory_space=pltpu.VMEM)
    return pl.pallas_call(
        functools.partial(up_kernel, tile=tile),
        in_specs=[pl.BlockSpec(memory_space=pltpu.SMEM)] + [vmem] * 6,
        out_specs=[vmem] * parts,
        out_shape=[sds((cap, width))] * parts,
        compiler_params=params(),
        cost_estimate=cost(2**34, weight.size * 2),
        name="up",
    )(ranks, *shares, slot, weight)


def finish_kernel(pick_ref, y0, y1, y2, a2, a3, a1, a0, out):
    rows = jnp.concatenate([a[...] for a in (a0, a1, a2, a3)], axis=0)
    pick = pick_ref[...][:, : rows.shape[0]]
    adapted = jnp.dot(pick, rows, preferred_element_type=F32)
    base = y0[...].astype(F32) + y1[...].astype(F32) + y2[...].astype(F32)
    out[...] = (base + adapted).astype(BF16)


def finish(pick, shares, adapted):
    vmem = pl.BlockSpec(memory_space=pltpu.VMEM)
    return pl.pallas_call(
        finish_kernel,
        in_specs=[vmem] * 8,
        out_specs=vmem,
        out_shape=sds(shares[0].shape),
        compiler_params=params(),
        cost_estimate=cost(2**24, shares[0].size * 16),
        name="finish",
    )(pick, *shares, *adapted)


def across(value, axis, r):
    n = lax.axis_size(axis)
    return lax.ppermute(value, axis, [(i, i ^ r) for i in range(n)])


def per_device_four(
    query,
    fresh_key,
    fresh_value,
    stored_keys,
    stored_values,
    cached_length,
    request_adapter,
    rank_per_adapter,
    output_weight,
    adapter_down_weight,
    adapter_up_weight,
):
    tensor_count = lax.axis_size("tensor")
    batch_count = lax.axis_size("batch")
    local = adapter_down_weight.shape[0]
    width = adapter_up_weight.shape[2]
    requests = query.shape[0]
    cap = 2 * requests * tensor_count // batch_count
    blocks = attend_blocks(
        cached_length,
        request_adapter,
        query,
        fresh_key,
        fresh_value,
        stored_keys,
        stored_values,
    )
    blocks = [across(blocks[3 - r], "tensor", r) for r in (3, 2, 1)] + [blocks[3]]
    rows, pick, *chosen = route(blocks, local, cap)

    gathered = [chosen[0]] + [across(chosen[r], "batch", r) for r in (1, 2, 3)]
    far, near = project(rows, output_weight, width, (3, 1))
    far_in = across(far, "tensor", 1)
    near_in = across(near, "tensor", 1)

    low, slot = down(gathered, adapter_down_weight)
    shares = [low] + [across(low, "tensor", r) for r in (1, 2, 3)]
    (cross,) = project(rows, output_weight, width, (2,), addend=far_in)
    (mine,) = project(rows, output_weight, width, (0,))
    cross_in = across(cross, "tensor", 2)

    lifted = up(rank_per_adapter, shares, slot, adapter_up_weight, batch_count)
    lifted = [across(a, "batch", r) for a, r in zip(lifted, (2, 3, 1))] + [lifted[3]]
    return finish(pick, (mine, near_in, cross_in), lifted)


def attend(query, fresh_key, fresh_value, stored_keys, stored_values, cached_length):
    requests = query.shape[0]
    kv_heads, longest, head_dim = stored_keys.shape[1:]
    group_size = query.shape[1] // (kv_heads * head_dim)
    queries = query.reshape(requests, kv_heads, group_size, head_dim)
    scaling = 1.0 / math.sqrt(head_dim)
    scores = (
        jnp.einsum("rkgd,rkld->rkgl", queries, stored_keys, preferred_element_type=F32) * scaling
    )
    own_score = (
        jnp.einsum(
            "rkgd,rkd->rkg",
            queries,
            fresh_key.reshape(requests, kv_heads, head_dim),
            preferred_element_type=F32,
        )
        * scaling
    )
    valid = (jnp.arange(longest, dtype=jnp.int32)[None, :] < cached_length[:, None])[
        :, None, None, :
    ]
    scores = jnp.where(valid, scores, -1e30)
    highest = jnp.maximum(jnp.max(scores, axis=-1), own_score)
    exponent = jnp.where(valid, jnp.exp(scores - highest[..., None]), 0.0)
    own_exp = jnp.exp(own_score - highest)
    sum_exp = jnp.sum(exponent, axis=-1) + own_exp
    weights = (exponent / sum_exp[..., None]).astype(BF16)
    own_weight = (own_exp / sum_exp).astype(BF16)
    result = jnp.einsum("rkgl,rkld->rkgd", weights, stored_values, preferred_element_type=F32)
    own_value = fresh_value.reshape(requests, kv_heads, 1, head_dim).astype(F32)
    result = result + own_weight.astype(F32)[..., None] * own_value
    return result.reshape(requests, -1).astype(BF16)


def per_device_any(
    query,
    fresh_key,
    fresh_value,
    stored_keys,
    stored_values,
    cached_length,
    request_adapter,
    rank_per_adapter,
    output_weight,
    adapter_down_weight,
    adapter_up_weight,
):
    attended = attend(query, fresh_key, fresh_value, stored_keys, stored_values, cached_length)
    batch_count = lax.axis_size("batch")
    local, _, rank_span = adapter_down_weight.shape
    head_rows = lax.all_to_all(attended, "tensor", split_axis=1, concat_axis=0, tiled=True)
    row_count = head_rows.shape[0]
    products = jnp.dot(head_rows, output_weight, preferred_element_type=F32)
    base = lax.psum_scatter(
        products.astype(BF16), "tensor", scatter_dimension=1, tiled=True
    ).astype(F32)
    all_rows = lax.all_gather(head_rows, "batch", axis=0, tiled=True)
    ids = lax.all_gather(request_adapter, ("batch", "tensor"), axis=0, tiled=True)
    slot = ids - lax.axis_index("batch") * local
    one_hot = slot[:, None] == jnp.arange(local, dtype=jnp.int32)[None, :]
    low_every = jnp.einsum("rk,skj->rsj", all_rows, adapter_down_weight, preferred_element_type=F32)
    low = jnp.sum(jnp.where(one_hot[:, :, None], low_every, 0.0), axis=1)
    low = lax.psum(low.astype(BF16), "tensor").astype(F32)
    adapter_count = rank_per_adapter.shape[0]
    picked = ids[:, None] == jnp.arange(adapter_count, dtype=jnp.int32)[None, :]
    row_rank = jnp.sum(jnp.where(picked, rank_per_adapter[None, :], 0), axis=1)[:, None]
    kept = jnp.arange(rank_span, dtype=jnp.int32)[None, :] < row_rank
    delta = jnp.where(kept, low * (ADAPTER_SCALE / row_rank.astype(F32)), 0.0).astype(BF16)
    widened = jnp.where(one_hot[:, :, None], delta[:, None, :], jnp.zeros((), BF16))
    adapted = jnp.dot(
        widened.reshape(ids.shape[0], local * rank_span),
        adapter_up_weight.reshape(local * rank_span, -1),
        preferred_element_type=F32,
    ).astype(BF16)
    adapted = lax.all_to_all(
        adapted.reshape(batch_count, row_count, -1), "batch", split_axis=0, concat_axis=0, tiled=True
    )
    adapted = jnp.sum(adapted.astype(F32), axis=0)
    return (base + adapted).astype(BF16)


def solution(mesh):
    in_specs = (
        P(("group", "batch", "tensor"), None),
        P(("group", "batch", "tensor"), None),
        P(("group", "batch", "tensor"), None),
        P(("group", "batch", "tensor"), None, None, None),
        P(("group", "batch", "tensor"), None, None, None),
        P(("group", "batch", "tensor")),
        P(("group", "batch", "tensor")),
        P(),
        P("tensor", None),
        P("batch", "tensor", None),
        P("batch", None, "tensor"),
    )
    out_specs = P(("group", "batch"), "tensor")

    def whole(*arrays):
        tensor_count, batch_count = mesh.shape["tensor"], mesh.shape["batch"]
        four = tensor_count == batch_count == arrays[3].shape[1] == 4
        body = per_device_four if four else per_device_any
        return jax.shard_map(
            body, mesh=mesh, in_specs=in_specs, out_specs=out_specs, check_vma=False
        )(*arrays)

    return whole
```

```python
import functools
import math

import jax
import jax.numpy as jnp
from jax import lax
from jax.experimental import pallas as pl
from jax.experimental.pallas import tpu as pltpu
from jax.sharding import PartitionSpec as P

ADAPTER_SCALE = 16.0
F32 = jnp.float32
BF16 = jnp.bfloat16
LANES = 128
MIB = 1024 * 1024


def params(grid_rank=0, vmem=24 * MIB):
    if grid_rank:
        return pltpu.CompilerParams(
            dimension_semantics=("arbitrary",) * grid_rank, vmem_limit_bytes=vmem
        )
    return pltpu.CompilerParams(vmem_limit_bytes=vmem)


def cost(flops, nbytes):
    return pl.CostEstimate(flops=flops, bytes_accessed=nbytes, transcendentals=0)


def sds(shape, dtype=BF16):
    return jax.ShapeDtypeStruct(shape, dtype)


def column_of(values):
    count = len(values)
    rows = lax.broadcasted_iota(jnp.int32, (count, LANES), 0)
    out = jnp.full((count, LANES), values[0], jnp.int32)
    for i in range(1, count):
        out = jnp.where(rows == i, values[i], out)
    return out


def attend_kernel(*refs, kv):
    length_hbm, adapter_hbm, ranks_hbm, q_hbm, fk_hbm, fv_hbm, k_hbm, v_hbm = refs[:8]
    outs = refs[8 : 8 + kv]
    length, adapter, ranks, q_buf, fk_buf, fv_buf, k_buf, v_buf, small, big = refs[8 + kv :]
    requests, _, longest, dim = k_hbm.shape
    width = q_hbm.shape[1] // kv
    group = width // dim
    rows = group * requests
    scaling = 1.0 / math.sqrt(dim)
    me = lax.axis_index("tensor")
    order = tuple(range(kv - 1, -1, -1))

    ready = [
        pltpu.make_async_copy(source, target, small.at[i])
        for i, (source, target) in enumerate(
            (
                (q_hbm, q_buf),
                (fk_hbm, fk_buf),
                (fv_hbm, fv_buf),
                (length_hbm, length),
                (adapter_hbm, adapter),
                (ranks_hbm, ranks),
            )
        )
    ]
    keys_in = pltpu.make_async_copy(k_hbm, k_buf, big.at[0])
    values_in = pltpu.make_async_copy(v_hbm, v_buf, big.at[1])
    for copy in ready:
        copy.start()
    keys_in.start()
    values_in.start()
    for copy in ready:
        copy.wait()

    request = lax.rem(lax.broadcasted_iota(jnp.int32, (rows, longest), 0), requests)
    lengths = jnp.concatenate(
        [column_of([length[i] for i in range(requests)])] * group, axis=0
    )
    valid = lax.broadcasted_iota(jnp.int32, (rows, longest), 1) < lengths
    named = [adapter[i] for i in range(requests)]
    lane = lax.broadcasted_iota(jnp.int32, (requests, LANES), 1)
    ids = jnp.where(
        lane < LANES // 2, column_of(named), column_of([ranks[a] for a in named])
    ).astype(F32)
    scores, own, fresh_value = {}, {}, {}
    for r in order:
        head = jnp.bitwise_xor(me, r)
        mine = pl.ds(pl.multiple_of(head * dim, dim), dim)
        q32 = q_buf[:, pl.ds(pl.multiple_of(head * width, width), width)].astype(F32)
        queries = jnp.concatenate([q32[:, h * dim : (h + 1) * dim] for h in range(group)], axis=0)
        fresh_key = jnp.concatenate([fk_buf[:, mine].astype(F32)] * group, axis=0)
        fresh_value[r] = jnp.concatenate([fv_buf[:, mine].astype(F32)] * group, axis=0)
        own[r] = jnp.sum(queries * fresh_key, axis=1, keepdims=True) * scaling
        scores[r] = queries.astype(BF16)
    keys_in.wait()
    for r in order:
        every = lax.dot_general(
            scores[r],
            k_buf[:, jnp.bitwise_xor(me, r)].reshape(requests * longest, dim),
            (((1,), (1,)), ((), ())),
            preferred_element_type=F32,
        )
        picked = every[:, :longest]
        for i in range(1, requests):
            picked = jnp.where(request == i, every[:, i * longest : (i + 1) * longest], picked)
        scores[r] = jnp.where(valid, picked * scaling, -1e30)
    highest = {r: jnp.maximum(jnp.max(scores[r], axis=1, keepdims=True), own[r]) for r in order}
    exponent = {r: jnp.where(valid, jnp.exp(scores[r] - highest[r]), 0.0) for r in order}
    own_exp = {r: jnp.exp(own[r] - highest[r]) for r in order}
    inverse = {
        r: 1.0 / (jnp.sum(exponent[r], axis=1, keepdims=True) + own_exp[r]) for r in order
    }
    spread = {}
    for r in order:
        weights = exponent[r] * inverse[r]
        spread[r] = jnp.concatenate(
            [jnp.where(request == i, weights, 0.0) for i in range(requests)], axis=1
        ).astype(BF16)
    values_in.wait()
    for r in order:
        own_weight = (own_exp[r] * inverse[r]).astype(BF16).astype(F32)
        result = (
            jnp.dot(
                spread[r], v_buf[:, jnp.bitwise_xor(me, r)].reshape(requests * longest, dim), preferred_element_type=F32
            )
            + own_weight * fresh_value[r]
        )
        pieces = [result[h * requests : (h + 1) * requests] for h in range(group)]
        outs[kv - 1 - r][...] = jnp.concatenate(pieces + [ids], axis=1).astype(BF16)


def attend_blocks(length, adapter, ranks, query, fresh_key, fresh_value, keys, values):
    requests, kv, longest, dim = keys.shape
    width = query.shape[1] // kv
    hbm = pl.BlockSpec(memory_space=pltpu.HBM)
    return pl.pallas_call(
        functools.partial(attend_kernel, kv=kv),
        in_specs=[hbm] * 8,
        out_specs=[pl.BlockSpec(memory_space=pltpu.VMEM)] * kv,
        out_shape=[sds((requests, width + LANES))] * kv,
        scratch_shapes=[
            pltpu.SMEM(length.shape, jnp.int32),
            pltpu.SMEM(adapter.shape, jnp.int32),
            pltpu.SMEM(ranks.shape, jnp.int32),
            pltpu.VMEM(query.shape, BF16),
            pltpu.VMEM(fresh_key.shape, BF16),
            pltpu.VMEM(fresh_value.shape, BF16),
            pltpu.VMEM(keys.shape, BF16),
            pltpu.VMEM(values.shape, BF16),
            pltpu.SemaphoreType.DMA((6,)),
            pltpu.SemaphoreType.DMA((2,)),
        ],
        compiler_params=params(),
        cost_estimate=cost(2**35, 2 * keys.size * 2),
        name="attend",
    )(*[pltpu.with_memory_space_constraint(x, pltpu.HBM) for x in (length, adapter, ranks, query, fresh_key, fresh_value, keys, values)])


def route_kernel(x0, x1, x2, x3, rows_ref, pick_ref, c0, c1, c2, c3, held, *, local, cap):
    me, mine = lax.axis_index("tensor"), lax.axis_index("batch")
    count = x0.shape[0]
    for r, x in zip((3, 2, 1, 0), (x0, x1, x2, x3)):
        held[pl.ds(pl.multiple_of(jnp.bitwise_xor(me, r) * count, count), count), :] = x[
            ...
        ].astype(F32)
    every = held[...]
    packed = every.astype(BF16)
    rows, wide = every.shape
    width = wide - LANES
    rows_ref[...] = packed[:, :width]
    adapter = every[:, width:].astype(jnp.int32)
    lane = lax.broadcasted_iota(jnp.int32, (rows, LANES), 1)
    part, slot = lax.div(lane, cap), lax.rem(lane, cap)
    first = jnp.bitwise_xor(mine, part) * local
    held_there = (adapter >= first) & (adapter < first + local) & (part < 4)
    held_f = held_there.astype(F32)
    lower = lax.broadcasted_iota(jnp.int32, (rows, rows), 0) >= lax.broadcasted_iota(
        jnp.int32, (rows, rows), 1
    )
    place_in = jnp.dot(
        lower.astype(F32).astype(BF16), held_f.astype(BF16), preferred_element_type=F32
    )
    pick = jnp.where(held_there & (place_in == (slot + 1).astype(F32)), 1.0, 0.0).astype(BF16)
    pick_ref[...] = pick
    chosen = lax.dot_general(
        pick, packed, (((0,), (0,)), ((), ())), preferred_element_type=F32
    ).astype(BF16)
    for r, c in enumerate((c0, c1, c2, c3)):
        c[...] = chosen[r * cap : (r + 1) * cap]


def route(blocks, local, cap):
    count, wide = blocks[0].shape
    rows = count * len(blocks)
    vmem = pl.BlockSpec(memory_space=pltpu.VMEM)
    return pl.pallas_call(
        functools.partial(route_kernel, local=local, cap=cap),
        in_specs=[vmem] * 4,
        out_specs=[vmem] * 6,
        out_shape=[sds((rows, wide - LANES)), sds((rows, LANES))] + [sds((cap, wide))] * 4,
        scratch_shapes=[pltpu.VMEM((rows, wide), F32)],
        compiler_params=params(),
        cost_estimate=cost(2**20, rows * wide * 8),
        name="route",
    )(*blocks)


def project_kernel(rows_ref, w_ref, *refs, which, tile, add):
    addend, outs = (refs[0], refs[1:]) if add else (None, refs)
    width = outs[0].shape[1]
    me = lax.axis_index("tensor")
    rows = rows_ref[...]
    for k, r in enumerate(which):
        start = jnp.bitwise_xor(me, r) * width
        for low in range(0, width, tile):
            at = pl.ds(pl.multiple_of(start + low, tile), tile)
            product = jnp.dot(rows, w_ref[:, at], preferred_element_type=F32)
            span = slice(low, low + tile)
            if add and k == 0:
                product = product + addend[:, span].astype(F32)
            outs[k][:, span] = product.astype(BF16)


def project(rows, weight, width, which, addend=None, tile=512):
    count, depth = rows.shape
    parts = len(which)
    vmem = pl.BlockSpec(memory_space=pltpu.VMEM)
    operands = [rows, weight] + ([] if addend is None else [addend])
    return pl.pallas_call(
        functools.partial(project_kernel, which=which, tile=tile, add=addend is not None),
        in_specs=[vmem] * len(operands),
        out_specs=[vmem] * parts,
        out_shape=[sds((count, width))] * parts,
        compiler_params=params(),
        cost_estimate=cost(2 * count * depth * width * parts, depth * width * 2 * parts),
        name="project",
    )(*operands)


def down_kernel(c0, c1, c2, c3, down_ref, low_ref, slot_ref, factor_ref):
    local, width, rank = down_ref.shape
    chosen = jnp.concatenate([c[...] for c in (c0, c1, c2, c3)], axis=0)
    values = chosen[:, :width]
    tail = chosen[:, width:].astype(F32)
    half = tail.shape[1] // 2
    slot = jnp.concatenate([tail[:, :half]] * 2, axis=1).astype(jnp.int32)
    slot = slot - lax.axis_index("batch") * local
    ranks = jnp.concatenate([tail[:, half:]] * 2, axis=1)
    lane = lax.broadcasted_iota(jnp.int32, slot.shape, 1).astype(F32)
    factor_ref[...] = jnp.where(lane < ranks, ADAPTER_SCALE / jnp.maximum(ranks, 1.0), 0.0)
    low = jnp.zeros((chosen.shape[0], rank), F32)
    for a in range(local):
        product = jnp.dot(values, down_ref[a], preferred_element_type=F32)
        low = jnp.where(slot == a, product, low)
    low_ref[...] = low.astype(BF16)
    slot_ref[...] = slot


def down(chosen, weight):
    local, width, rank = weight.shape
    rows = chosen[0].shape[0] * len(chosen)
    vmem = pl.BlockSpec(memory_space=pltpu.VMEM)
    return pl.pallas_call(
        down_kernel,
        in_specs=[vmem] * 5,
        out_specs=[vmem] * 3,
        out_shape=[sds((rows, rank)), sds((rows, rank), jnp.int32), sds((rows, rank), F32)],
        compiler_params=params(),
        cost_estimate=cost(2**34, weight.size * 2),
        name="down",
    )(*chosen, weight)


def up_kernel(l0, l1, l2, l3, slot_ref, factor_ref, up_ref, *outs, tile):
    local, depth, width = up_ref.shape
    low = l0[...].astype(F32)
    for share in (l1, l2, l3):
        low = low + share[...].astype(F32)
    low = low * factor_ref[...]
    slot = slot_ref[...]
    kept = jnp.concatenate(
        [jnp.where(slot == a, low, 0.0).astype(BF16) for a in range(local)], axis=1
    )
    cap = outs[0].shape[0]
    for start in range(0, width, tile):
        span = slice(start, start + tile)
        block = up_ref[:, :, span].reshape(local * depth, tile)
        adapted = jnp.dot(kept, block, preferred_element_type=F32).astype(BF16)
        for r, out in zip((2, 3, 1, 0), outs):
            out[:, span] = adapted[r * cap : (r + 1) * cap]


def up(shares, slot, factor, weight, parts, tile=512):
    local, rank, width = weight.shape
    rows = slot.shape[0]
    cap = rows // parts
    vmem = pl.BlockSpec(memory_space=pltpu.VMEM)
    return pl.pallas_call(
        functools.partial(up_kernel, tile=tile),
        in_specs=[vmem] * 7,
        out_specs=[vmem] * parts,
        out_shape=[sds((cap, width))] * parts,
        compiler_params=params(),
        cost_estimate=cost(2**34, weight.size * 2),
        name="up",
    )(*shares, slot, factor, weight)


def finish_kernel(pick_ref, y0, y1, y2, a2, a3, a1, a0, out):
    rows = jnp.concatenate([a[...] for a in (a0, a1, a2, a3)], axis=0)
    pick = pick_ref[...][:, : rows.shape[0]]
    adapted = jnp.dot(pick, rows, preferred_element_type=F32)
    base = y0[...].astype(F32) + y1[...].astype(F32) + y2[...].astype(F32)
    out[...] = (base + adapted).astype(BF16)


def finish(pick, shares, adapted):
    vmem = pl.BlockSpec(memory_space=pltpu.VMEM)
    return pl.pallas_call(
        finish_kernel,
        in_specs=[vmem] * 8,
        out_specs=vmem,
        out_shape=sds(shares[0].shape),
        compiler_params=params(),
        cost_estimate=cost(2**24, shares[0].size * 16),
        name="finish",
    )(pick, *shares, *adapted)


def across(value, axis, r):
    n = lax.axis_size(axis)
    return lax.ppermute(value, axis, [(i, i ^ r) for i in range(n)])


def per_device_four(
    query,
    fresh_key,
    fresh_value,
    stored_keys,
    stored_values,
    cached_length,
    request_adapter,
    rank_per_adapter,
    output_weight,
    adapter_down_weight,
    adapter_up_weight,
):
    tensor_count = lax.axis_size("tensor")
    batch_count = lax.axis_size("batch")
    local = adapter_down_weight.shape[0]
    width = adapter_up_weight.shape[2]
    requests = query.shape[0]
    cap = 2 * requests * tensor_count // batch_count
    blocks = attend_blocks(
        cached_length,
        request_adapter,
        rank_per_adapter,
        query,
        fresh_key,
        fresh_value,
        stored_keys,
        stored_values,
    )
    blocks = [across(blocks[3 - r], "tensor", r) for r in (3, 2, 1)] + [blocks[3]]
    rows, pick, *chosen = route(blocks, local, cap)

    gathered = [chosen[0]] + [across(chosen[r], "batch", r) for r in (1, 2, 3)]
    far, near = project(rows, output_weight, width, (3, 1))
    far_in = across(far, "tensor", 1)
    near_in = across(near, "tensor", 1)

    low, slot, factor = down(gathered, adapter_down_weight)
    shares = [low] + [across(low, "tensor", r) for r in (1, 2, 3)]
    (cross,) = project(rows, output_weight, width, (2,), addend=far_in)
    (mine,) = project(rows, output_weight, width, (0,))
    cross_in = across(cross, "tensor", 2)

    lifted = up(shares, slot, factor, adapter_up_weight, batch_count)
    lifted = [across(a, "batch", r) for a, r in zip(lifted, (2, 3, 1))] + [lifted[3]]
    return finish(pick, (mine, near_in, cross_in), lifted)


def attend(query, fresh_key, fresh_value, stored_keys, stored_values, cached_length):
    requests = query.shape[0]
    kv_heads, longest, head_dim = stored_keys.shape[1:]
    group_size = query.shape[1] // (kv_heads * head_dim)
    queries = query.reshape(requests, kv_heads, group_size, head_dim)
    scaling = 1.0 / math.sqrt(head_dim)
    scores = (
        jnp.einsum("rkgd,rkld->rkgl", queries, stored_keys, preferred_element_type=F32) * scaling
    )
    own_score = (
        jnp.einsum(
            "rkgd,rkd->rkg",
            queries,
            fresh_key.reshape(requests, kv_heads, head_dim),
            preferred_element_type=F32,
        )
        * scaling
    )
    valid = (jnp.arange(longest, dtype=jnp.int32)[None, :] < cached_length[:, None])[
        :, None, None, :
    ]
    scores = jnp.where(valid, scores, -1e30)
    highest = jnp.maximum(jnp.max(scores, axis=-1), own_score)
    exponent = jnp.where(valid, jnp.exp(scores - highest[..., None]), 0.0)
    own_exp = jnp.exp(own_score - highest)
    sum_exp = jnp.sum(exponent, axis=-1) + own_exp
    weights = (exponent / sum_exp[..., None]).astype(BF16)
    own_weight = (own_exp / sum_exp).astype(BF16)
    result = jnp.einsum("rkgl,rkld->rkgd", weights, stored_values, preferred_element_type=F32)
    own_value = fresh_value.reshape(requests, kv_heads, 1, head_dim).astype(F32)
    result = result + own_weight.astype(F32)[..., None] * own_value
    return result.reshape(requests, -1).astype(BF16)


def per_device_any(
    query,
    fresh_key,
    fresh_value,
    stored_keys,
    stored_values,
    cached_length,
    request_adapter,
    rank_per_adapter,
    output_weight,
    adapter_down_weight,
    adapter_up_weight,
):
    attended = attend(query, fresh_key, fresh_value, stored_keys, stored_values, cached_length)
    batch_count = lax.axis_size("batch")
    local, _, rank_span = adapter_down_weight.shape
    head_rows = lax.all_to_all(attended, "tensor", split_axis=1, concat_axis=0, tiled=True)
    row_count = head_rows.shape[0]
    products = jnp.dot(head_rows, output_weight, preferred_element_type=F32)
    base = lax.psum_scatter(
        products.astype(BF16), "tensor", scatter_dimension=1, tiled=True
    ).astype(F32)
    all_rows = lax.all_gather(head_rows, "batch", axis=0, tiled=True)
    ids = lax.all_gather(request_adapter, ("batch", "tensor"), axis=0, tiled=True)
    slot = ids - lax.axis_index("batch") * local
    one_hot = slot[:, None] == jnp.arange(local, dtype=jnp.int32)[None, :]
    low_every = jnp.einsum("rk,skj->rsj", all_rows, adapter_down_weight, preferred_element_type=F32)
    low = jnp.sum(jnp.where(one_hot[:, :, None], low_every, 0.0), axis=1)
    low = lax.psum(low.astype(BF16), "tensor").astype(F32)
    adapter_count = rank_per_adapter.shape[0]
    picked = ids[:, None] == jnp.arange(adapter_count, dtype=jnp.int32)[None, :]
    row_rank = jnp.sum(jnp.where(picked, rank_per_adapter[None, :], 0), axis=1)[:, None]
    kept = jnp.arange(rank_span, dtype=jnp.int32)[None, :] < row_rank
    delta = jnp.where(kept, low * (ADAPTER_SCALE / row_rank.astype(F32)), 0.0).astype(BF16)
    widened = jnp.where(one_hot[:, :, None], delta[:, None, :], jnp.zeros((), BF16))
    adapted = jnp.dot(
        widened.reshape(ids.shape[0], local * rank_span),
        adapter_up_weight.reshape(local * rank_span, -1),
        preferred_element_type=F32,
    ).astype(BF16)
    adapted = lax.all_to_all(
        adapted.reshape(batch_count, row_count, -1), "batch", split_axis=0, concat_axis=0, tiled=True
    )
    adapted = jnp.sum(adapted.astype(F32), axis=0)
    return (base + adapted).astype(BF16)


def solution(mesh):
    in_specs = (
        P(("group", "batch", "tensor"), None),
        P(("group", "batch", "tensor"), None),
        P(("group", "batch", "tensor"), None),
        P(("group", "batch", "tensor"), None, None, None),
        P(("group", "batch", "tensor"), None, None, None),
        P(("group", "batch", "tensor")),
        P(("group", "batch", "tensor")),
        P(),
        P("tensor", None),
        P("batch", "tensor", None),
        P("batch", None, "tensor"),
    )
    out_specs = P(("group", "batch"), "tensor")

    def whole(*arrays):
        tensor_count, batch_count = mesh.shape["tensor"], mesh.shape["batch"]
        four = tensor_count == batch_count == arrays[3].shape[1] == 4
        body = per_device_four if four else per_device_any
        return jax.shard_map(
            body, mesh=mesh, in_specs=in_specs, out_specs=out_specs, check_vma=False
        )(*arrays)

    return whole
```

```python
import functools
import math

import jax
import jax.numpy as jnp
from jax import lax
from jax.experimental import pallas as pl
from jax.experimental.pallas import tpu as pltpu
from jax.sharding import PartitionSpec as P

ADAPTER_SCALE = 16.0
F32 = jnp.float32
BF16 = jnp.bfloat16
LANES = 128
MIB = 1024 * 1024


def params(grid_rank=0, vmem=24 * MIB):
    if grid_rank:
        return pltpu.CompilerParams(
            dimension_semantics=("arbitrary",) * grid_rank, vmem_limit_bytes=vmem
        )
    return pltpu.CompilerParams(vmem_limit_bytes=vmem)


def cost(flops, nbytes):
    return pl.CostEstimate(flops=flops, bytes_accessed=nbytes, transcendentals=0)


def sds(shape, dtype=BF16):
    return jax.ShapeDtypeStruct(shape, dtype)


def column_of(values):
    count = len(values)
    rows = lax.broadcasted_iota(jnp.int32, (count, LANES), 0)
    out = jnp.full((count, LANES), values[0], jnp.int32)
    for i in range(1, count):
        out = jnp.where(rows == i, values[i], out)
    return out


def attend_kernel(*refs, kv):
    length_hbm, adapter_hbm, ranks_hbm, q_hbm, fk_hbm, fv_hbm, k_hbm, v_hbm = refs[:8]
    outs = refs[8 : 8 + kv]
    length, adapter, ranks, q_buf, fk_buf, fv_buf, k_buf, v_buf, small, big = refs[8 + kv :]
    requests, _, longest, dim = k_hbm.shape
    width = q_hbm.shape[1] // kv
    group = width // dim
    rows = group * requests
    scaling = 1.0 / math.sqrt(dim)
    me = lax.axis_index("tensor")
    order = tuple(range(kv - 1, -1, -1))

    ready = [
        pltpu.make_async_copy(source, target, small.at[i])
        for i, (source, target) in enumerate(
            (
                (q_hbm, q_buf),
                (fk_hbm, fk_buf),
                (fv_hbm, fv_buf),
                (length_hbm, length),
                (adapter_hbm, adapter),
                (ranks_hbm, ranks),
            )
        )
    ]
    keys_in = pltpu.make_async_copy(k_hbm, k_buf, big.at[0])
    values_in = pltpu.make_async_copy(v_hbm, v_buf, big.at[1])
    for copy in ready:
        copy.start()
    keys_in.start()
    values_in.start()
    for copy in ready:
        copy.wait()

    request = lax.rem(lax.broadcasted_iota(jnp.int32, (rows, longest), 0), requests)
    lengths = jnp.concatenate(
        [column_of([length[i] for i in range(requests)])] * group, axis=0
    )
    valid = lax.broadcasted_iota(jnp.int32, (rows, longest), 1) < lengths
    named = [adapter[i] for i in range(requests)]
    lane = lax.broadcasted_iota(jnp.int32, (requests, LANES), 1)
    ids = jnp.where(
        lane < LANES // 2, column_of(named), column_of([ranks[a] for a in named])
    ).astype(F32)
    scores, own, fresh_value = {}, {}, {}
    for r in order:
        head = jnp.bitwise_xor(me, r)
        mine = pl.ds(pl.multiple_of(head * dim, dim), dim)
        q32 = q_buf[:, pl.ds(pl.multiple_of(head * width, width), width)].astype(F32)
        queries = jnp.concatenate([q32[:, h * dim : (h + 1) * dim] for h in range(group)], axis=0)
        fresh_key = jnp.concatenate([fk_buf[:, mine].astype(F32)] * group, axis=0)
        fresh_value[r] = jnp.concatenate([fv_buf[:, mine].astype(F32)] * group, axis=0)
        own[r] = jnp.sum(queries * fresh_key, axis=1, keepdims=True) * scaling
        scores[r] = queries.astype(BF16)
    keys_in.wait()
    for r in order:
        every = lax.dot_general(
            scores[r],
            k_buf[:, jnp.bitwise_xor(me, r)].reshape(requests * longest, dim),
            (((1,), (1,)), ((), ())),
            preferred_element_type=F32,
        )
        picked = every[:, :longest]
        for i in range(1, requests):
            picked = jnp.where(request == i, every[:, i * longest : (i + 1) * longest], picked)
        scores[r] = jnp.where(valid, picked * scaling, -1e30)
    highest = {r: jnp.maximum(jnp.max(scores[r], axis=1, keepdims=True), own[r]) for r in order}
    exponent = {r: jnp.where(valid, jnp.exp(scores[r] - highest[r]), 0.0) for r in order}
    own_exp = {r: jnp.exp(own[r] - highest[r]) for r in order}
    inverse = {
        r: 1.0 / (jnp.sum(exponent[r], axis=1, keepdims=True) + own_exp[r]) for r in order
    }
    spread = {}
    for r in order:
        weights = exponent[r] * inverse[r]
        spread[r] = jnp.concatenate(
            [jnp.where(request == i, weights, 0.0) for i in range(requests)], axis=1
        ).astype(BF16)
    values_in.wait()
    for r in order:
        own_weight = (own_exp[r] * inverse[r]).astype(BF16).astype(F32)
        result = (
            jnp.dot(
                spread[r], v_buf[:, jnp.bitwise_xor(me, r)].reshape(requests * longest, dim), preferred_element_type=F32
            )
            + own_weight * fresh_value[r]
        )
        pieces = [result[h * requests : (h + 1) * requests] for h in range(group)]
        outs[kv - 1 - r][...] = jnp.concatenate(pieces + [ids], axis=1).astype(BF16)


def attend_blocks(length, adapter, ranks, query, fresh_key, fresh_value, keys, values):
    requests, kv, longest, dim = keys.shape
    width = query.shape[1] // kv
    hbm = pl.BlockSpec(memory_space=pltpu.HBM)
    return pl.pallas_call(
        functools.partial(attend_kernel, kv=kv),
        in_specs=[hbm] * 8,
        out_specs=[pl.BlockSpec(memory_space=pltpu.VMEM)] * kv,
        out_shape=[sds((requests, width + LANES))] * kv,
        scratch_shapes=[
            pltpu.SMEM(length.shape, jnp.int32),
            pltpu.SMEM(adapter.shape, jnp.int32),
            pltpu.SMEM(ranks.shape, jnp.int32),
            pltpu.VMEM(query.shape, BF16),
            pltpu.VMEM(fresh_key.shape, BF16),
            pltpu.VMEM(fresh_value.shape, BF16),
            pltpu.VMEM(keys.shape, BF16),
            pltpu.VMEM(values.shape, BF16),
            pltpu.SemaphoreType.DMA((6,)),
            pltpu.SemaphoreType.DMA((2,)),
        ],
        compiler_params=params(),
        cost_estimate=cost(2**35, 2 * keys.size * 2),
        name="attend",
    )(*[pltpu.with_memory_space_constraint(x, pltpu.HBM) for x in (length, adapter, ranks, query, fresh_key, fresh_value, keys, values)])


def route_kernel(x0, x1, x2, x3, rows_ref, pick_ref, c0, c1, c2, c3, held, *, local, cap):
    me, mine = lax.axis_index("tensor"), lax.axis_index("batch")
    count = x0.shape[0]
    for r, x in zip((3, 2, 1, 0), (x0, x1, x2, x3)):
        held[pl.ds(pl.multiple_of(jnp.bitwise_xor(me, r) * count, count), count), :] = x[
            ...
        ].astype(F32)
    every = held[...]
    packed = every.astype(BF16)
    rows, wide = every.shape
    width = wide - LANES
    rows_ref[...] = packed[:, :width]
    adapter = every[:, width:].astype(jnp.int32)
    lane = lax.broadcasted_iota(jnp.int32, (rows, LANES), 1)
    part, slot = lax.div(lane, cap), lax.rem(lane, cap)
    first = jnp.bitwise_xor(mine, part) * local
    held_there = (adapter >= first) & (adapter < first + local) & (part < 4)
    held_f = held_there.astype(F32)
    lower = lax.broadcasted_iota(jnp.int32, (rows, rows), 0) >= lax.broadcasted_iota(
        jnp.int32, (rows, rows), 1
    )
    place_in = jnp.dot(
        lower.astype(F32).astype(BF16), held_f.astype(BF16), preferred_element_type=F32
    )
    pick = jnp.where(held_there & (place_in == (slot + 1).astype(F32)), 1.0, 0.0).astype(BF16)
    pick_ref[...] = pick
    chosen = lax.dot_general(
        pick, packed, (((0,), (0,)), ((), ())), preferred_element_type=F32
    ).astype(BF16)
    for r, c in enumerate((c0, c1, c2, c3)):
        c[...] = chosen[r * cap : (r + 1) * cap]


def route(blocks, local, cap):
    count, wide = blocks[0].shape
    rows = count * len(blocks)
    vmem = pl.BlockSpec(memory_space=pltpu.VMEM)
    return pl.pallas_call(
        functools.partial(route_kernel, local=local, cap=cap),
        in_specs=[vmem] * 4,
        out_specs=[vmem] * 6,
        out_shape=[sds((rows, wide - LANES)), sds((rows, LANES))] + [sds((cap, wide))] * 4,
        scratch_shapes=[pltpu.VMEM((rows, wide), F32)],
        compiler_params=params(),
        cost_estimate=cost(2**20, rows * wide * 8),
        name="route",
    )(*blocks)


def project_kernel(rows_ref, w_ref, *refs, which, tile, add):
    addend, outs = (refs[0], refs[1:]) if add else (None, refs)
    width = outs[0].shape[1]
    me = lax.axis_index("tensor")
    rows = rows_ref[...]
    for k, r in enumerate(which):
        start = jnp.bitwise_xor(me, r) * width
        for low in range(0, width, tile):
            at = pl.ds(pl.multiple_of(start + low, tile), tile)
            product = jnp.dot(rows, w_ref[:, at], preferred_element_type=F32)
            span = slice(low, low + tile)
            if add and k == 0:
                product = product + addend[:, span].astype(F32)
            outs[k][:, span] = product.astype(BF16)


def project(rows, weight, width, which, addend=None, tile=512):
    count, depth = rows.shape
    parts = len(which)
    vmem = pl.BlockSpec(memory_space=pltpu.VMEM)
    operands = [rows, weight] + ([] if addend is None else [addend])
    return pl.pallas_call(
        functools.partial(project_kernel, which=which, tile=tile, add=addend is not None),
        in_specs=[vmem] * len(operands),
        out_specs=[vmem] * parts,
        out_shape=[sds((count, width))] * parts,
        compiler_params=params(),
        cost_estimate=cost(2 * count * depth * width * parts, depth * width * 2 * parts),
        name="project",
    )(*operands)


def down_kernel(c0, c1, c2, c3, down_ref, low_ref, slot_ref, factor_ref):
    local, width, rank = down_ref.shape
    chosen = jnp.concatenate([c[...] for c in (c0, c1, c2, c3)], axis=0)
    values = chosen[:, :width]
    tail = chosen[:, width:].astype(F32)
    half = tail.shape[1] // 2
    slot = jnp.concatenate([tail[:, :half]] * 2, axis=1).astype(jnp.int32)
    slot = slot - lax.axis_index("batch") * local
    ranks = jnp.concatenate([tail[:, half:]] * 2, axis=1)
    lane = lax.broadcasted_iota(jnp.int32, slot.shape, 1).astype(F32)
    factor_ref[...] = jnp.where(lane < ranks, ADAPTER_SCALE / jnp.maximum(ranks, 1.0), 0.0)
    low = jnp.zeros((chosen.shape[0], rank), F32)
    for a in range(local):
        product = jnp.dot(values, down_ref[a], preferred_element_type=F32)
        low = jnp.where(slot == a, product, low)
    low_ref[...] = low.astype(BF16)
    slot_ref[...] = slot


def down(chosen, weight):
    local, width, rank = weight.shape
    rows = chosen[0].shape[0] * len(chosen)
    vmem = pl.BlockSpec(memory_space=pltpu.VMEM)
    return pl.pallas_call(
        down_kernel,
        in_specs=[vmem] * 5,
        out_specs=[vmem] * 3,
        out_shape=[sds((rows, rank)), sds((rows, rank), jnp.int32), sds((rows, rank), F32)],
        compiler_params=params(),
        cost_estimate=cost(2**34, weight.size * 2),
        name="down",
    )(*chosen, weight)


def up_kernel(l0, l1, l2, l3, slot_ref, factor_ref, up_ref, *outs, tile):
    local, depth, width = up_ref.shape
    low = l0[...].astype(F32)
    for share in (l1, l2, l3):
        low = low + share[...].astype(F32)
    low = low * factor_ref[...]
    slot = slot_ref[...]
    kept = jnp.concatenate(
        [jnp.where(slot == a, low, 0.0).astype(BF16) for a in range(local)], axis=1
    )
    cap = outs[0].shape[0]
    for start in range(0, width, tile):
        span = slice(start, start + tile)
        block = up_ref[:, :, span].reshape(local * depth, tile)
        adapted = jnp.dot(kept, block, preferred_element_type=F32).astype(BF16)
        for r, out in zip((2, 3, 1, 0), outs):
            out[:, span] = adapted[r * cap : (r + 1) * cap]


def up(shares, slot, factor, weight, parts, tile=512):
    local, rank, width = weight.shape
    rows = slot.shape[0]
    cap = rows // parts
    vmem = pl.BlockSpec(memory_space=pltpu.VMEM)
    return pl.pallas_call(
        functools.partial(up_kernel, tile=tile),
        in_specs=[vmem] * 7,
        out_specs=[vmem] * parts,
        out_shape=[sds((cap, width))] * parts,
        compiler_params=params(),
        cost_estimate=cost(2**34, weight.size * 2),
        name="up",
    )(*shares, slot, factor, weight)


def finish_kernel(pick_ref, y0, y1, y2, a2, a3, a1, a0, out):
    rows = jnp.concatenate([a[...] for a in (a0, a1, a2, a3)], axis=0)
    pick = pick_ref[...][:, : rows.shape[0]]
    adapted = jnp.dot(pick, rows, preferred_element_type=F32)
    base = y0[...].astype(F32) + y1[...].astype(F32) + y2[...].astype(F32)
    out[...] = (base + adapted).astype(BF16)


def finish(pick, shares, adapted):
    vmem = pl.BlockSpec(memory_space=pltpu.VMEM)
    return pl.pallas_call(
        finish_kernel,
        in_specs=[vmem] * 8,
        out_specs=vmem,
        out_shape=sds(shares[0].shape),
        compiler_params=params(),
        cost_estimate=cost(2**24, shares[0].size * 16),
        name="finish",
    )(pick, *shares, *adapted)


def across(value, axis, r):
    n = lax.axis_size(axis)
    return lax.ppermute(value, axis, [(i, i ^ r) for i in range(n)])


def per_device_four(
    query,
    fresh_key,
    fresh_value,
    stored_keys,
    stored_values,
    cached_length,
    request_adapter,
    rank_per_adapter,
    output_weight,
    adapter_down_weight,
    adapter_up_weight,
):
    tensor_count = lax.axis_size("tensor")
    batch_count = lax.axis_size("batch")
    local = adapter_down_weight.shape[0]
    width = adapter_up_weight.shape[2]
    requests = query.shape[0]
    cap = 2 * requests * tensor_count // batch_count
    blocks = attend_blocks(
        cached_length,
        request_adapter,
        rank_per_adapter,
        query,
        fresh_key,
        fresh_value,
        stored_keys,
        stored_values,
    )
    blocks = [across(blocks[3 - r], "tensor", r) for r in (3, 2, 1)] + [blocks[3]]
    rows, pick, *chosen = route(blocks, local, cap)

    gathered = [chosen[0]] + [across(chosen[r], "batch", r) for r in (1, 2, 3)]
    far, near = project(rows, output_weight, width, (3, 1))
    far_in = across(far, "tensor", 1)

    low, slot, factor = down(gathered, adapter_down_weight)
    shares = [low] + [across(low, "tensor", r) for r in (1, 2, 3)]
    (cross,) = project(rows, output_weight, width, (2,), addend=far_in)
    (mine,) = project(rows, output_weight, width, (0,))
    near, cross = lax.optimization_barrier((near, cross))
    cross_in = across(cross, "tensor", 2)
    near_in = across(near, "tensor", 1)

    lifted = up(shares, slot, factor, adapter_up_weight, batch_count)
    lifted = [across(a, "batch", r) for a, r in zip(lifted, (2, 3, 1))] + [lifted[3]]
    return finish(pick, (mine, near_in, cross_in), lifted)


def attend(query, fresh_key, fresh_value, stored_keys, stored_values, cached_length):
    requests = query.shape[0]
    kv_heads, longest, head_dim = stored_keys.shape[1:]
    group_size = query.shape[1] // (kv_heads * head_dim)
    queries = query.reshape(requests, kv_heads, group_size, head_dim)
    scaling = 1.0 / math.sqrt(head_dim)
    scores = (
        jnp.einsum("rkgd,rkld->rkgl", queries, stored_keys, preferred_element_type=F32) * scaling
    )
    own_score = (
        jnp.einsum(
            "rkgd,rkd->rkg",
            queries,
            fresh_key.reshape(requests, kv_heads, head_dim),
            preferred_element_type=F32,
        )
        * scaling
    )
    valid = (jnp.arange(longest, dtype=jnp.int32)[None, :] < cached_length[:, None])[
        :, None, None, :
    ]
    scores = jnp.where(valid, scores, -1e30)
    highest = jnp.maximum(jnp.max(scores, axis=-1), own_score)
    exponent = jnp.where(valid, jnp.exp(scores - highest[..., None]), 0.0)
    own_exp = jnp.exp(own_score - highest)
    sum_exp = jnp.sum(exponent, axis=-1) + own_exp
    weights = (exponent / sum_exp[..., None]).astype(BF16)
    own_weight = (own_exp / sum_exp).astype(BF16)
    result = jnp.einsum("rkgl,rkld->rkgd", weights, stored_values, preferred_element_type=F32)
    own_value = fresh_value.reshape(requests, kv_heads, 1, head_dim).astype(F32)
    result = result + own_weight.astype(F32)[..., None] * own_value
    return result.reshape(requests, -1).astype(BF16)


def per_device_any(
    query,
    fresh_key,
    fresh_value,
    stored_keys,
    stored_values,
    cached_length,
    request_adapter,
    rank_per_adapter,
    output_weight,
    adapter_down_weight,
    adapter_up_weight,
):
    attended = attend(query, fresh_key, fresh_value, stored_keys, stored_values, cached_length)
    batch_count = lax.axis_size("batch")
    local, _, rank_span = adapter_down_weight.shape
    head_rows = lax.all_to_all(attended, "tensor", split_axis=1, concat_axis=0, tiled=True)
    row_count = head_rows.shape[0]
    products = jnp.dot(head_rows, output_weight, preferred_element_type=F32)
    base = lax.psum_scatter(
        products.astype(BF16), "tensor", scatter_dimension=1, tiled=True
    ).astype(F32)
    all_rows = lax.all_gather(head_rows, "batch", axis=0, tiled=True)
    ids = lax.all_gather(request_adapter, ("batch", "tensor"), axis=0, tiled=True)
    slot = ids - lax.axis_index("batch") * local
    one_hot = slot[:, None] == jnp.arange(local, dtype=jnp.int32)[None, :]
    low_every = jnp.einsum("rk,skj->rsj", all_rows, adapter_down_weight, preferred_element_type=F32)
    low = jnp.sum(jnp.where(one_hot[:, :, None], low_every, 0.0), axis=1)
    low = lax.psum(low.astype(BF16), "tensor").astype(F32)
    adapter_count = rank_per_adapter.shape[0]
    picked = ids[:, None] == jnp.arange(adapter_count, dtype=jnp.int32)[None, :]
    row_rank = jnp.sum(jnp.where(picked, rank_per_adapter[None, :], 0), axis=1)[:, None]
    kept = jnp.arange(rank_span, dtype=jnp.int32)[None, :] < row_rank
    delta = jnp.where(kept, low * (ADAPTER_SCALE / row_rank.astype(F32)), 0.0).astype(BF16)
    widened = jnp.where(one_hot[:, :, None], delta[:, None, :], jnp.zeros((), BF16))
    adapted = jnp.dot(
        widened.reshape(ids.shape[0], local * rank_span),
        adapter_up_weight.reshape(local * rank_span, -1),
        preferred_element_type=F32,
    ).astype(BF16)
    adapted = lax.all_to_all(
        adapted.reshape(batch_count, row_count, -1), "batch", split_axis=0, concat_axis=0, tiled=True
    )
    adapted = jnp.sum(adapted.astype(F32), axis=0)
    return (base + adapted).astype(BF16)


def solution(mesh):
    in_specs = (
        P(("group", "batch", "tensor"), None),
        P(("group", "batch", "tensor"), None),
        P(("group", "batch", "tensor"), None),
        P(("group", "batch", "tensor"), None, None, None),
        P(("group", "batch", "tensor"), None, None, None),
        P(("group", "batch", "tensor")),
        P(("group", "batch", "tensor")),
        P(),
        P("tensor", None),
        P("batch", "tensor", None),
        P("batch", None, "tensor"),
    )
    out_specs = P(("group", "batch"), "tensor")

    def whole(*arrays):
        tensor_count, batch_count = mesh.shape["tensor"], mesh.shape["batch"]
        four = tensor_count == batch_count == arrays[3].shape[1] == 4
        body = per_device_four if four else per_device_any
        return jax.shard_map(
            body, mesh=mesh, in_specs=in_specs, out_specs=out_specs, check_vma=False
        )(*arrays)

    return whole
```

```python
import functools
import math

import jax
import jax.numpy as jnp
from jax import lax
from jax.experimental import pallas as pl
from jax.experimental.pallas import tpu as pltpu
from jax.sharding import PartitionSpec as P

ADAPTER_SCALE = 16.0
F32 = jnp.float32
BF16 = jnp.bfloat16
LANES = 128
MIB = 1024 * 1024


def params(grid_rank=0, vmem=24 * MIB):
    if grid_rank:
        return pltpu.CompilerParams(
            dimension_semantics=("arbitrary",) * grid_rank, vmem_limit_bytes=vmem
        )
    return pltpu.CompilerParams(vmem_limit_bytes=vmem)


def cost(flops, nbytes):
    return pl.CostEstimate(flops=flops, bytes_accessed=nbytes, transcendentals=0)


def sds(shape, dtype=BF16):
    return jax.ShapeDtypeStruct(shape, dtype)


def column_of(values):
    count = len(values)
    rows = lax.broadcasted_iota(jnp.int32, (count, LANES), 0)
    out = jnp.full((count, LANES), values[0], jnp.int32)
    for i in range(1, count):
        out = jnp.where(rows == i, values[i], out)
    return out


def attend_kernel(*refs, kv):
    length_hbm, adapter_hbm, ranks_hbm, q_hbm, fk_hbm, fv_hbm, k_hbm, v_hbm = refs[:8]
    outs = refs[8 : 8 + kv]
    length, adapter, ranks, q_buf, fk_buf, fv_buf, k_buf, v_buf, small, big = refs[8 + kv :]
    requests, _, longest, dim = k_hbm.shape
    width = q_hbm.shape[1] // kv
    group = width // dim
    rows = group * requests
    scaling = 1.0 / math.sqrt(dim)
    me = lax.axis_index("tensor")
    order = tuple(range(kv - 1, -1, -1))

    ready = [
        pltpu.make_async_copy(source, target, small.at[i])
        for i, (source, target) in enumerate(
            (
                (q_hbm, q_buf),
                (fk_hbm, fk_buf),
                (fv_hbm, fv_buf),
                (length_hbm, length),
                (adapter_hbm, adapter),
                (ranks_hbm, ranks),
            )
        )
    ]
    keys_in = pltpu.make_async_copy(k_hbm, k_buf, big.at[0])
    values_in = pltpu.make_async_copy(v_hbm, v_buf, big.at[1])
    for copy in ready:
        copy.start()
    keys_in.start()
    values_in.start()
    for copy in ready:
        copy.wait()

    request = lax.rem(lax.broadcasted_iota(jnp.int32, (rows, longest), 0), requests)
    lengths = jnp.concatenate(
        [column_of([length[i] for i in range(requests)])] * group, axis=0
    )
    valid = lax.broadcasted_iota(jnp.int32, (rows, longest), 1) < lengths
    named = [adapter[i] for i in range(requests)]
    lane = lax.broadcasted_iota(jnp.int32, (requests, LANES), 1)
    ids = jnp.where(
        lane < LANES // 2, column_of(named), column_of([ranks[a] for a in named])
    ).astype(F32)
    scores, own, fresh_value = {}, {}, {}
    for r in order:
        head = jnp.bitwise_xor(me, r)
        mine = pl.ds(pl.multiple_of(head * dim, dim), dim)
        q32 = q_buf[:, pl.ds(pl.multiple_of(head * width, width), width)].astype(F32)
        queries = jnp.concatenate([q32[:, h * dim : (h + 1) * dim] for h in range(group)], axis=0)
        fresh_key = jnp.concatenate([fk_buf[:, mine].astype(F32)] * group, axis=0)
        fresh_value[r] = jnp.concatenate([fv_buf[:, mine].astype(F32)] * group, axis=0)
        own[r] = jnp.sum(queries * fresh_key, axis=1, keepdims=True) * scaling
        scores[r] = queries.astype(BF16)
    keys_in.wait()
    for r in order:
        every = lax.dot_general(
            scores[r],
            k_buf[:, jnp.bitwise_xor(me, r)].reshape(requests * longest, dim),
            (((1,), (1,)), ((), ())),
            preferred_element_type=F32,
        )
        picked = every[:, :longest]
        for i in range(1, requests):
            picked = jnp.where(request == i, every[:, i * longest : (i + 1) * longest], picked)
        scores[r] = jnp.where(valid, picked * scaling, -1e30)
    highest = {r: jnp.maximum(jnp.max(scores[r], axis=1, keepdims=True), own[r]) for r in order}
    exponent = {r: jnp.where(valid, jnp.exp(scores[r] - highest[r]), 0.0) for r in order}
    own_exp = {r: jnp.exp(own[r] - highest[r]) for r in order}
    inverse = {
        r: 1.0 / (jnp.sum(exponent[r], axis=1, keepdims=True) + own_exp[r]) for r in order
    }
    spread = {}
    for r in order:
        weights = exponent[r] * inverse[r]
        spread[r] = jnp.concatenate(
            [jnp.where(request == i, weights, 0.0) for i in range(requests)], axis=1
        ).astype(BF16)
    values_in.wait()
    for r in order:
        own_weight = (own_exp[r] * inverse[r]).astype(BF16).astype(F32)
        result = (
            jnp.dot(
                spread[r], v_buf[:, jnp.bitwise_xor(me, r)].reshape(requests * longest, dim), preferred_element_type=F32
            )
            + own_weight * fresh_value[r]
        )
        pieces = [result[h * requests : (h + 1) * requests] for h in range(group)]
        outs[kv - 1 - r][...] = jnp.concatenate(pieces + [ids], axis=1).astype(BF16)


def attend_blocks(length, adapter, ranks, query, fresh_key, fresh_value, keys, values):
    requests, kv, longest, dim = keys.shape
    width = query.shape[1] // kv
    hbm = pl.BlockSpec(memory_space=pltpu.HBM)
    return pl.pallas_call(
        functools.partial(attend_kernel, kv=kv),
        in_specs=[hbm] * 8,
        out_specs=[pl.BlockSpec(memory_space=pltpu.VMEM)] * kv,
        out_shape=[sds((requests, width + LANES))] * kv,
        scratch_shapes=[
            pltpu.SMEM(length.shape, jnp.int32),
            pltpu.SMEM(adapter.shape, jnp.int32),
            pltpu.SMEM(ranks.shape, jnp.int32),
            pltpu.VMEM(query.shape, BF16),
            pltpu.VMEM(fresh_key.shape, BF16),
            pltpu.VMEM(fresh_value.shape, BF16),
            pltpu.VMEM(keys.shape, BF16),
            pltpu.VMEM(values.shape, BF16),
            pltpu.SemaphoreType.DMA((6,)),
            pltpu.SemaphoreType.DMA((2,)),
        ],
        compiler_params=params(),
        cost_estimate=cost(2**35, 2 * keys.size * 2),
        name="attend",
    )(*[pltpu.with_memory_space_constraint(x, pltpu.HBM) for x in (length, adapter, ranks, query, fresh_key, fresh_value, keys, values)])


def route_kernel(x0, x1, x2, x3, rows_ref, pick_ref, c0, c1, c2, c3, held, *, local, cap):
    me, mine = lax.axis_index("tensor"), lax.axis_index("batch")
    count = x0.shape[0]
    for r, x in zip((3, 2, 1, 0), (x0, x1, x2, x3)):
        held[pl.ds(pl.multiple_of(jnp.bitwise_xor(me, r) * count, count), count), :] = x[
            ...
        ].astype(F32)
    every = held[...]
    packed = every.astype(BF16)
    rows, wide = every.shape
    width = wide - LANES
    rows_ref[...] = packed[:, :width]
    adapter = every[:, width:].astype(jnp.int32)
    lane = lax.broadcasted_iota(jnp.int32, (rows, LANES), 1)
    part, slot = lax.div(lane, cap), lax.rem(lane, cap)
    first = jnp.bitwise_xor(mine, part) * local
    held_there = (adapter >= first) & (adapter < first + local) & (part < 4)
    held_f = held_there.astype(F32)
    lower = lax.broadcasted_iota(jnp.int32, (rows, rows), 0) >= lax.broadcasted_iota(
        jnp.int32, (rows, rows), 1
    )
    place_in = jnp.dot(
        lower.astype(F32).astype(BF16), held_f.astype(BF16), preferred_element_type=F32
    )
    pick = jnp.where(held_there & (place_in == (slot + 1).astype(F32)), 1.0, 0.0).astype(BF16)
    pick_ref[...] = pick
    chosen = lax.dot_general(
        pick, packed, (((0,), (0,)), ((), ())), preferred_element_type=F32
    ).astype(BF16)
    for r, c in enumerate((c0, c1, c2, c3)):
        c[...] = chosen[r * cap : (r + 1) * cap]


def route(blocks, local, cap):
    count, wide = blocks[0].shape
    rows = count * len(blocks)
    vmem = pl.BlockSpec(memory_space=pltpu.VMEM)
    return pl.pallas_call(
        functools.partial(route_kernel, local=local, cap=cap),
        in_specs=[vmem] * 4,
        out_specs=[vmem] * 6,
        out_shape=[sds((rows, wide - LANES)), sds((rows, LANES))] + [sds((cap, wide))] * 4,
        scratch_shapes=[pltpu.VMEM((rows, wide), F32)],
        compiler_params=params(),
        cost_estimate=cost(2**20, rows * wide * 8),
        name="route",
    )(*blocks)


def project_kernel(rows_ref, w_ref, *refs, which, tile, add):
    addend, outs = (refs[0], refs[1:]) if add else (None, refs)
    width = outs[0].shape[1]
    me = lax.axis_index("tensor")
    rows = rows_ref[...]
    for k, r in enumerate(which):
        start = jnp.bitwise_xor(me, r) * width
        for low in range(0, width, tile):
            at = pl.ds(pl.multiple_of(start + low, tile), tile)
            product = jnp.dot(rows, w_ref[:, at], preferred_element_type=F32)
            span = slice(low, low + tile)
            if add and k == 0:
                product = product + addend[:, span].astype(F32)
            outs[k][:, span] = product.astype(BF16)


def project(rows, weight, width, which, addend=None, tile=512):
    count, depth = rows.shape
    parts = len(which)
    vmem = pl.BlockSpec(memory_space=pltpu.VMEM)
    operands = [rows, weight] + ([] if addend is None else [addend])
    return pl.pallas_call(
        functools.partial(project_kernel, which=which, tile=tile, add=addend is not None),
        in_specs=[vmem] * len(operands),
        out_specs=[vmem] * parts,
        out_shape=[sds((count, width))] * parts,
        compiler_params=params(),
        cost_estimate=cost(2 * count * depth * width * parts, depth * width * 2 * parts),
        name="project",
    )(*operands)


def down_kernel(c0, c1, c2, c3, down_ref, low_ref, slot_ref, factor_ref):
    local, width, rank = down_ref.shape
    chosen = jnp.concatenate([c[...] for c in (c0, c1, c2, c3)], axis=0)
    values = chosen[:, :width]
    tail = chosen[:, width:].astype(F32)
    half = tail.shape[1] // 2
    slot = jnp.concatenate([tail[:, :half]] * 2, axis=1).astype(jnp.int32)
    slot = slot - lax.axis_index("batch") * local
    ranks = jnp.concatenate([tail[:, half:]] * 2, axis=1)
    lane = lax.broadcasted_iota(jnp.int32, slot.shape, 1).astype(F32)
    factor_ref[...] = jnp.where(lane < ranks, ADAPTER_SCALE / jnp.maximum(ranks, 1.0), 0.0)
    low = jnp.zeros((chosen.shape[0], rank), F32)
    for a in range(local):
        product = jnp.dot(values, down_ref[a], preferred_element_type=F32)
        low = jnp.where(slot == a, product, low)
    low_ref[...] = low.astype(BF16)
    slot_ref[...] = slot


def down(chosen, weight):
    local, width, rank = weight.shape
    rows = chosen[0].shape[0] * len(chosen)
    vmem = pl.BlockSpec(memory_space=pltpu.VMEM)
    return pl.pallas_call(
        down_kernel,
        in_specs=[vmem] * 5,
        out_specs=[vmem] * 3,
        out_shape=[sds((rows, rank)), sds((rows, rank), jnp.int32), sds((rows, rank), F32)],
        compiler_params=params(),
        cost_estimate=cost(2**34, weight.size * 2),
        name="down",
    )(*chosen, weight)


def up_kernel(l0, l1, l2, l3, slot_ref, factor_ref, up_ref, *outs, tile):
    local, depth, width = up_ref.shape
    low = l0[...].astype(F32)
    for share in (l1, l2, l3):
        low = low + share[...].astype(F32)
    low = low * factor_ref[...]
    slot = slot_ref[...]
    kept = jnp.concatenate(
        [jnp.where(slot == a, low, 0.0).astype(BF16) for a in range(local)], axis=1
    )
    cap = outs[0].shape[0]
    for start in range(0, width, tile):
        span = slice(start, start + tile)
        block = up_ref[:, :, span].reshape(local * depth, tile)
        adapted = jnp.dot(kept, block, preferred_element_type=F32).astype(BF16)
        for r, out in zip((3, 2, 1, 0), outs):
            out[:, span] = adapted[r * cap : (r + 1) * cap]


def up(shares, slot, factor, weight, parts, tile=512):
    local, rank, width = weight.shape
    rows = slot.shape[0]
    cap = rows // parts
    vmem = pl.BlockSpec(memory_space=pltpu.VMEM)
    return pl.pallas_call(
        functools.partial(up_kernel, tile=tile),
        in_specs=[vmem] * 7,
        out_specs=[vmem] * parts,
        out_shape=[sds((cap, width))] * parts,
        compiler_params=params(),
        cost_estimate=cost(2**34, weight.size * 2),
        name="up",
    )(*shares, slot, factor, weight)


def finish_kernel(pick_ref, y0, y1, y2, a3, a2, a1, a0, out):
    rows = jnp.concatenate([a[...] for a in (a0, a1, a2, a3)], axis=0)
    pick = pick_ref[...][:, : rows.shape[0]]
    adapted = jnp.dot(pick, rows, preferred_element_type=F32)
    base = y0[...].astype(F32) + y1[...].astype(F32) + y2[...].astype(F32)
    out[...] = (base + adapted).astype(BF16)


def finish(pick, shares, adapted):
    vmem = pl.BlockSpec(memory_space=pltpu.VMEM)
    return pl.pallas_call(
        finish_kernel,
        in_specs=[vmem] * 8,
        out_specs=vmem,
        out_shape=sds(shares[0].shape),
        compiler_params=params(),
        cost_estimate=cost(2**24, shares[0].size * 16),
        name="finish",
    )(pick, *shares, *adapted)


def across(value, axis, r):
    n = lax.axis_size(axis)
    return lax.ppermute(value, axis, [(i, i ^ r) for i in range(n)])


def per_device_four(
    query,
    fresh_key,
    fresh_value,
    stored_keys,
    stored_values,
    cached_length,
    request_adapter,
    rank_per_adapter,
    output_weight,
    adapter_down_weight,
    adapter_up_weight,
):
    tensor_count = lax.axis_size("tensor")
    batch_count = lax.axis_size("batch")
    local = adapter_down_weight.shape[0]
    width = adapter_up_weight.shape[2]
    requests = query.shape[0]
    cap = 2 * requests * tensor_count // batch_count
    blocks = attend_blocks(
        cached_length,
        request_adapter,
        rank_per_adapter,
        query,
        fresh_key,
        fresh_value,
        stored_keys,
        stored_values,
    )
    blocks = [across(blocks[3 - r], "tensor", r) for r in (3, 2, 1)] + [blocks[3]]
    rows, pick, *chosen = route(blocks, local, cap)

    gathered = [chosen[0]] + [across(chosen[r], "batch", r) for r in (1, 2, 3)]
    far, near = project(rows, output_weight, width, (3, 1))
    far_in = across(far, "tensor", 1)

    low, slot, factor = down(gathered, adapter_down_weight)
    shares = [low] + [across(low, "tensor", r) for r in (1, 2, 3)]
    (cross,) = project(rows, output_weight, width, (2,), addend=far_in)
    (mine,) = project(rows, output_weight, width, (0,))
    near, cross = lax.optimization_barrier((near, cross))
    cross_in = across(cross, "tensor", 2)
    near_in = across(near, "tensor", 1)

    lifted = up(shares, slot, factor, adapter_up_weight, batch_count)
    lifted = [across(a, "batch", r) for a, r in zip(lifted, (3, 2, 1))] + [lifted[3]]
    return finish(pick, (mine, near_in, cross_in), lifted)


def attend(query, fresh_key, fresh_value, stored_keys, stored_values, cached_length):
    requests = query.shape[0]
    kv_heads, longest, head_dim = stored_keys.shape[1:]
    group_size = query.shape[1] // (kv_heads * head_dim)
    queries = query.reshape(requests, kv_heads, group_size, head_dim)
    scaling = 1.0 / math.sqrt(head_dim)
    scores = (
        jnp.einsum("rkgd,rkld->rkgl", queries, stored_keys, preferred_element_type=F32) * scaling
    )
    own_score = (
        jnp.einsum(
            "rkgd,rkd->rkg",
            queries,
            fresh_key.reshape(requests, kv_heads, head_dim),
            preferred_element_type=F32,
        )
        * scaling
    )
    valid = (jnp.arange(longest, dtype=jnp.int32)[None, :] < cached_length[:, None])[
        :, None, None, :
    ]
    scores = jnp.where(valid, scores, -1e30)
    highest = jnp.maximum(jnp.max(scores, axis=-1), own_score)
    exponent = jnp.where(valid, jnp.exp(scores - highest[..., None]), 0.0)
    own_exp = jnp.exp(own_score - highest)
    sum_exp = jnp.sum(exponent, axis=-1) + own_exp
    weights = (exponent / sum_exp[..., None]).astype(BF16)
    own_weight = (own_exp / sum_exp).astype(BF16)
    result = jnp.einsum("rkgl,rkld->rkgd", weights, stored_values, preferred_element_type=F32)
    own_value = fresh_value.reshape(requests, kv_heads, 1, head_dim).astype(F32)
    result = result + own_weight.astype(F32)[..., None] * own_value
    return result.reshape(requests, -1).astype(BF16)


def per_device_any(
    query,
    fresh_key,
    fresh_value,
    stored_keys,
    stored_values,
    cached_length,
    request_adapter,
    rank_per_adapter,
    output_weight,
    adapter_down_weight,
    adapter_up_weight,
):
    attended = attend(query, fresh_key, fresh_value, stored_keys, stored_values, cached_length)
    batch_count = lax.axis_size("batch")
    local, _, rank_span = adapter_down_weight.shape
    head_rows = lax.all_to_all(attended, "tensor", split_axis=1, concat_axis=0, tiled=True)
    row_count = head_rows.shape[0]
    products = jnp.dot(head_rows, output_weight, preferred_element_type=F32)
    base = lax.psum_scatter(
        products.astype(BF16), "tensor", scatter_dimension=1, tiled=True
    ).astype(F32)
    all_rows = lax.all_gather(head_rows, "batch", axis=0, tiled=True)
    ids = lax.all_gather(request_adapter, ("batch", "tensor"), axis=0, tiled=True)
    slot = ids - lax.axis_index("batch") * local
    one_hot = slot[:, None] == jnp.arange(local, dtype=jnp.int32)[None, :]
    low_every = jnp.einsum("rk,skj->rsj", all_rows, adapter_down_weight, preferred_element_type=F32)
    low = jnp.sum(jnp.where(one_hot[:, :, None], low_every, 0.0), axis=1)
    low = lax.psum(low.astype(BF16), "tensor").astype(F32)
    adapter_count = rank_per_adapter.shape[0]
    picked = ids[:, None] == jnp.arange(adapter_count, dtype=jnp.int32)[None, :]
    row_rank = jnp.sum(jnp.where(picked, rank_per_adapter[None, :], 0), axis=1)[:, None]
    kept = jnp.arange(rank_span, dtype=jnp.int32)[None, :] < row_rank
    delta = jnp.where(kept, low * (ADAPTER_SCALE / row_rank.astype(F32)), 0.0).astype(BF16)
    widened = jnp.where(one_hot[:, :, None], delta[:, None, :], jnp.zeros((), BF16))
    adapted = jnp.dot(
        widened.reshape(ids.shape[0], local * rank_span),
        adapter_up_weight.reshape(local * rank_span, -1),
        preferred_element_type=F32,
    ).astype(BF16)
    adapted = lax.all_to_all(
        adapted.reshape(batch_count, row_count, -1), "batch", split_axis=0, concat_axis=0, tiled=True
    )
    adapted = jnp.sum(adapted.astype(F32), axis=0)
    return (base + adapted).astype(BF16)


def solution(mesh):
    in_specs = (
        P(("group", "batch", "tensor"), None),
        P(("group", "batch", "tensor"), None),
        P(("group", "batch", "tensor"), None),
        P(("group", "batch", "tensor"), None, None, None),
        P(("group", "batch", "tensor"), None, None, None),
        P(("group", "batch", "tensor")),
        P(("group", "batch", "tensor")),
        P(),
        P("tensor", None),
        P("batch", "tensor", None),
        P("batch", None, "tensor"),
    )
    out_specs = P(("group", "batch"), "tensor")

    def whole(*arrays):
        tensor_count, batch_count = mesh.shape["tensor"], mesh.shape["batch"]
        four = tensor_count == batch_count == arrays[3].shape[1] == 4
        body = per_device_four if four else per_device_any
        return jax.shard_map(
            body, mesh=mesh, in_specs=in_specs, out_specs=out_specs, check_vma=False
        )(*arrays)

    return whole
```
